256 devices in a mesh: ctx: 8 (over y, core), exp: 32 (over x, z).
Axes of the slice: x: 4, y: 4, z: 8, core: 2. Of those that a mesh axis runs over, the one named last changes fastest.
Arguments:
- tokens: bfloat16 [32, 1024, 2048], P('exp', 'ctx'), may hold values from -6 to 6
- input_gain: float32 [2048], replicated, may hold values from 0.1 to 1.9
- mixer_weight: bfloat16 [2048, 6144], P(None, 'ctx'), may hold values from -0.125 to 0.125
- rate_weight: bfloat16 [2048, 8, 4], P(None, 'ctx'), may hold values from -3 to 3
- conv_kernel: float32 [4, 8, 512], P(None, 'ctx'), may hold values from -3 to 3
- decay_scale: float32 [16], P('ctx'), may hold values from 0 to 0.05
- decay_bias: float32 [16], P('ctx'), may hold values from -3 to 3
- value_gain: float32 [128], replicated, may hold values from 0.1 to 1.9
- output_weight: bfloat16 [2048, 2048], P('ctx'), may hold values from -0.125 to 0.125
- start_state: float32 [16, 128, 128], P('ctx'), may hold values from -0.8 to 0.8
- post_gain: float32 [2048], replicated, may hold values from 0.1 to 1.9
- expert_gateup: bfloat16 [32, 2048, 1024], P('exp'), may hold values from -0.125 to 0.125
- expert_down: bfloat16 [32, 512, 2048], P('exp'), may hold values from -0.25 to 0.25
- route_ids: int32 [32, 1024, 4], P('exp', 'ctx'), may hold values from 0 to 31, all different within a row; in each aligned block of 128 rows (0 to 127, 128 to 255, ..., all dimensions but the last counted through in order) at most 20 rows name the same one
- route_weights: float32 [32, 1024, 4], P('exp', 'ctx'), may hold values from 0.05 to 0.5
Outputs:
- layer_out: float32 [32, 1024, 2048], P('exp', 'ctx')
- segment_states: float32 [32, 16, 128, 128], P('exp', 'ctx')
The draws below stay inside these ranges and needn't reach their ends.
Inputs may be any that keep to these rules, and one draw needn't show every extreme that they name: `route_ids`: each token names 4 different experts. Within the 128 rows of one device (aligned blocks) no expert is named by more than 20 rows, a bound that some block reaches.
All inputs are finite; a program needn't handle non-finite values.
Results may differ from the reference program's by a relative error of at most 0.012.
Values may be sent and summed in bfloat16 or wider, within the bound.
No kernel may reach another device: no remote copies, remote signals or barrier semaphores. Data moves between devices by JAX's collectives and lax.ppermute only.
A program may use at most 128 MiB of HBM per device.

```python
import math
import jax
import jax.numpy as jnp
import numpy as np
from jax import lax

D = 2048
DK = 128
DV = 128
FFE = 512
KCONV = 4
HK = 8
HV = 16
BLOCK = 64
ROUTES = 4
TOK_DEV = 128
SEGS = 32
SEG_LEN = 1024
EXPERTS = 32
CAP = 20


outlier_level = 3.0


def feature_layout(key, slow_count):
    base = jax.random.fold_in(key, 5101)
    feature = jax.random.randint(jax.random.fold_in(base, 1), (), 0, D)
    flipped = jax.random.randint(jax.random.fold_in(base, 2), (), 0, 2)
    polarity = jnp.where(flipped == 0, -1.0, 1.0).astype(jnp.float32)
    marked = (jnp.arange(D) == feature).astype(jnp.float32)
    ordering = jax.random.permutation(jax.random.fold_in(base, 3), HV)
    slow_heads = jnp.zeros((HV,), jnp.float32).at[ordering[:slow_count]].set(1.0)
    return (marked, polarity, slow_heads)


def draw_tokens(key, part):
    marked, polarity, unused = feature_layout(key, HV // 2)
    noise_key = jax.random.fold_in(key, 11)
    array_shape = (SEGS, SEG_LEN, D)
    noise = jnp.clip(jax.random.normal(noise_key, array_shape, jnp.float32), -5.0, 5.0)
    height = jax.random.uniform(jax.random.fold_in(key, 12), array_shape, jnp.float32, 0.9 * outlier_level, 1.1 * outlier_level)
    values = marked * polarity * height + (1.0 - marked) * noise
    return values.astype(jnp.bfloat16)


def draw_input_gain(key, part):
    marked, polarity, unused = feature_layout(key, HV // 2)
    gain_key = jax.random.fold_in(key, 21)
    spread = 1.0 + 0.18 * jnp.clip(jax.random.normal(gain_key, (D,), jnp.float32), -5.0, 5.0)
    steady = jax.random.uniform(jax.random.fold_in(key, 22), (D,), jnp.float32, 0.9, 1.1)
    return marked * steady + (1.0 - marked) * spread


def draw_rate_weight(key, part):
    slow_count = HV // 2
    marked, polarity, slow_heads = feature_layout(key, slow_count)
    per_group = HV // HK
    array_shape = (D, HK, 2 * per_group)
    weight_key = jax.random.fold_in(key, 31)
    random_part = jnp.clip(jax.random.normal(weight_key, array_shape, jnp.float32), -5.0, 5.0) / math.sqrt(D)
    target = math.log(DK / (2.0 * SEGS * SEG_LEN))
    typical = outlier_level / math.sqrt((D - 1.0 + outlier_level ** 2) / D)
    slow_columns = jnp.concatenate([slow_heads.reshape(HK, per_group), jnp.zeros((HK, per_group), jnp.float32)], axis=1)[None]
    feature_mask = marked[:, None, None]
    slow_entries = (1.0 - feature_mask) * 0.3 * random_part + feature_mask * (target / typical) * polarity
    values = slow_columns * slow_entries + (1.0 - slow_columns) * random_part
    return values.astype(jnp.bfloat16)


def draw_decay_scale(key, part):
    slow_count = HV // 2
    marked, polarity, slow_heads = feature_layout(key, slow_count)
    fraction = jax.random.uniform(jax.random.fold_in(key, 41), (HV,), jnp.float32, 0.0, 1.0)
    slow_rate = jnp.exp(math.log(0.05) + fraction * (math.log(0.3) - math.log(0.05))) / (SEGS * SEG_LEN)
    fast_rate = jnp.exp(math.log(0.015) + fraction * (math.log(0.05) - math.log(0.015)))
    return slow_heads * slow_rate + (1.0 - slow_heads) * fast_rate


def level_of(own_key, dims, cuts, low, largest):
    loudness = 1.0
    for axis_at, parts in cuts:
        heights = jax.random.uniform(jax.random.fold_in(jax.random.fold_in(own_key, 6), axis_at), (parts,), jnp.float32, low / len(cuts), largest / len(cuts))
        loudness = loudness * jnp.repeat(jnp.exp(heights), dims[axis_at] // parts).reshape((-1,) + (1,) * (len(dims) - 1 - axis_at))
    return loudness


def deal_out(stream_key, own, number, rows, amount, top, bound, skew):
    ranking = jax.random.permutation(stream_key, amount)
    heavy_load, ordinary = load_shares(amount, rows * top, bound, skew, True), load_shares(amount, rows * top, bound, skew, False)
    places = jnp.arange(amount)

    def named(lengths, turn):
        used = int((lengths > 0).sum())
        fixed = max(1, used // 4)
        moved = fixed + (places - fixed + turn * (used - fixed)) % max(1, amount - fixed)
        return jnp.zeros((amount,), jnp.int32).at[ranking[jnp.where(places < fixed, places, moved)]].set(jnp.asarray(lengths, jnp.int32))

    lengths = jnp.where(number % 4 == 0, named(heavy_load, number // 4), named(ordinary, number - number // 4 - 1))
    mixed = jax.random.permutation(jax.random.fold_in(own, 3), amount)
    donor, receiver = mixed[0:amount // 2 * 2:2], mixed[1:amount // 2 * 2:2]
    room = jnp.minimum(lengths[donor] - 1, bound - lengths[receiver]) // 2
    room = jnp.where((donor == ranking[0]) | (receiver == ranking[0]) | (lengths[receiver] == 0), 0, jnp.maximum(room, 0))
    moved = jax.random.randint(jax.random.fold_in(own, 4), (amount // 2,), 0, 1 << 20) % (room + 1)
    lengths = lengths.at[donor].add(-moved).at[receiver].add(moved)
    items = jnp.searchsorted(jnp.cumsum(lengths), jnp.arange(rows * top), side="right").astype(jnp.int32)
    grid = items.reshape(top, rows).T
    grid = grid[jax.random.permutation(jax.random.fold_in(own, 1), rows)]
    turn = jax.random.randint(jax.random.fold_in(own, 2), (rows, 1), 0, top)
    return jnp.take_along_axis(grid, (jnp.arange(top)[None, :] + turn) % top, axis=1)


def load_shares(count, total, most, slope, full):
    weights = [(1 << 20) // math.isqrt(standing ** slope) + 1 for standing in range(1, count + 1)]
    largest = most if full else min(most, max(-(-total // count), total * weights[0] // sum(weights)))
    least = 1 if total - largest >= count - 1 else 0
    given, spare = [largest] + [least] * (count - 1), total - largest - least * (count - 1)
    while spare > 0:
        movable = [i for i in range(1, count) if given[i] < largest] or [i for i in range(1, count) if given[i] < most]
        pool, remaining = sum([weights[i] for i in movable]), spare
        for i in movable:
            addition = min(most - given[i], max(1, remaining * weights[i] // pool), spare)
            given[i] = given[i] + addition
            spare = spare - addition
    return np.array(given)


def scatter_about(key, shape, width, limit, cuts=(), held_as=jnp.bfloat16):
    entries = width * jax.random.normal(key, shape, jnp.float32)
    if cuts:
        entries = entries * level_of(key, shape, cuts, -0.22, 0.18)
    return jnp.clip(entries, -limit, limit).astype(held_as)


def setup_inputs(seed: int = 0) -> dict:
    splits = jax.random.split(jax.random.key(seed), 16)
    tokens = draw_tokens(jax.random.fold_in(splits[15], 71), 0)
    input_gain = draw_input_gain(jax.random.fold_in(splits[15], 71), 0)
    mixer_weight = scatter_about(splits[2], (D, 2 * HK * DK + 2 * HV * DV), D ** -0.5, 0.125, ((1, 8),))
    rate_weight = draw_rate_weight(jax.random.fold_in(splits[15], 71), 0)
    conv_kernel = scatter_about(splits[4], (KCONV, HK, 2 * DK + HV // HK * DV), KCONV ** -0.5, 3.0, ((1, 8),), jnp.float32)
    decay_scale = draw_decay_scale(jax.random.fold_in(splits[15], 71), 0)
    decay_bias = scatter_about(splits[6], (HV,), 1.0, 3.0, ((0, 8),), jnp.float32)
    value_gain = jnp.clip(1.0 + 0.18 * jax.random.normal(splits[7], (DV,), jnp.float32), 0.1, 1.9)
    output_weight = scatter_about(splits[8], (HV * DV, D), (HV * DV) ** -0.5, 0.125, ((0, 8),))
    start_state = scatter_about(splits[9], (HV, DK, DV), 0.1, 0.8, ((0, 8),), jnp.float32)
    post_gain = jnp.clip(1.0 + 0.18 * jax.random.normal(splits[10], (D,), jnp.float32), 0.1, 1.9)
    expert_gateup = scatter_about(splits[11], (EXPERTS, D, 2 * FFE), D ** -0.5, 0.125, ((0, 32),))
    expert_down = scatter_about(splits[12], (EXPERTS, FFE, D), FFE ** -0.5, 0.25, ((0, 32),))
    route_ids_keys = jax.random.split(jax.random.fold_in(splits[13], 1), SEGS * SEG_LEN // TOK_DEV)
    route_ids_turns = jax.random.permutation(jax.random.fold_in(splits[13], 3), SEGS * SEG_LEN // TOK_DEV)
    route_ids = jax.vmap(lambda own, number: deal_out(jax.random.fold_in(splits[13], 2), own, number, TOK_DEV, EXPERTS, ROUTES, CAP, 2))(route_ids_keys, route_ids_turns).reshape((SEGS, SEG_LEN, ROUTES))
    route_weights = jnp.clip(0.05 + 0.45 * jax.random.uniform(splits[14], (SEGS, SEG_LEN, ROUTES), jnp.float32) ** level_of(splits[14], (SEGS, SEG_LEN, ROUTES), ((0, 32), (1, 8)), -0.2, 0.2), 0.05, 0.5)
    return {"tokens": tokens, "input_gain": input_gain, "mixer_weight": mixer_weight, "rate_weight": rate_weight, "conv_kernel": conv_kernel, "decay_scale": decay_scale, "decay_bias": decay_bias, "value_gain": value_gain, "output_weight": output_weight, "start_state": start_state, "post_gain": post_gain, "expert_gateup": expert_gateup, "expert_down": expert_down, "route_ids": route_ids, "route_weights": route_weights}


EPSILON = 1e-06
highest = lax.Precision.HIGHEST

def rms_scale(values, scaling):
    widened = values.astype(jnp.float32)
    return widened * lax.rsqrt(lax.optimization_barrier(jnp.mean(widened * widened, axis=-1, keepdims=True)) + EPSILON) * scaling

def unit_rows(values):
    return values * lax.rsqrt(lax.optimization_barrier(jnp.sum(values * values, axis=-1, keepdims=True)) + EPSILON)

def lower_solve(strict_lower, right_side):
    result = right_side - jnp.einsum('...ij,...jk->...ik', strict_lower, right_side, precision=highest)
    powered = strict_lower
    for _ in range((strict_lower.shape[-1] - 1).bit_length() - 1):
        powered = jnp.einsum('...ij,...jk->...ik', powered, powered, precision=highest)
        result = result + jnp.einsum('...ij,...jk->...ik', powered, result, precision=highest)
    return result

def short_conv(pre_conv, tail_rows, kernel):
    padded = jnp.concatenate([tail_rows, pre_conv], axis=0).astype(jnp.float32)
    length = pre_conv.shape[0]
    summed = jnp.zeros(pre_conv.shape, jnp.float32)
    for offset in range(kernel.shape[0]):
        summed = summed + kernel[offset] * padded[offset:offset + length]
    return jax.nn.silu(summed)

def to_blocks(array):
    moved = jnp.moveaxis(array, 1, 0)
    return moved.reshape((moved.shape[0], moved.shape[1] // BLOCK, BLOCK) + moved.shape[2:])

def head_inputs(activated, rate_rows, decay_scale, decay_bias):
    length = activated.shape[0]
    per_group = HV // HK
    head_count = activated.shape[1] * per_group
    queries = jnp.repeat(unit_rows(activated[..., :DK]) * DK ** (-0.5), per_group, axis=1)
    key_rows = jnp.repeat(unit_rows(activated[..., DK:2 * DK]), per_group, axis=1)
    values = activated[..., 2 * DK:].reshape(length, head_count, DV)
    betas = jax.nn.sigmoid(rate_rows[..., :per_group].astype(jnp.float32)).reshape(length, head_count)
    decay_input = rate_rows[..., per_group:].astype(jnp.float32).reshape(length, head_count)
    decays = -decay_scale * jax.nn.softplus(decay_input + decay_bias)
    return (to_blocks(queries), to_blocks(key_rows), to_blocks(values), to_blocks(betas), to_blocks(decays))

def block_terms(queries, key_rows, values, betas, decays):
    cumulative = jnp.cumsum(decays, axis=-1)
    row_index = jnp.arange(BLOCK)[:, None]
    col_index = jnp.arange(BLOCK)[None, :]
    decay_gaps = cumulative[..., :, None] - cumulative[..., None, :]
    causal = jnp.exp(jnp.where(row_index >= col_index, decay_gaps, -1e+30))
    strict = jnp.where(row_index > col_index, causal, 0.0)
    key_gram = jnp.einsum('hncd,hnmd->hncm', key_rows, key_rows, precision=highest)
    strict_lower = betas[..., :, None] * key_gram * strict
    grown = jnp.exp(cumulative)[..., None]
    right_side = jnp.concatenate([betas[..., None] * key_rows * grown, betas[..., None] * values], axis=-1)
    solved = lower_solve(strict_lower, right_side)
    wide_keys = solved[..., :DK]
    new_values = solved[..., DK:]
    scores = jnp.einsum('hncd,hnmd->hncm', queries, key_rows, precision=highest) * causal
    readers = queries * grown - jnp.einsum('hncm,hnmd->hncd', scores, wide_keys, precision=highest)
    local_out = jnp.einsum('hncm,hnme->hnce', scores, new_values, precision=highest)
    last_sum = cumulative[..., -1:]
    faded_keys = key_rows * jnp.exp(last_sum - cumulative)[..., None]
    identity = jnp.eye(DK, dtype=jnp.float32)
    transfer = jnp.exp(last_sum)[..., None] * identity - jnp.einsum('hncd,hnce->hnde', faded_keys, wide_keys, precision=highest)
    inject = jnp.einsum('hncd,hnce->hnde', faded_keys, new_values, precision=highest)
    return (readers, local_out, transfer, inject)

def apply_state(readers, state):
    return jnp.einsum('hcd,hde->hce', readers, state, precision=highest)

def advance(transfer, state):
    return jnp.einsum('hde,hef->hdf', transfer, state, precision=highest)

def gate_norm(mixer_out, gate_part, value_gain):
    normed = mixer_out * lax.rsqrt(lax.optimization_barrier(jnp.mean(mixer_out * mixer_out, axis=-1, keepdims=True)) + EPSILON) * value_gain
    gated = normed * jax.nn.silu(gate_part.astype(jnp.float32))
    return gated.reshape(mixer_out.shape[0], -1).astype(jnp.bfloat16)

def reference(tokens, input_gain, mixer_weight, rate_weight, conv_kernel, decay_scale, decay_bias, value_gain, output_weight, start_state, post_gain, expert_gateup, expert_down, route_ids, route_weights):
    conv_width = 2 * DK + HV // HK * DV

    def segment_step(carried, seg_tokens):
        state, tail_rows = carried
        normed = rms_scale(seg_tokens, input_gain).astype(jnp.bfloat16)
        projected = jnp.dot(normed, mixer_weight, preferred_element_type=jnp.float32).astype(jnp.bfloat16).reshape(SEG_LEN, HK, -1)
        rate_rows = jnp.dot(normed, rate_weight.reshape(D, -1), preferred_element_type=jnp.float32).astype(jnp.bfloat16).reshape(SEG_LEN, HK, -1)
        pre_conv = projected[..., :conv_width]
        activated = short_conv(pre_conv, tail_rows, conv_kernel)
        queries, key_rows, values, betas, decays = head_inputs(activated, rate_rows, decay_scale, decay_bias)
        readers, local_out, transfer, inject = block_terms(queries, key_rows, values, betas, decays)
        stacked = tuple((jnp.moveaxis(member, 1, 0) for member in (readers, local_out, transfer, inject)))

        def block_step(inner, block_parts):
            out_rows = apply_state(block_parts[0], inner) + block_parts[1]
            return (advance(block_parts[2], inner) + block_parts[3], out_rows)
        state_end, outputs = lax.scan(block_step, state, stacked)
        mixer_out = jnp.moveaxis(outputs, 0, 1).reshape(HV, SEG_LEN, DV).transpose(1, 0, 2)
        gate_part = projected[..., conv_width:].reshape(SEG_LEN, HV, DV)
        gated = gate_norm(mixer_out, gate_part, value_gain)
        mixed = jnp.dot(gated, output_weight, preferred_element_type=jnp.float32)
        hidden_state = seg_tokens.astype(jnp.float32) + mixed
        return ((state_end, pre_conv[SEG_LEN - (KCONV - 1):]), (hidden_state, state_end))
    tail_start = jnp.zeros((KCONV - 1, HK, conv_width), jnp.bfloat16)
    _, (hidden_all, segment_states) = lax.scan(segment_step, (start_state, tail_start), tokens)
    total_rows = SEGS * SEG_LEN
    flat_hidden = hidden_all.reshape(total_rows, D)
    post = rms_scale(flat_hidden, post_gain).astype(jnp.bfloat16)
    device_blocks = total_rows // TOK_DEV
    id_rows = route_ids.reshape(device_blocks, TOK_DEV * ROUTES)
    onehot = (id_rows[..., None] == jnp.arange(EXPERTS)[None, None, :]).astype(jnp.int32)
    slots = lax.optimization_barrier(jnp.sum((jnp.cumsum(onehot, axis=1) - onehot) * onehot, axis=-1))
    block_number = jnp.arange(device_blocks, dtype=jnp.int32)[:, None]
    token_index = block_number * TOK_DEV + jnp.arange(TOK_DEV * ROUTES, dtype=jnp.int32)[None, :] // ROUTES
    target = (id_rows * device_blocks + block_number) * CAP + slots
    source_row = jnp.zeros(EXPERTS * device_blocks * CAP, jnp.int32).at[target.reshape(-1)].set(token_index.reshape(-1)).reshape(EXPERTS, -1)
    slot_weight = jnp.zeros(EXPERTS * device_blocks * CAP, jnp.float32).at[target.reshape(-1)].set(route_weights.reshape(-1)).reshape(EXPERTS, -1)

    def expert_step(accum, expert_parts):
        rows_index, weight_rows, gateup, down_proj = expert_parts
        picked = post[rows_index]
        gate_up = jnp.dot(picked, gateup, preferred_element_type=jnp.float32)
        expert_hidden = (jax.nn.silu(gate_up[:, :FFE]) * gate_up[:, FFE:]).astype(jnp.bfloat16)
        expert_out = jnp.dot(expert_hidden, down_proj, preferred_element_type=jnp.float32).astype(jnp.bfloat16)
        return (accum.at[rows_index].add(weight_rows[:, None] * expert_out.astype(jnp.float32)), None)
    routed, _ = lax.scan(expert_step, jnp.zeros((total_rows, D), jnp.float32), (source_row, slot_weight, expert_gateup, expert_down))
    layer_out = (flat_hidden + routed).reshape(SEGS, SEG_LEN, D)
    return (layer_out, segment_states)
```

```python
import functools

import jax
import jax.numpy as jnp
from jax import lax
from jax.experimental import pallas as pl
from jax.experimental.pallas import tpu as pltpu
from jax.sharding import Mesh
from jax.sharding import PartitionSpec as P

DK = 128
DV = 128
FFE = 512
HEADS = 2
ROUTES = 4
CHUNK = 128
EPSILON = 1e-06
CTX = ("y", "core")
EXP = ("x", "z")
bf16 = jnp.bfloat16
f32 = jnp.float32
highest = lax.Precision.HIGHEST
VMEM = pl.BlockSpec(memory_space=pltpu.VMEM)
SMEM = pl.BlockSpec(memory_space=pltpu.SMEM)
GRANT = 56 * 1024 * 1024


def mm(a, b):
    return jnp.dot(a.astype(bf16), b.astype(bf16), preferred_element_type=f32)


def mm_t(a, b):
    return lax.dot_general(
        a.astype(bf16), b.astype(bf16), (((1,), (1,)), ((), ())), preferred_element_type=f32
    )


def rms_scale(values, scaling):
    widened = values.astype(f32)
    return (
        widened * lax.rsqrt(jnp.mean(widened * widened, axis=-1, keepdims=True) + EPSILON) * scaling
    )


def unit_rows(values):
    return values * lax.rsqrt(jnp.sum(values * values, axis=-1, keepdims=True) + EPSILON)


def silu(values):
    return values / (1.0 + jnp.exp(-values))


def square_iota(size, axis):
    return lax.broadcasted_iota(jnp.int32, (size, size), axis)


def delta_kernel(
    seg_ref, halo_ref, weight_ref, conv_ref, rate_par_ref,
    gate_ref, reader_ref, local_ref, summary_ref, packed_ref,
    rows_scr, rate_scr,
):
    seg_rows = seg_ref.shape[0]
    width = conv_ref.shape[1]
    steps = seg_rows // CHUNK

    def project(rows):
        return jnp.dot(rows, weight_ref[...], preferred_element_type=f32).astype(bf16)

    rows_scr[0:8, :] = project(halo_ref[...])[:, :width].astype(f32)

    def project_step(i, _):
        at = pl.multiple_of(i * CHUNK, CHUNK)
        made = project(seg_ref[pl.ds(at, CHUNK), :])
        rows_scr[pl.ds(pl.multiple_of(at + 8, 8), CHUNK), :] = made[:, :width].astype(f32)
        gate_ref[pl.ds(at, CHUNK), :] = made[:, width : width + HEADS * DV]
        rate_scr[pl.ds(at, CHUNK), :] = made[:, width + HEADS * DV :].astype(f32)
        return 0

    lax.fori_loop(0, steps, project_step, 0)

    row = square_iota(CHUNK, 0)
    col = square_iota(CHUNK, 1)
    lower = (row >= col).astype(f32)
    eye = (row == col).astype(f32)
    for h in range(HEADS):
        summary_ref[h, :, :DK] = eye
        summary_ref[h, :, DK:] = jnp.zeros((DK, DV), f32)

    pair = 2

    def chunk_step(i, _):
        units = []
        for u in range(pair):
            at = pl.multiple_of((i * pair + u) * CHUNK, CHUNK)
            window = rows_scr[pl.ds(at, CHUNK + 8), :]
            summed = conv_ref[0:1, :] * window[5 : 5 + CHUNK]
            for tap in range(1, 4):
                summed = summed + conv_ref[tap : tap + 1, :] * window[5 + tap : 5 + tap + CHUNK]
            active = silu(summed)
            query = unit_rows(active[:, :DK]) * DK ** (-0.5)
            key = unit_rows(active[:, DK : 2 * DK])
            rate = rate_scr[pl.ds(at, CHUNK), :]
            shifted = rate + rate_par_ref[0:1, :]
            soft = jnp.maximum(shifted, 0.0) + jnp.log1p(jnp.exp(-jnp.abs(shifted)))
            decay = -rate_par_ref[1:2, :] * soft
            beta_all = 1.0 / (1.0 + jnp.exp(-rate))
            total = jnp.dot(lower, decay, preferred_element_type=f32, precision=highest)
            total_t = total.T
            key_low = key.astype(bf16)
            gram = mm_t(key_low, key_low)
            raw_scores = mm_t(query, key_low)
            for h in range(HEADS):
                cum = total[:, HEADS + h : HEADS + h + 1]
                cum_row = total_t[HEADS + h : HEADS + h + 1, :]
                beta = beta_all[:, h : h + 1]
                causal = jnp.exp(jnp.where(row >= col, cum - cum_row, -1e30))
                grown = jnp.exp(cum)
                last = cum[CHUNK - 1 : CHUNK, :]
                value = active[:, 2 * DK + h * DV : 2 * DK + (h + 1) * DV]
                units.append(
                    dict(
                        at=at,
                        h=h,
                        low=jnp.where(row > col, beta * gram * causal, 0.0),
                        right=jnp.concatenate([beta * key * grown, beta * value], axis=1).astype(bf16),
                        scores=(raw_scores * causal).astype(bf16),
                        read=(query * grown).astype(bf16),
                        faded=(key * jnp.exp(last - cum)).T.astype(bf16),
                        fade=jnp.exp(last),
                    )
                )
        inverses = [
            eye - jnp.where((row // 2 == col // 2), unit["low"], 0.0) for unit in units
        ]
        size = 2
        while size < CHUNK:
            off = (row // (2 * size) == col // (2 * size)) & (row // size != col // size)
            lows = [x.astype(bf16) for x in inverses]
            firsts = [mm(jnp.where(off, unit["low"], 0.0), x) for unit, x in zip(units, lows)]
            inverses = [x - mm(x_low, y) for x, x_low, y in zip(inverses, lows, firsts)]
            size *= 2
        solved = [mm(x, unit["right"]) for unit, x in zip(units, inverses)]
        for unit, done in zip(units, solved):
            h = unit["h"]
            state = summary_ref[h]
            stacked = jnp.concatenate([done[:, :DK].astype(bf16), unit["read"]], axis=0)
            applied = mm(stacked, state)
            fresh = jnp.concatenate([-applied[:CHUNK, :DK], done[:, DK:] - applied[:CHUNK, DK:]], axis=1)
            fresh = fresh.astype(bf16)
            out = applied[CHUNK:] + mm(unit["scores"], fresh)
            summary_ref[h] = unit["fade"] * state + mm(unit["faded"], fresh)
            reader_ref[h, pl.ds(unit["at"], CHUNK), :] = out[:, :DK].astype(bf16)
            local_ref[h, pl.ds(unit["at"], CHUNK), :] = out[:, DK:]
        return 0

    lax.fori_loop(0, steps // pair, chunk_step, 0)
    for h in range(HEADS):
        packed_ref[h, :, :DK] = (summary_ref[h, :, :DK] - eye).astype(bf16)
        packed_ref[h, :, DK:] = summary_ref[h, :, DK:].astype(bf16)


def run_delta(segment, halo, weight, conv, rate_par):
    rows = segment.shape[0]
    return pl.pallas_call(
        delta_kernel,
        out_shape=(
            jax.ShapeDtypeStruct((rows, HEADS * DV), bf16),
            jax.ShapeDtypeStruct((HEADS, rows, DK), bf16),
            jax.ShapeDtypeStruct((HEADS, rows, DV), f32),
            jax.ShapeDtypeStruct((HEADS, DK, DK + DV), f32),
            jax.ShapeDtypeStruct((HEADS, DK, DK + DV), bf16),
        ),
        in_specs=[VMEM] * 5,
        out_specs=(VMEM,) * 5,
        scratch_shapes=[
            pltpu.VMEM((rows + 8, conv.shape[1]), f32),
            pltpu.VMEM((rows, 128), f32),
        ],
        compiler_params=pltpu.CompilerParams(vmem_limit_bytes=GRANT),
        name="delta",
        cost_estimate=pl.CostEstimate(flops=12 * 10**9, bytes_accessed=12 * 10**6, transcendentals=0),
    )(segment, halo, weight, conv, rate_par)


def compose(state, packed):
    moved = state + mm(packed[:, :DK], state)
    return moved, packed[:, DK:].astype(f32)


def row_kernel(place_ref, all_ref, prefix_ref, total_ref):
    place = place_ref[0]
    count = all_ref.shape[0]
    eye = (square_iota(DK, 0) == square_iota(DK, 1)).astype(f32)
    zero = jnp.zeros((DK, DV), f32)
    states = [jnp.concatenate([eye, zero], axis=1) for _ in range(HEADS)]
    for j in range(count):
        for h in range(HEADS):
            state = states[h]

            @pl.when(place == j)
            def _(state=state, h=h):
                prefix_ref[h] = state

            moved, added = compose(state, all_ref[j, h])
            states[h] = jnp.concatenate([moved[:, :DK], moved[:, DK:] + added], axis=1)
    for h in range(HEADS):
        total_ref[h, :, :DK] = (states[h][:, :DK] - eye).astype(bf16)
        total_ref[h, :, DK:] = states[h][:, DK:].astype(bf16)


def run_row(place, gathered):
    return pl.pallas_call(
        row_kernel,
        out_shape=(
            jax.ShapeDtypeStruct(gathered.shape[1:], f32),
            jax.ShapeDtypeStruct(gathered.shape[1:], bf16),
        ),
        in_specs=[SMEM, VMEM],
        out_specs=(VMEM, VMEM),
        compiler_params=pltpu.CompilerParams(vmem_limit_bytes=GRANT),
        name="row",
    )(place, gathered)


def finish_kernel(
    place_ref, rows_ref, start_ref, prefix_ref, summary_ref, reader_ref, local_ref, gate_ref, gain_ref, weight_ref,
    out_ref, final_ref,
):
    place = place_ref[0]
    count = rows_ref.shape[0]
    eye = (square_iota(DK, 0) == square_iota(DK, 1)).astype(f32)
    entering = []
    for h in range(HEADS):
        state = start_ref[h]
        for j in range(count - 1):
            moved, added = compose(state, rows_ref[j, h])
            state = jnp.where(place > j, moved + added, state)
        state = state + mm(prefix_ref[h, :, :DK] - eye, state) + prefix_ref[h, :, DK:]
        final_ref[h] = state + mm(summary_ref[h, :, :DK] - eye, state) + summary_ref[h, :, DK:]
        entering.append(state.astype(bf16))

    def tile(i, _):
        at = pl.ds(pl.multiple_of(i * CHUNK, CHUNK), CHUNK)
        parts = []
        for h in range(HEADS):
            mixed = mm(reader_ref[h, at, :], entering[h]) + local_ref[h, at, :]
            gate = gate_ref[at, h * DV : (h + 1) * DV].astype(f32)
            parts.append((rms_scale(mixed, gain_ref[...]) * silu(gate)).astype(bf16))
        gated = jnp.concatenate(parts, axis=1)
        out_ref[at, :] = jnp.dot(gated, weight_ref[...], preferred_element_type=f32).astype(bf16)
        return 0

    lax.fori_loop(0, reader_ref.shape[1] // CHUNK, tile, 0)


def run_finish(place, rows, start, prefix, summary, reader, local, gate, gain, weight):
    return pl.pallas_call(
        finish_kernel,
        out_shape=(
            jax.ShapeDtypeStruct((gate.shape[0], weight.shape[1]), bf16),
            jax.ShapeDtypeStruct(start.shape, f32),
        ),
        in_specs=[SMEM] + [VMEM] * 9,
        out_specs=(VMEM, VMEM),
        compiler_params=pltpu.CompilerParams(vmem_limit_bytes=GRANT),
        name="finish",
    )(place, rows, start, prefix, summary, reader, local, gate, gain, weight)


def dispatch_kernel(own_ref, mixed_ref, gain_ref, pick_ref, hidden_ref, out_ref):
    hidden = own_ref[...].astype(f32) + mixed_ref[...].astype(f32)
    hidden_ref[...] = hidden
    post = rms_scale(hidden, gain_ref[...]).astype(bf16)
    half = post.shape[1] // 2
    stacked = jnp.concatenate([post[:, :half], post[:, half:]], axis=0)
    out_ref[...] = jnp.dot(pick_ref[...], stacked, preferred_element_type=f32).astype(bf16)


def run_dispatch(own, mixed, gain, pick):
    return pl.pallas_call(
        dispatch_kernel,
        out_shape=(
            jax.ShapeDtypeStruct(own.shape, f32),
            jax.ShapeDtypeStruct((pick.shape[0], own.shape[1] // 2), bf16),
        ),
        in_specs=[VMEM] * 4,
        out_specs=(VMEM, VMEM),
        compiler_params=pltpu.CompilerParams(vmem_limit_bytes=GRANT),
        name="dispatch",
    )(own, mixed, gain, pick)


def expert_kernel(rows_ref, up_ref, down_ref, out_ref):
    count, _, half = rows_ref.shape

    def hidden_of(gate_up):
        return (silu(gate_up[:, :FFE]) * gate_up[:, FFE:]).astype(bf16)

    group = 8

    def step(i, _):
        some = pl.ds(i * group, group)
        left = rows_ref[some, 0:16, :].reshape(group * 16, half)
        right = rows_ref[some, 16:32, :].reshape(group * 16, half)
        gate_up = jnp.dot(left, up_ref[:half, :], preferred_element_type=f32) + jnp.dot(
            right, up_ref[half:, :], preferred_element_type=f32
        )
        done = jnp.dot(hidden_of(gate_up), down_ref[...], preferred_element_type=f32).astype(bf16)
        out_ref[some, 0:16, :] = done[:, :half].reshape(group, 16, half)
        out_ref[some, 16:32, :] = done[:, half:].reshape(group, 16, half)
        return 0

    lax.fori_loop(0, count // group, step, 0)
    tail = rows_ref[:, 32:40, :].reshape(count * 8, half)
    first = jnp.dot(tail, up_ref[:half, :], preferred_element_type=f32)
    second = jnp.dot(tail, up_ref[half:, :], preferred_element_type=f32)
    turned = count * 8 - 4
    gate_up = first + pltpu.roll(second, turned, 0)
    done = jnp.dot(hidden_of(gate_up), down_ref[...], preferred_element_type=f32)
    upper = lax.broadcasted_iota(jnp.int32, (count * 8, half), 0) % 8 < 4
    packed = jnp.where(upper, done[:, :half], pltpu.roll(done[:, half:], 4, 0)).astype(bf16)
    out_ref[:, 32:40, :] = packed.reshape(count, 8, half)


def run_expert(rows, up, down):
    return pl.pallas_call(
        expert_kernel,
        out_shape=jax.ShapeDtypeStruct(rows.shape, bf16),
        in_specs=[VMEM] * 3,
        out_specs=VMEM,
        compiler_params=pltpu.CompilerParams(vmem_limit_bytes=GRANT),
        name="expert",
    )(rows, up, down)


def combine_kernel(hidden_ref, back_ref, high_ref, low_ref, out_ref):
    rows = hidden_ref.shape[0]
    half = back_ref.shape[1]
    back = back_ref[...]
    routed = jnp.dot(high_ref[...], back, preferred_element_type=f32) + jnp.dot(
        low_ref[...], back, preferred_element_type=f32
    )
    out_ref[:, :half] = hidden_ref[:, :half] + routed[:rows]
    out_ref[:, half:] = hidden_ref[:, half:] + routed[rows:]


def run_combine(hidden, back, high, low):
    return pl.pallas_call(
        combine_kernel,
        out_shape=jax.ShapeDtypeStruct(hidden.shape, f32),
        in_specs=[VMEM] * 4,
        out_specs=VMEM,
        compiler_params=pltpu.CompilerParams(vmem_limit_bytes=GRANT),
        name="combine",
    )(hidden, back, high, low)


def slot_rows(ids, experts):
    rows = ids.shape[0]
    choice = ids[:, :, None] == jnp.arange(experts, dtype=jnp.int32)
    named = jnp.any(choice, axis=1).astype(bf16)
    before = jnp.tril(jnp.ones((rows, rows), bf16), -1)
    ranks = jnp.dot(before, named, preferred_element_type=f32)
    slots = jnp.sum(jnp.where(choice, ranks[:, None, :], 0.0), axis=2).astype(jnp.int32)
    early = slots < 16
    left = ids * 40 + jnp.where(early, slots, slots + 16)
    right = ids * 40 + jnp.where(early, slots + 16, slots + 20)
    return jnp.concatenate([left, right], axis=0)


def body(
    tokens,
    input_gain,
    mixer_weight,
    rate_weight,
    conv_kernel,
    decay_scale,
    decay_bias,
    value_gain,
    output_weight,
    start_state,
    post_gain,
    expert_gateup,
    expert_down,
    route_ids,
    route_weights,
):
    own = tokens[0]
    model_width = own.shape[1]
    experts = lax.axis_size(EXP)
    normed = rms_scale(own, input_gain).astype(bf16)
    segment = lax.all_gather(normed, CTX, axis=0, tiled=True)
    last_rows = lax.ppermute(normed[-8:], EXP, [(i, i + 1) for i in range(experts - 1)])
    halo = lax.all_gather(last_rows, CTX, axis=0)[-1]
    weight = jnp.concatenate(
        [
            mixer_weight,
            rate_weight.reshape(model_width, -1),
            jnp.zeros((model_width, 128 - 2 * HEADS), bf16),
        ],
        axis=1,
    )
    room = 128 - 2 * HEADS
    rate_par = jnp.stack(
        [
            jnp.concatenate([jnp.zeros(HEADS, f32), decay_bias, jnp.zeros(room, f32)]),
            jnp.concatenate([jnp.zeros(HEADS, f32), decay_scale, jnp.zeros(room, f32)]),
        ]
    )
    gate, reader, local, summary, packed = run_delta(
        segment, halo, weight, conv_kernel[:, 0], rate_par
    )
    depth = lax.axis_size("z")
    gathered = lax.all_to_all(
        jnp.broadcast_to(packed[None], (depth,) + packed.shape), "z", 0, 0, tiled=True
    )
    prefix, total = run_row(lax.axis_index("z").reshape(1), gathered)
    rows = lax.all_gather(total, "x", axis=0)
    partial, final_state = run_finish(
        lax.axis_index("x").reshape(1), rows, start_state, prefix, summary, reader, local, gate,
        value_gain.reshape(1, -1), output_weight,
    )
    mixed = lax.psum_scatter(partial, CTX, scatter_dimension=0, tiled=True)

    places = slot_rows(route_ids[0], experts)
    count = experts * 40
    hits = places[:, :, None] == jnp.arange(count, dtype=jnp.int32)
    pick = jnp.any(
        places.T[:, None, :] == jnp.arange(count, dtype=jnp.int32)[None, :, None], axis=0
    ).astype(bf16)
    doubled = jnp.concatenate([route_weights[0], route_weights[0]], axis=0)
    share = jnp.sum(jnp.where(hits, doubled[:, :, None], 0.0), axis=1)
    high = share.astype(bf16)
    low = (share - high.astype(f32)).astype(bf16)

    hidden, outgoing = run_dispatch(own, mixed, post_gain.reshape(1, -1), pick)
    half = model_width // 2
    arrived = lax.all_to_all(outgoing.reshape(experts, 40, half), EXP, 0, 0, tiled=True)
    made = run_expert(arrived, expert_gateup[0], expert_down[0])
    back = lax.all_to_all(made, EXP, 0, 0, tiled=True)
    layer_out = run_combine(hidden, back.reshape(count, half), high, low)
    return (layer_out[None], final_state[None])


def solution(mesh):
    fine = Mesh(mesh.devices.reshape(4, 2, 4, 8), CTX + EXP)
    in_specs = (
        P(EXP, CTX, None),
        P(),
        P(None, CTX),
        P(None, CTX, None),
        P(None, CTX, None),
        P(CTX),
        P(CTX),
        P(),
        P(CTX, None),
        P(CTX, None, None),
        P(),
        P(EXP, None, None),
        P(EXP, None, None),
        P(EXP, CTX, None),
        P(EXP, CTX, None),
    )
    out_specs = (P(EXP, CTX, None), P(EXP, CTX, None, None))
    return jax.shard_map(body, mesh=fine, in_specs=in_specs, out_specs=out_specs, check_vma=False)
```

```python
import functools

import jax
import jax.numpy as jnp
from jax import lax
from jax.experimental import pallas as pl
from jax.experimental.pallas import tpu as pltpu
from jax.sharding import Mesh
from jax.sharding import PartitionSpec as P

DK = 128
DV = 128
FFE = 512
HEADS = 2
ROUTES = 4
CHUNK = 128
TILE = 512
EPSILON = 1e-06
CTX = ("y", "core")
EXP = ("x", "z")
bf16 = jnp.bfloat16
f32 = jnp.float32
highest = lax.Precision.HIGHEST
VMEM = pl.BlockSpec(memory_space=pltpu.VMEM)
SMEM = pl.BlockSpec(memory_space=pltpu.SMEM)
GRANT = 24 * 1024 * 1024


def mm(a, b):
    return jnp.dot(a.astype(bf16), b.astype(bf16), preferred_element_type=f32)


def mm_t(a, b):
    return lax.dot_general(
        a.astype(bf16), b.astype(bf16), (((1,), (1,)), ((), ())), preferred_element_type=f32
    )


def rms_scale(values, scaling):
    widened = values.astype(f32)
    return (
        widened * lax.rsqrt(jnp.mean(widened * widened, axis=-1, keepdims=True) + EPSILON) * scaling
    )


def unit_rows(values):
    return values * lax.rsqrt(jnp.sum(values * values, axis=-1, keepdims=True) + EPSILON)


def silu(values):
    return values / (1.0 + jnp.exp(-values))


def square_iota(size, axis):
    return lax.broadcasted_iota(jnp.int32, (size, size), axis)


def delta_kernel(
    seg_ref, halo_ref, weight_ref, conv_ref, rate_par_ref,
    gate_ref, reader_ref, local_ref, summary_ref, packed_ref,
    rows_scr, rate_scr,
):
    seg_rows = seg_ref.shape[0]
    width = conv_ref.shape[1]
    steps = seg_rows // CHUNK

    def project(rows):
        return jnp.dot(rows, weight_ref[...], preferred_element_type=f32).astype(bf16)

    rows_scr[0:8, :] = project(halo_ref[...])[:, :width].astype(f32)

    def project_step(i, _):
        at = pl.multiple_of(i * TILE, TILE)
        made = project(seg_ref[pl.ds(at, TILE), :])
        rows_scr[pl.ds(pl.multiple_of(at + 8, 8), TILE), :] = made[:, :width].astype(f32)
        gate_ref[pl.ds(at, TILE), :] = made[:, width : width + HEADS * DV]
        rate_scr[pl.ds(at, TILE), :] = made[:, width + HEADS * DV :].astype(f32)
        return 0

    lax.fori_loop(0, seg_rows // TILE, project_step, 0)

    row = square_iota(CHUNK, 0)
    col = square_iota(CHUNK, 1)
    lower = (row >= col).astype(f32)
    eye = (row == col).astype(f32)
    for h in range(HEADS):
        summary_ref[h, :, :DK] = eye
        summary_ref[h, :, DK:] = jnp.zeros((DK, DV), f32)

    pair = 8

    def chunk_step(i, _):
        units = []
        for u in range(pair):
            at = pl.multiple_of((i * pair + u) * CHUNK, CHUNK)
            window = rows_scr[pl.ds(at, CHUNK + 8), :]
            summed = conv_ref[0:1, :] * window[5 : 5 + CHUNK]
            for tap in range(1, 4):
                summed = summed + conv_ref[tap : tap + 1, :] * window[5 + tap : 5 + tap + CHUNK]
            active = silu(summed)
            query = unit_rows(active[:, :DK]) * DK ** (-0.5)
            key = unit_rows(active[:, DK : 2 * DK])
            rate = rate_scr[pl.ds(at, CHUNK), :]
            shifted = rate + rate_par_ref[0:1, :]
            soft = jnp.maximum(shifted, 0.0) + jnp.log1p(jnp.exp(-jnp.abs(shifted)))
            decay = -rate_par_ref[1:2, :] * soft
            beta_all = 1.0 / (1.0 + jnp.exp(-rate))
            total = jnp.dot(lower, decay, preferred_element_type=f32, precision=highest)
            total_t = total.T
            key_low = key.astype(bf16)
            gram = mm_t(key_low, key_low)
            raw_scores = mm_t(query, key_low)
            for h in range(HEADS):
                cum = total[:, HEADS + h : HEADS + h + 1]
                cum_row = total_t[HEADS + h : HEADS + h + 1, :]
                beta = beta_all[:, h : h + 1]
                causal = jnp.exp(jnp.where(row >= col, cum - cum_row, -1e30))
                grown = jnp.exp(cum)
                last = cum[CHUNK - 1 : CHUNK, :]
                value = active[:, 2 * DK + h * DV : 2 * DK + (h + 1) * DV]
                units.append(
                    dict(
                        at=at,
                        h=h,
                        low=jnp.where(row > col, beta * gram * causal, 0.0),
                        right=jnp.concatenate([beta * key * grown, beta * value], axis=1).astype(bf16),
                        scores=(raw_scores * causal).astype(bf16),
                        read=(query * grown).astype(bf16),
                        faded=(key * jnp.exp(last - cum)).T.astype(bf16),
                        fade=jnp.exp(last),
                    )
                )
        inverses = [
            eye - jnp.where((row // 2 == col // 2), unit["low"], 0.0) for unit in units
        ]
        size = 2
        while size < CHUNK:
            off = (row // (2 * size) == col // (2 * size)) & (row // size != col // size)
            lows = [x.astype(bf16) for x in inverses]
            firsts = [mm(jnp.where(off, unit["low"], 0.0), x) for unit, x in zip(units, lows)]
            inverses = [x - mm(x_low, y) for x, x_low, y in zip(inverses, lows, firsts)]
            size *= 2
        solved = [mm(x, unit["right"]) for unit, x in zip(units, inverses)]
        for unit, done in zip(units, solved):
            h = unit["h"]
            state = summary_ref[h]
            stacked = jnp.concatenate([done[:, :DK].astype(bf16), unit["read"]], axis=0)
            applied = mm(stacked, state)
            fresh = jnp.concatenate([-applied[:CHUNK, :DK], done[:, DK:] - applied[:CHUNK, DK:]], axis=1)
            fresh = fresh.astype(bf16)
            out = applied[CHUNK:] + mm(unit["scores"], fresh)
            summary_ref[h] = unit["fade"] * state + mm(unit["faded"], fresh)
            reader_ref[h, pl.ds(unit["at"], CHUNK), :] = out[:, :DK].astype(bf16)
            local_ref[h, pl.ds(unit["at"], CHUNK), :] = out[:, DK:]
        return 0

    lax.fori_loop(0, steps // pair, chunk_step, 0)
    for h in range(HEADS):
        change = summary_ref[h, :, :DK] - eye
        summary_ref[h, :, :DK] = change
        packed_ref[h, :, :DK] = change.astype(bf16)
        packed_ref[h, :, DK:] = summary_ref[h, :, DK:].astype(bf16)


def run_delta(segment, halo, weight, conv, rate_par):
    rows = segment.shape[0]
    return pl.pallas_call(
        delta_kernel,
        out_shape=(
            jax.ShapeDtypeStruct((rows, HEADS * DV), bf16),
            jax.ShapeDtypeStruct((HEADS, rows, DK), bf16),
            jax.ShapeDtypeStruct((HEADS, rows, DV), f32),
            jax.ShapeDtypeStruct((HEADS, DK, DK + DV), f32),
            jax.ShapeDtypeStruct((HEADS, DK, DK + DV), bf16),
        ),
        in_specs=[VMEM] * 5,
        out_specs=(VMEM,) * 5,
        scratch_shapes=[
            pltpu.VMEM((rows + 8, conv.shape[1]), f32),
            pltpu.VMEM((rows, 128), f32),
        ],
        compiler_params=pltpu.CompilerParams(vmem_limit_bytes=GRANT),
        name="delta",
        cost_estimate=pl.CostEstimate(flops=12 * 10**9, bytes_accessed=12 * 10**6, transcendentals=0),
    )(segment, halo, weight, conv, rate_par)


def then(first, second):
    return first + mm(second[:, :DK], first) + second.astype(f32)


def apply(change, state):
    return state + mm(change[:, :DK], state) + change[:, DK:].astype(f32)


def couple_kernel(place_ref, own_ref, other_ref, both_ref):
    odd = place_ref[0] % 2 == 1
    for h in range(HEADS):
        own = own_ref[h].astype(f32)
        other = other_ref[h].astype(f32)
        both_ref[h] = then(jnp.where(odd, other, own), jnp.where(odd, own, other)).astype(bf16)


def run_couple(place, own, other):
    return pl.pallas_call(
        couple_kernel,
        out_shape=jax.ShapeDtypeStruct(own.shape, bf16),
        in_specs=[SMEM, VMEM, VMEM],
        out_specs=VMEM,
        compiler_params=pltpu.CompilerParams(vmem_limit_bytes=8 * 1024 * 1024),
        name="couple",
    )(place, own, other)


def row_kernel(place_ref, own_ref, back1_ref, back2_ref, back3_ref, other_ref, prefix_ref, total_ref, all_scr):
    odd = place_ref[0] % 2 == 1
    place = place_ref[0] // 2
    for offset, ref in enumerate((own_ref, back1_ref, back2_ref, back3_ref)):
        all_scr[(place + 4 - offset) % 4] = ref[...]
    changes = [jnp.zeros((DK, DK + DV), f32) for _ in range(HEADS)]
    for j in range(4):
        for h in range(HEADS):
            change = changes[h]

            @pl.when(place == j)
            def _(change=change, h=h):
                prefix_ref[h] = change

            changes[h] = then(change, all_scr[j, h])
    for h in range(HEADS):
        total_ref[h] = changes[h].astype(bf16)
        before = prefix_ref[h]
        prefix_ref[h] = jnp.where(odd, then(before, other_ref[h]), before)


def run_row(place, own, back1, back2, back3, other):
    return pl.pallas_call(
        row_kernel,
        out_shape=(
            jax.ShapeDtypeStruct(own.shape, f32),
            jax.ShapeDtypeStruct(own.shape, bf16),
        ),
        in_specs=[SMEM] + [VMEM] * 5,
        out_specs=(VMEM, VMEM),
        scratch_shapes=[pltpu.VMEM((4,) + own.shape, bf16)],
        compiler_params=pltpu.CompilerParams(vmem_limit_bytes=8 * 1024 * 1024),
        name="row",
    )(place, own, back1, back2, back3, other)


def finish_kernel(
    place_ref, back1_ref, back2_ref, back3_ref, start_ref, prefix_ref, summary_ref, reader_ref, local_ref, gate_ref,
    gain_ref, weight_ref, out_ref, final_ref,
):
    place = place_ref[0]
    entering = []
    for h in range(HEADS):
        state = start_ref[h]
        for offset, ref in ((3, back3_ref), (2, back2_ref), (1, back1_ref)):
            state = jnp.where(place >= offset, apply(ref[h], state), state)
        state = apply(prefix_ref[h], state)
        final_ref[h] = apply(summary_ref[h], state)
        entering.append(state.astype(bf16))

    def tile(i, _):
        at = pl.ds(pl.multiple_of(i * TILE, TILE), TILE)
        parts = []
        for h in range(HEADS):
            mixed = mm(reader_ref[h, at, :], entering[h]) + local_ref[h, at, :]
            gate = gate_ref[at, h * DV : (h + 1) * DV].astype(f32)
            parts.append((rms_scale(mixed, gain_ref[...]) * silu(gate)).astype(bf16))
        gated = jnp.concatenate(parts, axis=1)
        out_ref[at, :] = jnp.dot(gated, weight_ref[...], preferred_element_type=f32).astype(bf16)
        return 0

    lax.fori_loop(0, reader_ref.shape[1] // TILE, tile, 0)


def run_finish(place, back1, back2, back3, start, prefix, summary, reader, local, gate, gain, weight):
    return pl.pallas_call(
        finish_kernel,
        out_shape=(
            jax.ShapeDtypeStruct((gate.shape[0], weight.shape[1]), bf16),
            jax.ShapeDtypeStruct(start.shape, f32),
        ),
        in_specs=[SMEM] + [VMEM] * 11,
        out_specs=(VMEM, VMEM),
        compiler_params=pltpu.CompilerParams(vmem_limit_bytes=GRANT),
        name="finish",
    )(place, back1, back2, back3, start, prefix, summary, reader, local, gate, gain, weight)


def dispatch_kernel(own_ref, mixed_ref, gain_ref, pick_ref, hidden_ref, out_ref):
    hidden = own_ref[...].astype(f32) + mixed_ref[...].astype(f32)
    hidden_ref[...] = hidden
    post = rms_scale(hidden, gain_ref[...]).astype(bf16)
    half = post.shape[1] // 2
    stacked = jnp.concatenate([post[:, :half], post[:, half:]], axis=0)
    out_ref[...] = jnp.dot(pick_ref[...], stacked, preferred_element_type=f32).astype(bf16)


def run_dispatch(own, mixed, gain, pick):
    return pl.pallas_call(
        dispatch_kernel,
        out_shape=(
            jax.ShapeDtypeStruct(own.shape, f32),
            jax.ShapeDtypeStruct((pick.shape[0], own.shape[1] // 2), bf16),
        ),
        in_specs=[VMEM] * 4,
        out_specs=(VMEM, VMEM),
        compiler_params=pltpu.CompilerParams(vmem_limit_bytes=GRANT),
        name="dispatch",
    )(own, mixed, gain, pick)


def expert_kernel(rows_ref, up_ref, down_ref, out_ref):
    count, _, half = rows_ref.shape

    def hidden_of(gate_up):
        return (silu(gate_up[:, :FFE]) * gate_up[:, FFE:]).astype(bf16)

    group = 32

    def step(i, _):
        some = pl.ds(i * group, group)
        left = rows_ref[some, 0:16, :].reshape(group * 16, half)
        right = rows_ref[some, 16:32, :].reshape(group * 16, half)
        gate_up = jnp.dot(left, up_ref[:half, :], preferred_element_type=f32) + jnp.dot(
            right, up_ref[half:, :], preferred_element_type=f32
        )
        done = jnp.dot(hidden_of(gate_up), down_ref[...], preferred_element_type=f32).astype(bf16)
        out_ref[some, 0:16, :] = done[:, :half].reshape(group, 16, half)
        out_ref[some, 16:32, :] = done[:, half:].reshape(group, 16, half)
        return 0

    lax.fori_loop(0, count // group, step, 0)
    tail = rows_ref[:, 32:40, :].reshape(count * 8, half)
    first = jnp.dot(tail, up_ref[:half, :], preferred_element_type=f32)
    second = jnp.dot(tail, up_ref[half:, :], preferred_element_type=f32)
    turned = count * 8 - 4
    gate_up = first + pltpu.roll(second, turned, 0)
    done = jnp.dot(hidden_of(gate_up), down_ref[...], preferred_element_type=f32)
    upper = lax.broadcasted_iota(jnp.int32, (count * 8, half), 0) % 8 < 4
    packed = jnp.where(upper, done[:, :half], pltpu.roll(done[:, half:], 4, 0)).astype(bf16)
    out_ref[:, 32:40, :] = packed.reshape(count, 8, half)


def run_expert(rows, up, down):
    return pl.pallas_call(
        expert_kernel,
        out_shape=jax.ShapeDtypeStruct(rows.shape, bf16),
        in_specs=[VMEM] * 3,
        out_specs=VMEM,
        compiler_params=pltpu.CompilerParams(vmem_limit_bytes=GRANT),
        name="expert",
    )(rows, up, down)


def combine_kernel(hidden_ref, back_ref, high_ref, low_ref, out_ref):
    rows = hidden_ref.shape[0]
    half = back_ref.shape[1]
    back = back_ref[...]
    routed = jnp.dot(high_ref[...], back, preferred_element_type=f32) + jnp.dot(
        low_ref[...], back, preferred_element_type=f32
    )
    out_ref[:, :half] = hidden_ref[:, :half] + routed[:rows]
    out_ref[:, half:] = hidden_ref[:, half:] + routed[rows:]


def run_combine(hidden, back, high, low):
    return pl.pallas_call(
        combine_kernel,
        out_shape=jax.ShapeDtypeStruct(hidden.shape, f32),
        in_specs=[VMEM] * 4,
        out_specs=VMEM,
        compiler_params=pltpu.CompilerParams(vmem_limit_bytes=GRANT),
        name="combine",
    )(hidden, back, high, low)


def turned(size, distance):
    return [(i, (i + distance) % size) for i in range(size)]


def slot_rows(ids, experts):
    rows = ids.shape[0]
    choice = ids[:, :, None] == jnp.arange(experts, dtype=jnp.int32)
    named = jnp.any(choice, axis=1).astype(bf16)
    before = jnp.tril(jnp.ones((rows, rows), bf16), -1)
    ranks = jnp.dot(before, named, preferred_element_type=f32)
    slots = jnp.sum(jnp.where(choice, ranks[:, None, :], 0.0), axis=2).astype(jnp.int32)
    early = slots < 16
    left = ids * 40 + jnp.where(early, slots, slots + 16)
    right = ids * 40 + jnp.where(early, slots + 16, slots + 20)
    return jnp.concatenate([left, right], axis=0)


def body(
    tokens,
    input_gain,
    mixer_weight,
    rate_weight,
    conv_kernel,
    decay_scale,
    decay_bias,
    value_gain,
    output_weight,
    start_state,
    post_gain,
    expert_gateup,
    expert_down,
    route_ids,
    route_weights,
):
    own = tokens[0]
    model_width = own.shape[1]
    experts = lax.axis_size(EXP)
    normed = rms_scale(own, input_gain).astype(bf16)
    segment = lax.all_gather(normed, CTX, axis=0, tiled=True)
    last_rows = lax.ppermute(normed[-8:], EXP, [(i, i + 1) for i in range(experts - 1)])
    halo = lax.all_gather(last_rows, CTX, axis=0)[-1]
    weight = jnp.concatenate(
        [
            mixer_weight,
            rate_weight.reshape(model_width, -1),
            jnp.zeros((model_width, 128 - 2 * HEADS), bf16),
        ],
        axis=1,
    )
    room = 128 - 2 * HEADS
    rate_par = jnp.stack(
        [
            jnp.concatenate([jnp.zeros(HEADS, f32), decay_bias, jnp.zeros(room, f32)]),
            jnp.concatenate([jnp.zeros(HEADS, f32), decay_scale, jnp.zeros(room, f32)]),
        ]
    )
    gate, reader, local, summary, packed = run_delta(
        segment, halo, weight, conv_kernel[:, 0], rate_par
    )
    depth = lax.axis_size("z")
    along_z = lax.axis_index("z").reshape(1)
    other = lax.ppermute(packed, "z", [(i, i ^ 1) for i in range(depth)])
    both = run_couple(along_z, packed, other)
    pairs = [lax.ppermute(both, "z", turned(depth, 2 * step)) for step in (1, 2, 3)]
    prefix, total = run_row(along_z, both, *pairs, other)
    rows = [lax.ppermute(total, "x", turned(lax.axis_size("x"), step)) for step in (1, 2, 3)]
    partial, final_state = run_finish(
        lax.axis_index("x").reshape(1), *rows, start_state, prefix, summary, reader, local, gate,
        value_gain.reshape(1, -1), output_weight,
    )
    mixed = lax.psum_scatter(partial, CTX, scatter_dimension=0, tiled=True)

    places = slot_rows(route_ids[0], experts)
    count = experts * 40
    hits = places[:, :, None] == jnp.arange(count, dtype=jnp.int32)
    pick = jnp.any(
        places.T[:, None, :] == jnp.arange(count, dtype=jnp.int32)[None, :, None], axis=0
    ).astype(bf16)
    doubled = jnp.concatenate([route_weights[0], route_weights[0]], axis=0)
    share = jnp.sum(jnp.where(hits, doubled[:, :, None], 0.0), axis=1)
    high = share.astype(bf16)
    low = (share - high.astype(f32)).astype(bf16)

    hidden, outgoing = run_dispatch(own, mixed, post_gain.reshape(1, -1), pick)
    half = model_width // 2
    arrived = lax.all_to_all(outgoing.reshape(experts, 40, half), EXP, 0, 0, tiled=True)
    made = run_expert(arrived, expert_gateup[0], expert_down[0])
    back = lax.all_to_all(made, EXP, 0, 0, tiled=True)
    layer_out = run_combine(hidden, back.reshape(count, half), high, low)
    return (layer_out[None], final_state[None])


def solution(mesh):
    fine = Mesh(mesh.devices.reshape(4, 2, 4, 8), CTX + EXP)
    in_specs = (
        P(EXP, CTX, None),
        P(),
        P(None, CTX),
        P(None, CTX, None),
        P(None, CTX, None),
        P(CTX),
        P(CTX),
        P(),
        P(CTX, None),
        P(CTX, None, None),
        P(),
        P(EXP, None, None),
        P(EXP, None, None),
        P(EXP, CTX, None),
        P(EXP, CTX, None),
    )
    out_specs = (P(EXP, CTX, None), P(EXP, CTX, None, None))
    return jax.shard_map(body, mesh=fine, in_specs=in_specs, out_specs=out_specs, check_vma=False)
```

```python
import functools

import jax
import jax.numpy as jnp
from jax import lax
from jax.experimental import pallas as pl
from jax.experimental.pallas import tpu as pltpu
from jax.sharding import Mesh
from jax.sharding import PartitionSpec as P

DK = 128
DV = 128
FFE = 512
HEADS = 2
ROUTES = 4
CHUNK = 128
EPSILON = 1e-06
CTX = ("y", "core")
EXP = ("x", "z")
bf16 = jnp.bfloat16
f32 = jnp.float32
highest = lax.Precision.HIGHEST
VMEM = pl.BlockSpec(memory_space=pltpu.VMEM)
SMEM = pl.BlockSpec(memory_space=pltpu.SMEM)
GRANT = 24 * 1024 * 1024


def mm(a, b):
    return jnp.dot(a.astype(bf16), b.astype(bf16), preferred_element_type=f32)


def mm_t(a, b):
    return lax.dot_general(
        a.astype(bf16), b.astype(bf16), (((1,), (1,)), ((), ())), preferred_element_type=f32
    )


def rms_scale(values, scaling):
    widened = values.astype(f32)
    return (
        widened * lax.rsqrt(jnp.mean(widened * widened, axis=-1, keepdims=True) + EPSILON) * scaling
    )


def unit_rows(values):
    return values * lax.rsqrt(jnp.sum(values * values, axis=-1, keepdims=True) + EPSILON)


def silu(values):
    return values / (1.0 + jnp.exp(-values))


def square_iota(size, axis):
    return lax.broadcasted_iota(jnp.int32, (size, size), axis)


def project_kernel(count, *refs):
    rows = jnp.concatenate([ref[...] for ref in refs[:count]], axis=0)
    weight_ref, rate_ref, made_ref, rates_ref = refs[count:]
    made_ref[...] = jnp.dot(rows, weight_ref[...], preferred_element_type=f32).astype(bf16)
    rates_ref[...] = jnp.dot(rows, rate_ref[...], preferred_element_type=f32).astype(bf16)


def run_project(blocks, weight, rate):
    rows = sum(block.shape[0] for block in blocks)
    return pl.pallas_call(
        functools.partial(project_kernel, len(blocks)),
        out_shape=(
            jax.ShapeDtypeStruct((rows, weight.shape[1]), bf16),
            jax.ShapeDtypeStruct((rows, rate.shape[1]), bf16),
        ),
        in_specs=[VMEM] * (len(blocks) + 2),
        out_specs=(VMEM, VMEM),
        compiler_params=pltpu.CompilerParams(vmem_limit_bytes=14 * 1024 * 1024),
        cost_estimate=pl.CostEstimate(
            flops=2 * rows * weight.size, bytes_accessed=8 * 10**6, transcendentals=0
        ),
        name="project",
    )(*blocks, weight, rate)


def delta_kernel(
    order_ref, early_ref, early_rate_ref, late_ref, late_rate_ref, halo_ref, weight_ref, conv_ref, rate_par_ref,
    gate_ref, reader_ref, local_ref, summary_ref, packed_ref,
    rows_scr, rate_scr,
):
    seg_rows = gate_ref.shape[0]
    width = conv_ref.shape[1]
    steps = seg_rows // CHUNK
    halo = jnp.dot(halo_ref[...], weight_ref[:, :width], preferred_element_type=f32)
    rows_scr[0:8, :] = halo.astype(bf16).astype(f32)
    for i in range(steps):
        made_ref, made_rate_ref = (
            (early_ref, early_rate_ref) if 2 * i < steps else (late_ref, late_rate_ref)
        )
        at = i % (steps // 2) * CHUNK
        to = pl.multiple_of(order_ref[i] * CHUNK, CHUNK)
        rows_scr[pl.ds(pl.multiple_of(to + 8, 8), CHUNK), :] = made_ref[at : at + CHUNK, :width].astype(f32)
        gate_ref[pl.ds(to, CHUNK), :] = made_ref[at : at + CHUNK, width:]
        rate_scr[pl.ds(to, CHUNK), :] = made_rate_ref[at : at + CHUNK, :].astype(f32)

    row = square_iota(CHUNK, 0)
    col = square_iota(CHUNK, 1)
    lower = (row >= col).astype(f32)
    eye = (row == col).astype(f32)
    for h in range(HEADS):
        summary_ref[h, :, :DK] = eye
        summary_ref[h, :, DK:] = jnp.zeros((DK, DV), f32)

    pair = 8

    def chunk_step(i, _):
        units = []
        for u in range(pair):
            at = pl.multiple_of((i * pair + u) * CHUNK, CHUNK)
            window = rows_scr[pl.ds(at, CHUNK + 8), :]
            summed = conv_ref[0:1, :] * window[5 : 5 + CHUNK]
            for tap in range(1, 4):
                summed = summed + conv_ref[tap : tap + 1, :] * window[5 + tap : 5 + tap + CHUNK]
            active = silu(summed)
            query = unit_rows(active[:, :DK]) * DK ** (-0.5)
            key = unit_rows(active[:, DK : 2 * DK])
            rate = rate_scr[pl.ds(at, CHUNK), :]
            shifted = rate + rate_par_ref[0:1, :]
            soft = jnp.maximum(shifted, 0.0) + jnp.log1p(jnp.exp(-jnp.abs(shifted)))
            decay = -rate_par_ref[1:2, :] * soft
            beta_all = 1.0 / (1.0 + jnp.exp(-rate))
            total = jnp.dot(lower, decay, preferred_element_type=f32, precision=highest)
            total_t = total.T
            key_low = key.astype(bf16)
            gram = mm_t(key_low, key_low)
            raw_scores = mm_t(query, key_low)
            for h in range(HEADS):
                cum = total[:, HEADS + h : HEADS + h + 1]
                cum_row = total_t[HEADS + h : HEADS + h + 1, :]
                beta = beta_all[:, h : h + 1]
                causal = jnp.exp(jnp.where(row >= col, cum - cum_row, -1e30))
                grown = jnp.exp(cum)
                last = cum[CHUNK - 1 : CHUNK, :]
                value = active[:, 2 * DK + h * DV : 2 * DK + (h + 1) * DV]
                units.append(
                    dict(
                        at=at,
                        h=h,
                        low=jnp.where(row > col, beta * gram * causal, 0.0),
                        right=jnp.concatenate([beta * key * grown, beta * value], axis=1).astype(bf16),
                        scores=(raw_scores * causal).astype(bf16),
                        read=(query * grown).astype(bf16),
                        faded=(key * jnp.exp(last - cum)).T.astype(bf16),
                        fade=jnp.exp(last),
                    )
                )
        inverses = [
            eye - jnp.where((row // 2 == col // 2), unit["low"], 0.0) for unit in units
        ]
        size = 2
        while size < CHUNK:
            off = (row // (2 * size) == col // (2 * size)) & (row // size != col // size)
            lows = [x.astype(bf16) for x in inverses]
            firsts = [mm(jnp.where(off, unit["low"], 0.0), x) for unit, x in zip(units, lows)]
            inverses = [x - mm(x_low, y) for x, x_low, y in zip(inverses, lows, firsts)]
            size *= 2
        solved = [mm(x, unit["right"]) for unit, x in zip(units, inverses)]
        for unit, done in zip(units, solved):
            h = unit["h"]
            state = summary_ref[h]
            stacked = jnp.concatenate([done[:, :DK].astype(bf16), unit["read"]], axis=0)
            applied = mm(stacked, state)
            fresh = jnp.concatenate([-applied[:CHUNK, :DK], done[:, DK:] - applied[:CHUNK, DK:]], axis=1)
            fresh = fresh.astype(bf16)
            out = applied[CHUNK:] + mm(unit["scores"], fresh)
            summary_ref[h] = unit["fade"] * state + mm(unit["faded"], fresh)
            reader_ref[h, pl.ds(unit["at"], CHUNK), :] = out[:, :DK].astype(bf16)
            local_ref[h, pl.ds(unit["at"], CHUNK), :] = out[:, DK:]
        return 0

    lax.fori_loop(0, steps // pair, chunk_step, 0)
    for h in range(HEADS):
        change = summary_ref[h, :, :DK] - eye
        summary_ref[h, :, :DK] = change
        packed_ref[h, :, :DK] = change.astype(bf16)
        packed_ref[h, :, DK:] = summary_ref[h, :, DK:].astype(bf16)


def run_delta(order, early, early_rate, late, late_rate, halo, weight, conv, rate_par):
    rows = 2 * early.shape[0]
    return pl.pallas_call(
        delta_kernel,
        out_shape=(
            jax.ShapeDtypeStruct((rows, HEADS * DV), bf16),
            jax.ShapeDtypeStruct((HEADS, rows, DK), bf16),
            jax.ShapeDtypeStruct((HEADS, rows, DV), f32),
            jax.ShapeDtypeStruct((HEADS, DK, DK + DV), f32),
            jax.ShapeDtypeStruct((HEADS, DK, DK + DV), bf16),
        ),
        in_specs=[SMEM] + [VMEM] * 8,
        out_specs=(VMEM,) * 5,
        scratch_shapes=[
            pltpu.VMEM((rows + 8, conv.shape[1]), f32),
            pltpu.VMEM((rows, 128), f32),
        ],
        compiler_params=pltpu.CompilerParams(vmem_limit_bytes=GRANT),
        name="delta",
    )(order, early, early_rate, late, late_rate, halo, weight, conv, rate_par)


def then(first, second):
    return first + mm(second[:, :DK], first) + second.astype(f32)


def apply(change, state):
    return state + mm(change[:, :DK], state) + change[:, DK:].astype(f32)


def couple_kernel(place_ref, own_ref, other_ref, both_ref):
    odd = place_ref[0] % 2 == 1
    for h in range(HEADS):
        own = own_ref[h].astype(f32)
        other = other_ref[h].astype(f32)
        both_ref[h] = then(jnp.where(odd, other, own), jnp.where(odd, own, other)).astype(bf16)


def run_couple(place, own, other):
    return pl.pallas_call(
        couple_kernel,
        out_shape=jax.ShapeDtypeStruct(own.shape, bf16),
        in_specs=[SMEM, VMEM, VMEM],
        out_specs=VMEM,
        compiler_params=pltpu.CompilerParams(vmem_limit_bytes=8 * 1024 * 1024),
        name="couple",
    )(place, own, other)


def row_kernel(place_ref, own_ref, back1_ref, back2_ref, back3_ref, other_ref, prefix_ref, total_ref, all_scr):
    odd = place_ref[0] % 2 == 1
    place = place_ref[0] // 2
    for offset, ref in enumerate((own_ref, back1_ref, back2_ref, back3_ref)):
        all_scr[(place + 4 - offset) % 4] = ref[...]
    changes = [jnp.zeros((DK, DK + DV), f32) for _ in range(HEADS)]
    for j in range(4):
        for h in range(HEADS):
            change = changes[h]

            @pl.when(place == j)
            def _(change=change, h=h):
                prefix_ref[h] = change

            changes[h] = then(change, all_scr[j, h])
    for h in range(HEADS):
        total_ref[h] = changes[h].astype(bf16)
        before = prefix_ref[h]
        prefix_ref[h] = jnp.where(odd, then(before, other_ref[h]), before)


def run_row(place, own, back1, back2, back3, other):
    return pl.pallas_call(
        row_kernel,
        out_shape=(
            jax.ShapeDtypeStruct(own.shape, f32),
            jax.ShapeDtypeStruct(own.shape, bf16),
        ),
        in_specs=[SMEM] + [VMEM] * 5,
        out_specs=(VMEM, VMEM),
        scratch_shapes=[pltpu.VMEM((4,) + own.shape, bf16)],
        compiler_params=pltpu.CompilerParams(vmem_limit_bytes=8 * 1024 * 1024),
        name="row",
    )(place, own, back1, back2, back3, other)


def mix(order_ref, entering, reader_ref, local_ref, gate_ref, gain_ref, weight_ref, out_ref):
    for i in range(out_ref.shape[0] // CHUNK):
        at = pl.ds(pl.multiple_of(order_ref[i] * CHUNK, CHUNK), CHUNK)
        parts = []
        for h in range(HEADS):
            mixed = mm(reader_ref[h, at, :], entering[h]) + local_ref[h, at, :]
            gate = gate_ref[at, h * DV : (h + 1) * DV].astype(f32)
            parts.append((rms_scale(mixed, gain_ref[...]) * silu(gate)).astype(bf16))
        gated = jnp.concatenate(parts, axis=1)
        at = slice(i * CHUNK, (i + 1) * CHUNK)
        out_ref[at, :] = jnp.dot(gated, weight_ref[...], preferred_element_type=f32).astype(bf16)


def give_kernel(
    place_ref, order_ref, back1_ref, back2_ref, back3_ref, start_ref, prefix_ref, summary_ref, reader_ref, local_ref,
    gate_ref, gain_ref, weight_ref, out_ref, final_ref, entering_ref,
):
    place = place_ref[0]
    entering = []
    for h in range(HEADS):
        state = start_ref[h]
        for offset, ref in ((3, back3_ref), (2, back2_ref), (1, back1_ref)):
            state = jnp.where(place >= offset, apply(ref[h], state), state)
        state = apply(prefix_ref[h], state)
        final_ref[h] = apply(summary_ref[h], state)
        entering.append(state.astype(bf16))
        entering_ref[h] = entering[h]
    mix(order_ref, entering, reader_ref, local_ref, gate_ref, gain_ref, weight_ref, out_ref)


def run_give(place, order, backs, start, prefix, summary, reader, local, gate, gain, weight):
    return pl.pallas_call(
        give_kernel,
        out_shape=(
            jax.ShapeDtypeStruct((gate.shape[0] // 2, weight.shape[1]), bf16),
            jax.ShapeDtypeStruct(start.shape, f32),
            jax.ShapeDtypeStruct(start.shape, bf16),
        ),
        in_specs=[SMEM] * 2 + [VMEM] * 11,
        out_specs=(VMEM,) * 3,
        compiler_params=pltpu.CompilerParams(vmem_limit_bytes=GRANT),
        name="give",
    )(place, order, *backs, start, prefix, summary, reader, local, gate, gain, weight)


def keep_kernel(order_ref, entering_ref, reader_ref, local_ref, gate_ref, gain_ref, weight_ref, out_ref):
    entering = [entering_ref[h] for h in range(HEADS)]
    mix(order_ref, entering, reader_ref, local_ref, gate_ref, gain_ref, weight_ref, out_ref)


def run_keep(order, entering, reader, local, gate, gain, weight):
    rows = gate.shape[0] // 2
    return pl.pallas_call(
        keep_kernel,
        out_shape=jax.ShapeDtypeStruct((rows, weight.shape[1]), bf16),
        in_specs=[SMEM] + [VMEM] * 6,
        out_specs=VMEM,
        compiler_params=pltpu.CompilerParams(vmem_limit_bytes=GRANT),
        cost_estimate=pl.CostEstimate(
            flops=2 * rows * weight.size, bytes_accessed=4 * 10**6, transcendentals=0
        ),
        name="keep",
    )(order, entering, reader, local, gate, gain, weight)


def split_kernel(kept_ref, got_ref, near_ref, up_ref, down_ref, far_up_ref, far_down_ref):
    rows = near_ref.shape[0]

    def summed(at, size):
        return kept_ref[at : at + size, :].astype(f32) + got_ref[at : at + size, :].astype(f32)

    half = rows // 2
    far_up_ref[...] = summed(2 * rows, half).astype(bf16)
    far_down_ref[...] = summed(2 * rows + half, half).astype(bf16)
    near_ref[...] = summed(0, rows)
    up_ref[...] = summed(rows, rows)
    down_ref[...] = summed(3 * rows, rows)


def run_split(kept, got):
    rows = kept.shape[0] // 4
    width = kept.shape[1]
    return pl.pallas_call(
        split_kernel,
        out_shape=(jax.ShapeDtypeStruct((rows, width), f32),) * 3
        + (jax.ShapeDtypeStruct((rows // 2, width), bf16),) * 2,
        in_specs=[VMEM] * 2,
        out_specs=(VMEM,) * 5,
        compiler_params=pltpu.CompilerParams(vmem_limit_bytes=12 * 1024 * 1024),
        name="split",
    )(kept, got)


def pass_kernel(up_ref, down_ref, from_below_ref, from_above_ref, send_up_ref, send_down_ref):
    half = from_below_ref.shape[0]
    send_up_ref[:half, :] = (up_ref[:half, :] + from_below_ref[...].astype(f32)).astype(bf16)
    send_up_ref[half:, :] = up_ref[half:, :].astype(bf16)
    send_down_ref[:half, :] = down_ref[:half, :].astype(bf16)
    send_down_ref[half:, :] = (down_ref[half:, :] + from_above_ref[...].astype(f32)).astype(bf16)


def run_pass(up, down, from_below, from_above):
    return pl.pallas_call(
        pass_kernel,
        out_shape=(jax.ShapeDtypeStruct(up.shape, bf16),) * 2,
        in_specs=[VMEM] * 4,
        out_specs=(VMEM,) * 2,
        compiler_params=pltpu.CompilerParams(vmem_limit_bytes=12 * 1024 * 1024),
        name="pass",
    )(up, down, from_below, from_above)


def dispatch_kernel(own_ref, near_ref, below_ref, above_ref, gain_ref, pick_ref, hidden_ref, out_ref):
    mixed = near_ref[...] + (below_ref[...].astype(f32) + above_ref[...].astype(f32))
    hidden = own_ref[...].astype(f32) + mixed
    hidden_ref[...] = hidden
    post = rms_scale(hidden, gain_ref[...]).astype(bf16)
    half = post.shape[1] // 2
    stacked = jnp.concatenate([post[:, :half], post[:, half:]], axis=0)
    out_ref[...] = jnp.dot(pick_ref[...], stacked, preferred_element_type=f32).astype(bf16)


def run_dispatch(own, near, below, above, gain, pick):
    return pl.pallas_call(
        dispatch_kernel,
        out_shape=(
            jax.ShapeDtypeStruct(own.shape, f32),
            jax.ShapeDtypeStruct((pick.shape[0], own.shape[1] // 2), bf16),
        ),
        in_specs=[VMEM] * 6,
        out_specs=(VMEM, VMEM),
        compiler_params=pltpu.CompilerParams(vmem_limit_bytes=GRANT),
        name="dispatch",
    )(own, near, below, above, gain, pick)


def expert_kernel(rows_ref, up_ref, down_ref, out_ref):
    count, _, half = rows_ref.shape

    def hidden_of(gate_up):
        return (silu(gate_up[:, :FFE]) * gate_up[:, FFE:]).astype(bf16)

    group = 32

    def step(i, _):
        some = pl.ds(i * group, group)
        left = rows_ref[some, 0:16, :].reshape(group * 16, half)
        right = rows_ref[some, 16:32, :].reshape(group * 16, half)
        gate_up = jnp.dot(left, up_ref[:half, :], preferred_element_type=f32) + jnp.dot(
            right, up_ref[half:, :], preferred_element_type=f32
        )
        done = jnp.dot(hidden_of(gate_up), down_ref[...], preferred_element_type=f32).astype(bf16)
        out_ref[some, 0:16, :] = done[:, :half].reshape(group, 16, half)
        out_ref[some, 16:32, :] = done[:, half:].reshape(group, 16, half)
        return 0

    lax.fori_loop(0, count // group, step, 0)
    tail = rows_ref[:, 32:40, :].reshape(count * 8, half)
    first = jnp.dot(tail, up_ref[:half, :], preferred_element_type=f32)
    second = jnp.dot(tail, up_ref[half:, :], preferred_element_type=f32)
    turned = count * 8 - 4
    gate_up = first + pltpu.roll(second, turned, 0)
    done = jnp.dot(hidden_of(gate_up), down_ref[...], preferred_element_type=f32)
    upper = lax.broadcasted_iota(jnp.int32, (count * 8, half), 0) % 8 < 4
    packed = jnp.where(upper, done[:, :half], pltpu.roll(done[:, half:], 4, 0)).astype(bf16)
    out_ref[:, 32:40, :] = packed.reshape(count, 8, half)


def run_expert(rows, up, down):
    return pl.pallas_call(
        expert_kernel,
        out_shape=jax.ShapeDtypeStruct(rows.shape, bf16),
        in_specs=[VMEM] * 3,
        out_specs=VMEM,
        compiler_params=pltpu.CompilerParams(vmem_limit_bytes=GRANT),
        name="expert",
    )(rows, up, down)


def combine_kernel(hidden_ref, back_ref, high_ref, low_ref, out_ref):
    rows = hidden_ref.shape[0]
    half = back_ref.shape[1]
    back = back_ref[...]
    routed = jnp.dot(high_ref[...], back, preferred_element_type=f32) + jnp.dot(
        low_ref[...], back, preferred_element_type=f32
    )
    out_ref[:, :half] = hidden_ref[:, :half] + routed[:rows]
    out_ref[:, half:] = hidden_ref[:, half:] + routed[rows:]


def run_combine(hidden, back, high, low):
    return pl.pallas_call(
        combine_kernel,
        out_shape=jax.ShapeDtypeStruct(hidden.shape, f32),
        in_specs=[VMEM] * 4,
        out_specs=VMEM,
        compiler_params=pltpu.CompilerParams(vmem_limit_bytes=GRANT),
        name="combine",
    )(hidden, back, high, low)


def turned(size, distance):
    return [(i, (i + distance) % size) for i in range(size)]


def slot_rows(ids, experts):
    rows = ids.shape[0]
    choice = ids[:, :, None] == jnp.arange(experts, dtype=jnp.int32)
    named = jnp.any(choice, axis=1).astype(bf16)
    before = jnp.tril(jnp.ones((rows, rows), bf16), -1)
    ranks = jnp.dot(before, named, preferred_element_type=f32)
    slots = jnp.sum(jnp.where(choice, ranks[:, None, :], 0.0), axis=2).astype(jnp.int32)
    early = slots < 16
    left = ids * 40 + jnp.where(early, slots, slots + 16)
    right = ids * 40 + jnp.where(early, slots + 16, slots + 20)
    return jnp.concatenate([left, right], axis=0)


def body(
    tokens,
    input_gain,
    mixer_weight,
    rate_weight,
    conv_kernel,
    decay_scale,
    decay_bias,
    value_gain,
    output_weight,
    start_state,
    post_gain,
    expert_gateup,
    expert_down,
    route_ids,
    route_weights,
):
    own = tokens[0]
    model_width = own.shape[1]
    experts = lax.axis_size(EXP)
    normed = rms_scale(own, input_gain).astype(bf16)
    rings = lax.axis_size("y")
    y, core = lax.axis_index("y"), lax.axis_index("core")
    tok_rows = own.shape[0]
    half = tok_rows // 2
    up, down, swap = turned(rings, 1), turned(rings, -1), [(0, 1), (1, 0)]
    below = lax.ppermute(normed, "y", up)
    above = lax.ppermute(normed, "y", down)
    beside = lax.ppermute(normed, "core", swap)
    rate = jnp.concatenate(
        [rate_weight.reshape(model_width, -1), jnp.zeros((model_width, 128 - 2 * HEADS), bf16)], axis=1
    )
    below, above, beside, rate = lax.optimization_barrier((below, above, beside, rate))
    far_low = lax.ppermute(below[:half], "y", up)
    far_high = lax.ppermute(above[half:], "y", down)
    flanks = lax.ppermute(jnp.concatenate([below, above], axis=0), "core", swap)
    early, early_rate = run_project([normed, beside, below, above], mixer_weight, rate)
    far_low, far_high, flanks, early = lax.optimization_barrier((far_low, far_high, flanks, early))
    far = lax.ppermute(jnp.concatenate([far_low, far_high], axis=0), "core", swap)
    late, late_rate = run_project([flanks, far_low, far_high, far], mixer_weight, rate)
    order = jnp.stack(
        [(y + step) % rings * 2 + (core + side) % 2 for step, side in
         ((0, 0), (0, 1), (3, 0), (1, 0), (3, 1), (1, 1), (2, 0), (2, 1))]
    ).astype(jnp.int32)
    ends = [
        normed[-8:], beside[-8:], below[-8:], above[-8:],
        flanks[tok_rows - 8 : tok_rows], flanks[-8:], far_high[-8:], far[-8:],
    ]
    closing = ends[0]
    for i in range(1, len(ends)):
        closing = jnp.where(order[i] == len(ends) - 1, ends[i], closing)
    halo = lax.ppermute(closing, EXP, [(i, i + 1) for i in range(experts - 1)])
    room = 128 - 2 * HEADS
    rate_par = jnp.stack(
        [
            jnp.concatenate([jnp.zeros(HEADS, f32), decay_bias, jnp.zeros(room, f32)]),
            jnp.concatenate([jnp.zeros(HEADS, f32), decay_scale, jnp.zeros(room, f32)]),
        ]
    )
    gate, reader, local, summary, packed = run_delta(
        order, early, early_rate, late, late_rate, halo, mixer_weight, conv_kernel[:, 0], rate_par
    )
    depth = lax.axis_size("z")
    along_z = lax.axis_index("z").reshape(1)
    other = lax.ppermute(packed, "z", [(i, i ^ 1) for i in range(depth)])
    both = run_couple(along_z, packed, other)
    pairs = [lax.ppermute(both, "z", turned(depth, 2 * step)) for step in (1, 2, 3)]
    prefix, total = run_row(along_z, both, *pairs, other)
    rows = [lax.ppermute(total, "x", turned(lax.axis_size("x"), step)) for step in (1, 2, 3)]
    kept_order = jnp.stack([(y + step) % rings * 2 + core for step in range(rings)]).astype(jnp.int32)
    given_order = jnp.stack([(y + step) % rings * 2 + 1 - core for step in range(rings)]).astype(jnp.int32)
    gain = value_gain.reshape(1, -1)
    given, final_state, entering = run_give(
        lax.axis_index("x").reshape(1), given_order, rows, start_state, prefix, summary, reader, local, gate,
        gain, output_weight,
    )
    got = lax.ppermute(given, "core", swap)
    kept = run_keep(kept_order, entering, reader, local, gate, gain, output_weight)
    near, to_up, to_down, far_up, far_down = run_split(kept, got)
    from_below = lax.ppermute(far_up, "y", up)
    from_above = lax.ppermute(far_down, "y", down)
    send_up, send_down = run_pass(to_up, to_down, from_below, from_above)
    mixed_below = lax.ppermute(send_up, "y", up)
    mixed_above = lax.ppermute(send_down, "y", down)

    places = slot_rows(route_ids[0], experts)
    count = experts * 40
    hits = places[:, :, None] == jnp.arange(count, dtype=jnp.int32)
    pick = jnp.any(
        places.T[:, None, :] == jnp.arange(count, dtype=jnp.int32)[None, :, None], axis=0
    ).astype(bf16)
    doubled = jnp.concatenate([route_weights[0], route_weights[0]], axis=0)
    share = jnp.sum(jnp.where(hits, doubled[:, :, None], 0.0), axis=1)
    high = share.astype(bf16)
    low = (share - high.astype(f32)).astype(bf16)

    hidden, outgoing = run_dispatch(
        own, near, mixed_below, mixed_above, post_gain.reshape(1, -1), pick
    )
    width = model_width // 2
    arrived = lax.all_to_all(outgoing.reshape(experts, 40, width), EXP, 0, 0, tiled=True)
    made = run_expert(arrived, expert_gateup[0], expert_down[0])
    back = lax.all_to_all(made, EXP, 0, 0, tiled=True)
    layer_out = run_combine(hidden, back.reshape(count, width), high, low)
    return (layer_out[None], final_state[None])


def solution(mesh):
    fine = Mesh(mesh.devices.reshape(4, 2, 4, 8), CTX + EXP)
    in_specs = (
        P(EXP, CTX, None),
        P(),
        P(None, CTX),
        P(None, CTX, None),
        P(None, CTX, None),
        P(CTX),
        P(CTX),
        P(),
        P(CTX, None),
        P(CTX, None, None),
        P(),
        P(EXP, None, None),
        P(EXP, None, None),
        P(EXP, CTX, None),
        P(EXP, CTX, None),
    )
    out_specs = (P(EXP, CTX, None), P(EXP, CTX, None, None))
    return jax.shard_map(body, mesh=fine, in_specs=in_specs, out_specs=out_specs, check_vma=False)
```

```python
import functools

import jax
import jax.numpy as jnp
from jax import lax
from jax.experimental import pallas as pl
from jax.experimental.pallas import tpu as pltpu
from jax.sharding import Mesh
from jax.sharding import PartitionSpec as P

DK = 128
DV = 128
FFE = 512
HEADS = 2
ROUTES = 4
CHUNK = 128
EPSILON = 1e-06
CTX = ("y", "core")
EXP = ("x", "z")
bf16 = jnp.bfloat16
f32 = jnp.float32
highest = lax.Precision.HIGHEST
VMEM = pl.BlockSpec(memory_space=pltpu.VMEM)
SMEM = pl.BlockSpec(memory_space=pltpu.SMEM)
GRANT = 24 * 1024 * 1024


def mm(a, b):
    return jnp.dot(a.astype(bf16), b.astype(bf16), preferred_element_type=f32)


def mm_t(a, b):
    return lax.dot_general(
        a.astype(bf16), b.astype(bf16), (((1,), (1,)), ((), ())), preferred_element_type=f32
    )


def rms_scale(values, scaling):
    widened = values.astype(f32)
    return (
        widened * lax.rsqrt(jnp.mean(widened * widened, axis=-1, keepdims=True) + EPSILON) * scaling
    )


def unit_rows(values):
    return values * lax.rsqrt(jnp.sum(values * values, axis=-1, keepdims=True) + EPSILON)


def silu(values):
    return values / (1.0 + jnp.exp(-values))


def square_iota(size, axis):
    return lax.broadcasted_iota(jnp.int32, (size, size), axis)


def norm_kernel(own_ref, gain_ref, out_ref):
    out_ref[...] = rms_scale(own_ref[...], gain_ref[...]).astype(bf16)


def run_norm(own, gain):
    return pl.pallas_call(
        norm_kernel,
        out_shape=jax.ShapeDtypeStruct(own.shape, bf16),
        in_specs=[VMEM] * 2,
        out_specs=VMEM,
        compiler_params=pltpu.CompilerParams(vmem_limit_bytes=8 * 1024 * 1024),
        name="norm",
    )(own, gain)


ORDER = ((0, 0), (0, 1), (3, 0), (1, 0), (3, 1), (1, 1), (2, 0), (2, 1))
CLOSING = (112, 112, 112, 112, 112, 240, 48, 112)


def block_of(y, core, i):
    step, side = ORDER[i]
    return (y + step) % 4 * 2 + (core + side) % 2


ANY = pl.BlockSpec(memory_space=pl.ANY)


def cut_kernel(below_ref, above_ref, low_ref, high_ref, both_ref, sems):
    rows = below_ref.shape[0]
    half = rows // 2
    copies = [
        pltpu.make_async_copy(below_ref.at[pl.ds(0, half)], low_ref, sems.at[0]),
        pltpu.make_async_copy(above_ref.at[pl.ds(half, half)], high_ref, sems.at[1]),
        pltpu.make_async_copy(below_ref, both_ref.at[pl.ds(0, rows)], sems.at[2]),
        pltpu.make_async_copy(above_ref, both_ref.at[pl.ds(rows, rows)], sems.at[3]),
    ]
    for copy in copies:
        copy.start()
    for copy in copies:
        copy.wait()


def run_cut(below, above):
    rows, width = below.shape
    return pl.pallas_call(
        cut_kernel,
        out_shape=(
            jax.ShapeDtypeStruct((rows // 2, width), bf16),
            jax.ShapeDtypeStruct((rows // 2, width), bf16),
            jax.ShapeDtypeStruct((2 * rows, width), bf16),
        ),
        in_specs=[ANY] * 2,
        out_specs=(ANY,) * 3,
        scratch_shapes=[pltpu.SemaphoreType.DMA((4,))],
        compiler_params=pltpu.CompilerParams(vmem_limit_bytes=4 * 1024 * 1024),
        name="cut",
    )(below, above)


def join_kernel(first_ref, second_ref, both_ref, sems):
    rows = first_ref.shape[0]
    copies = [
        pltpu.make_async_copy(first_ref, both_ref.at[pl.ds(0, rows)], sems.at[0]),
        pltpu.make_async_copy(second_ref, both_ref.at[pl.ds(rows, rows)], sems.at[1]),
    ]
    for copy in copies:
        copy.start()
    for copy in copies:
        copy.wait()


def run_join(first, second):
    rows, width = first.shape
    return pl.pallas_call(
        join_kernel,
        out_shape=jax.ShapeDtypeStruct((2 * rows, width), bf16),
        in_specs=[ANY] * 2,
        out_specs=ANY,
        scratch_shapes=[pltpu.SemaphoreType.DMA((2,))],
        compiler_params=pltpu.CompilerParams(vmem_limit_bytes=4 * 1024 * 1024),
        name="join",
    )(first, second)


def closing_kernel(place_ref, *refs):
    ends, out_ref, sem = refs[:-2], refs[-2], refs[-1]
    for i, (ref, at) in enumerate(zip(ends, CLOSING)):

        @pl.when(block_of(place_ref[1], place_ref[3], i) == len(ORDER) - 1)
        def _(ref=ref, at=at):
            copy = pltpu.make_async_copy(ref.at[pl.ds(at, 16)], out_ref, sem)
            copy.start()
            copy.wait()


def run_closing(place, ends):
    return pl.pallas_call(
        closing_kernel,
        out_shape=jax.ShapeDtypeStruct((16, ends[0].shape[1]), bf16),
        in_specs=[SMEM] + [ANY] * len(ends),
        out_specs=ANY,
        scratch_shapes=[pltpu.SemaphoreType.DMA],
        compiler_params=pltpu.CompilerParams(vmem_limit_bytes=4 * 1024 * 1024),
        name="closing",
    )(place, *ends)


def project_kernel(count, *refs):
    weight_ref, rate_ref, made_ref, rates_ref, rows_scr, sems = refs[count:]
    copies, at = [], 0
    for i, ref in enumerate(refs[:count]):
        copies.append(pltpu.make_async_copy(ref, rows_scr.at[pl.ds(at, ref.shape[0])], sems.at[i]))
        copies[i].start()
        at += ref.shape[0]
    for copy in copies:
        copy.wait()
    rows = rows_scr[...]
    made_ref[...] = jnp.dot(rows, weight_ref[...], preferred_element_type=f32).astype(bf16)
    rates_ref[...] = jnp.dot(rows, rate_ref[...], preferred_element_type=f32).astype(bf16)


def run_project(blocks, weight, rate):
    rows = sum(block.shape[0] for block in blocks)
    return pl.pallas_call(
        functools.partial(project_kernel, len(blocks)),
        out_shape=(
            jax.ShapeDtypeStruct((rows, weight.shape[1]), bf16),
            jax.ShapeDtypeStruct((rows, rate.shape[1]), bf16),
        ),
        in_specs=[ANY] * len(blocks) + [VMEM] * 2,
        out_specs=(VMEM, VMEM),
        scratch_shapes=[
            pltpu.VMEM((rows, weight.shape[0]), bf16),
            pltpu.SemaphoreType.DMA((len(blocks),)),
        ],
        compiler_params=pltpu.CompilerParams(vmem_limit_bytes=14 * 1024 * 1024),
        cost_estimate=pl.CostEstimate(
            flops=2 * rows * weight.size, bytes_accessed=8 * 10**6, transcendentals=0
        ),
        name="project",
    )(*blocks, weight, rate)


def delta_kernel(
    place_ref, early_ref, early_rate_ref, late_ref, late_rate_ref, halo_ref, weight_ref, conv_ref, rate_par_ref,
    gate_ref, reader_ref, local_ref, summary_ref, packed_ref,
    rows_scr, rate_scr,
):
    seg_rows = gate_ref.shape[0]
    width = conv_ref.shape[1]
    steps = seg_rows // CHUNK
    halo = jnp.dot(halo_ref[...], weight_ref[:, :width], preferred_element_type=f32)
    rows_scr[0:8, :] = halo[8:16].astype(bf16).astype(f32)
    for i in range(steps):
        made_ref, made_rate_ref = (
            (early_ref, early_rate_ref) if 2 * i < steps else (late_ref, late_rate_ref)
        )
        at = i % (steps // 2) * CHUNK
        to = pl.multiple_of(block_of(place_ref[1], place_ref[3], i) * CHUNK, CHUNK)
        rows_scr[pl.ds(pl.multiple_of(to + 8, 8), CHUNK), :] = made_ref[at : at + CHUNK, :width].astype(f32)
        gate_ref[pl.ds(to, CHUNK), :] = made_ref[at : at + CHUNK, width:]
        rate_scr[pl.ds(to, CHUNK), :] = made_rate_ref[at : at + CHUNK, :].astype(f32)

    row = square_iota(CHUNK, 0)
    col = square_iota(CHUNK, 1)
    lower = (row >= col).astype(f32)
    eye = (row == col).astype(f32)
    for h in range(HEADS):
        summary_ref[h, :, :DK] = eye
        summary_ref[h, :, DK:] = jnp.zeros((DK, DV), f32)

    pair = 8

    def chunk_step(i, _):
        units = []
        for u in range(pair):
            at = pl.multiple_of((i * pair + u) * CHUNK, CHUNK)
            window = rows_scr[pl.ds(at, CHUNK + 8), :]
            summed = conv_ref[0:1, :] * window[5 : 5 + CHUNK]
            for tap in range(1, 4):
                summed = summed + conv_ref[tap : tap + 1, :] * window[5 + tap : 5 + tap + CHUNK]
            active = silu(summed)
            query = unit_rows(active[:, :DK]) * DK ** (-0.5)
            key = unit_rows(active[:, DK : 2 * DK])
            rate = rate_scr[pl.ds(at, CHUNK), :]
            shifted = rate + rate_par_ref[0:1, :]
            soft = jnp.maximum(shifted, 0.0) + jnp.log1p(jnp.exp(-jnp.abs(shifted)))
            decay = -rate_par_ref[1:2, :] * soft
            beta_all = 1.0 / (1.0 + jnp.exp(-rate))
            total = jnp.dot(lower, decay, preferred_element_type=f32, precision=highest)
            total_t = total.T
            key_low = key.astype(bf16)
            gram = mm_t(key_low, key_low)
            raw_scores = mm_t(query, key_low)
            for h in range(HEADS):
                cum = total[:, HEADS + h : HEADS + h + 1]
                cum_row = total_t[HEADS + h : HEADS + h + 1, :]
                beta = beta_all[:, h : h + 1]
                causal = jnp.exp(jnp.where(row >= col, cum - cum_row, -1e30))
                grown = jnp.exp(cum)
                last = cum[CHUNK - 1 : CHUNK, :]
                value = active[:, 2 * DK + h * DV : 2 * DK + (h + 1) * DV]
                units.append(
                    dict(
                        at=at,
                        h=h,
                        low=jnp.where(row > col, beta * gram * causal, 0.0),
                        right=jnp.concatenate([beta * key * grown, beta * value], axis=1).astype(bf16),
                        scores=(raw_scores * causal).astype(bf16),
                        read=(query * grown).astype(bf16),
                        faded=(key * jnp.exp(last - cum)).T.astype(bf16),
                        fade=jnp.exp(last),
                    )
                )
        inverses = [
            eye - jnp.where((row // 2 == col // 2), unit["low"], 0.0) for unit in units
        ]
        size = 2
        while size < CHUNK:
            off = (row // (2 * size) == col // (2 * size)) & (row // size != col // size)
            lows = [x.astype(bf16) for x in inverses]
            firsts = [mm(jnp.where(off, unit["low"], 0.0), x) for unit, x in zip(units, lows)]
            inverses = [x - mm(x_low, y) for x, x_low, y in zip(inverses, lows, firsts)]
            size *= 2
        solved = [mm(x, unit["right"]) for unit, x in zip(units, inverses)]
        for unit, done in zip(units, solved):
            h = unit["h"]
            state = summary_ref[h]
            stacked = jnp.concatenate([done[:, :DK].astype(bf16), unit["read"]], axis=0)
            applied = mm(stacked, state)
            fresh = jnp.concatenate([-applied[:CHUNK, :DK], done[:, DK:] - applied[:CHUNK, DK:]], axis=1)
            fresh = fresh.astype(bf16)
            out = applied[CHUNK:] + mm(unit["scores"], fresh)
            summary_ref[h] = unit["fade"] * state + mm(unit["faded"], fresh)
            reader_ref[h, pl.ds(unit["at"], CHUNK), :] = out[:, :DK].astype(bf16)
            local_ref[h, pl.ds(unit["at"], CHUNK), :] = out[:, DK:]
        return 0

    lax.fori_loop(0, steps // pair, chunk_step, 0)
    for h in range(HEADS):
        change = summary_ref[h, :, :DK] - eye
        summary_ref[h, :, :DK] = change
        packed_ref[h, :, :DK] = change.astype(bf16)
        packed_ref[h, :, DK:] = summary_ref[h, :, DK:].astype(bf16)


def run_delta(place, early, early_rate, late, late_rate, halo, weight, conv, rate_par):
    rows = 2 * early.shape[0]
    return pl.pallas_call(
        delta_kernel,
        out_shape=(
            jax.ShapeDtypeStruct((rows, HEADS * DV), bf16),
            jax.ShapeDtypeStruct((HEADS, rows, DK), bf16),
            jax.ShapeDtypeStruct((HEADS, rows, DV), f32),
            jax.ShapeDtypeStruct((HEADS, DK, DK + DV), f32),
            jax.ShapeDtypeStruct((HEADS, DK, DK + DV), bf16),
        ),
        in_specs=[SMEM] + [VMEM] * 8,
        out_specs=(VMEM,) * 5,
        scratch_shapes=[
            pltpu.VMEM((rows + 8, conv.shape[1]), f32),
            pltpu.VMEM((rows, 128), f32),
        ],
        compiler_params=pltpu.CompilerParams(vmem_limit_bytes=GRANT),
        name="delta",
    )(place, early, early_rate, late, late_rate, halo, weight, conv, rate_par)


def then(first, second):
    return first + mm(second[:, :DK], first) + second.astype(f32)


def apply(change, state):
    return state + mm(change[:, :DK], state) + change[:, DK:].astype(f32)


def couple_kernel(place_ref, own_ref, other_ref, both_ref):
    odd = place_ref[2] % 2 == 1
    for h in range(HEADS):
        own = own_ref[h].astype(f32)
        other = other_ref[h].astype(f32)
        both_ref[h] = then(jnp.where(odd, other, own), jnp.where(odd, own, other)).astype(bf16)


def run_couple(place, own, other):
    return pl.pallas_call(
        couple_kernel,
        out_shape=jax.ShapeDtypeStruct(own.shape, bf16),
        in_specs=[SMEM, VMEM, VMEM],
        out_specs=VMEM,
        compiler_params=pltpu.CompilerParams(vmem_limit_bytes=8 * 1024 * 1024),
        name="couple",
    )(place, own, other)


def row_kernel(place_ref, own_ref, back1_ref, back2_ref, back3_ref, other_ref, prefix_ref, total_ref, all_scr):
    odd = place_ref[2] % 2 == 1
    place = place_ref[2] // 2
    for offset, ref in enumerate((own_ref, back1_ref, back2_ref, back3_ref)):
        all_scr[(place + 4 - offset) % 4] = ref[...]
    changes = [jnp.zeros((DK, DK + DV), f32) for _ in range(HEADS)]
    for j in range(4):
        for h in range(HEADS):
            change = changes[h]

            @pl.when(place == j)
            def _(change=change, h=h):
                prefix_ref[h] = change

            changes[h] = then(change, all_scr[j, h])
    for h in range(HEADS):
        total_ref[h] = changes[h].astype(bf16)
        before = prefix_ref[h]
        prefix_ref[h] = jnp.where(odd, then(before, other_ref[h]), before)


def run_row(place, own, back1, back2, back3, other):
    return pl.pallas_call(
        row_kernel,
        out_shape=(
            jax.ShapeDtypeStruct(own.shape, f32),
            jax.ShapeDtypeStruct(own.shape, bf16),
        ),
        in_specs=[SMEM] + [VMEM] * 5,
        out_specs=(VMEM, VMEM),
        scratch_shapes=[pltpu.VMEM((4,) + own.shape, bf16)],
        compiler_params=pltpu.CompilerParams(vmem_limit_bytes=8 * 1024 * 1024),
        name="row",
    )(place, own, back1, back2, back3, other)


def mix(y, core, entering, reader_ref, local_ref, gate_ref, gain_ref, weight_ref, out_ref):
    for i in range(out_ref.shape[0] // CHUNK):
        at = pl.ds(pl.multiple_of(((y + i) % 4 * 2 + core) * CHUNK, CHUNK), CHUNK)
        parts = []
        for h in range(HEADS):
            mixed = mm(reader_ref[h, at, :], entering[h]) + local_ref[h, at, :]
            gate = gate_ref[at, h * DV : (h + 1) * DV].astype(f32)
            parts.append((rms_scale(mixed, gain_ref[...]) * silu(gate)).astype(bf16))
        gated = jnp.concatenate(parts, axis=1)
        at = slice(i * CHUNK, (i + 1) * CHUNK)
        out_ref[at, :] = jnp.dot(gated, weight_ref[...], preferred_element_type=f32).astype(bf16)


def give_kernel(
    place_ref, back1_ref, back2_ref, back3_ref, start_ref, prefix_ref, summary_ref, reader_ref, local_ref,
    gate_ref, gain_ref, weight_ref, out_ref, final_ref, entering_ref,
):
    place = place_ref[0]
    entering = []
    for h in range(HEADS):
        state = start_ref[h]
        for offset, ref in ((3, back3_ref), (2, back2_ref), (1, back1_ref)):
            state = jnp.where(place >= offset, apply(ref[h], state), state)
        state = apply(prefix_ref[h], state)
        final_ref[h] = apply(summary_ref[h], state)
        entering.append(state.astype(bf16))
        entering_ref[h] = entering[h]
    mix(place_ref[1], 1 - place_ref[3], entering, reader_ref, local_ref, gate_ref, gain_ref, weight_ref, out_ref)


def run_give(place, backs, start, prefix, summary, reader, local, gate, gain, weight):
    return pl.pallas_call(
        give_kernel,
        out_shape=(
            jax.ShapeDtypeStruct((gate.shape[0] // 2, weight.shape[1]), bf16),
            jax.ShapeDtypeStruct(start.shape, f32),
            jax.ShapeDtypeStruct(start.shape, bf16),
        ),
        in_specs=[SMEM] + [VMEM] * 11,
        out_specs=(VMEM,) * 3,
        compiler_params=pltpu.CompilerParams(vmem_limit_bytes=GRANT),
        name="give",
    )(place, *backs, start, prefix, summary, reader, local, gate, gain, weight)


def keep_kernel(place_ref, entering_ref, reader_ref, local_ref, gate_ref, gain_ref, weight_ref, out_ref):
    entering = [entering_ref[h] for h in range(HEADS)]
    mix(place_ref[1], place_ref[3], entering, reader_ref, local_ref, gate_ref, gain_ref, weight_ref, out_ref)


def run_keep(place, entering, reader, local, gate, gain, weight):
    rows = gate.shape[0] // 2
    return pl.pallas_call(
        keep_kernel,
        out_shape=jax.ShapeDtypeStruct((rows, weight.shape[1]), bf16),
        in_specs=[SMEM] + [VMEM] * 6,
        out_specs=VMEM,
        compiler_params=pltpu.CompilerParams(vmem_limit_bytes=GRANT),
        cost_estimate=pl.CostEstimate(
            flops=2 * rows * weight.size, bytes_accessed=4 * 10**6, transcendentals=0
        ),
        name="keep",
    )(place, entering, reader, local, gate, gain, weight)


def split_kernel(kept_ref, got_ref, near_ref, up_ref, down_ref, far_up_ref, far_down_ref):
    rows = near_ref.shape[0]

    def summed(at, size):
        return kept_ref[at : at + size, :].astype(f32) + got_ref[at : at + size, :].astype(f32)

    half = rows // 2
    far_up_ref[...] = summed(2 * rows, half).astype(bf16)
    far_down_ref[...] = summed(2 * rows + half, half).astype(bf16)
    near_ref[...] = summed(0, rows)
    up_ref[...] = summed(rows, rows)
    down_ref[...] = summed(3 * rows, rows)


def run_split(kept, got):
    rows = kept.shape[0] // 4
    width = kept.shape[1]
    return pl.pallas_call(
        split_kernel,
        out_shape=(jax.ShapeDtypeStruct((rows, width), f32),) * 3
        + (jax.ShapeDtypeStruct((rows // 2, width), bf16),) * 2,
        in_specs=[VMEM] * 2,
        out_specs=(VMEM,) * 5,
        compiler_params=pltpu.CompilerParams(vmem_limit_bytes=12 * 1024 * 1024),
        name="split",
    )(kept, got)


def pass_kernel(up_ref, down_ref, from_below_ref, from_above_ref, send_up_ref, send_down_ref):
    half = from_below_ref.shape[0]
    send_up_ref[:half, :] = (up_ref[:half, :] + from_below_ref[...].astype(f32)).astype(bf16)
    send_up_ref[half:, :] = up_ref[half:, :].astype(bf16)
    send_down_ref[:half, :] = down_ref[:half, :].astype(bf16)
    send_down_ref[half:, :] = (down_ref[half:, :] + from_above_ref[...].astype(f32)).astype(bf16)


def run_pass(up, down, from_below, from_above):
    return pl.pallas_call(
        pass_kernel,
        out_shape=(jax.ShapeDtypeStruct(up.shape, bf16),) * 2,
        in_specs=[VMEM] * 4,
        out_specs=(VMEM,) * 2,
        compiler_params=pltpu.CompilerParams(vmem_limit_bytes=12 * 1024 * 1024),
        name="pass",
    )(up, down, from_below, from_above)


def dispatch_kernel(own_ref, near_ref, below_ref, above_ref, gain_ref, pick_ref, hidden_ref, out_ref):
    mixed = near_ref[...] + (below_ref[...].astype(f32) + above_ref[...].astype(f32))
    hidden = own_ref[...].astype(f32) + mixed
    hidden_ref[...] = hidden
    post = rms_scale(hidden, gain_ref[...]).astype(bf16)
    half = post.shape[1] // 2
    stacked = jnp.concatenate([post[:, :half], post[:, half:]], axis=0)
    out_ref[...] = jnp.dot(pick_ref[...], stacked, preferred_element_type=f32).astype(bf16)


def run_dispatch(own, near, below, above, gain, pick):
    return pl.pallas_call(
        dispatch_kernel,
        out_shape=(
            jax.ShapeDtypeStruct(own.shape, f32),
            jax.ShapeDtypeStruct((pick.shape[0], own.shape[1] // 2), bf16),
        ),
        in_specs=[VMEM] * 6,
        out_specs=(VMEM, VMEM),
        compiler_params=pltpu.CompilerParams(vmem_limit_bytes=GRANT),
        name="dispatch",
    )(own, near, below, above, gain, pick)


def expert_kernel(rows_ref, up_ref, down_ref, out_ref):
    count, _, half = rows_ref.shape

    def hidden_of(gate_up):
        return (silu(gate_up[:, :FFE]) * gate_up[:, FFE:]).astype(bf16)

    group = 32

    def step(i, _):
        some = pl.ds(i * group, group)
        left = rows_ref[some, 0:16, :].reshape(group * 16, half)
        right = rows_ref[some, 16:32, :].reshape(group * 16, half)
        gate_up = jnp.dot(left, up_ref[:half, :], preferred_element_type=f32) + jnp.dot(
            right, up_ref[half:, :], preferred_element_type=f32
        )
        done = jnp.dot(hidden_of(gate_up), down_ref[...], preferred_element_type=f32).astype(bf16)
        out_ref[some, 0:16, :] = done[:, :half].reshape(group, 16, half)
        out_ref[some, 16:32, :] = done[:, half:].reshape(group, 16, half)
        return 0

    lax.fori_loop(0, count // group, step, 0)
    tail = rows_ref[:, 32:40, :].reshape(count * 8, half)
    first = jnp.dot(tail, up_ref[:half, :], preferred_element_type=f32)
    second = jnp.dot(tail, up_ref[half:, :], preferred_element_type=f32)
    turned = count * 8 - 4
    gate_up = first + pltpu.roll(second, turned, 0)
    done = jnp.dot(hidden_of(gate_up), down_ref[...], preferred_element_type=f32)
    upper = lax.broadcasted_iota(jnp.int32, (count * 8, half), 0) % 8 < 4
    packed = jnp.where(upper, done[:, :half], pltpu.roll(done[:, half:], 4, 0)).astype(bf16)
    out_ref[:, 32:40, :] = packed.reshape(count, 8, half)


def run_expert(rows, up, down):
    return pl.pallas_call(
        expert_kernel,
        out_shape=jax.ShapeDtypeStruct(rows.shape, bf16),
        in_specs=[VMEM] * 3,
        out_specs=VMEM,
        compiler_params=pltpu.CompilerParams(vmem_limit_bytes=GRANT),
        name="expert",
    )(rows, up, down)


def combine_kernel(hidden_ref, back_ref, high_ref, low_ref, out_ref):
    rows = hidden_ref.shape[0]
    half = back_ref.shape[1]
    back = back_ref[...]
    routed = jnp.dot(high_ref[...], back, preferred_element_type=f32) + jnp.dot(
        low_ref[...], back, preferred_element_type=f32
    )
    out_ref[:, :half] = hidden_ref[:, :half] + routed[:rows]
    out_ref[:, half:] = hidden_ref[:, half:] + routed[rows:]


def run_combine(hidden, back, high, low):
    return pl.pallas_call(
        combine_kernel,
        out_shape=jax.ShapeDtypeStruct(hidden.shape, f32),
        in_specs=[VMEM] * 4,
        out_specs=VMEM,
        compiler_params=pltpu.CompilerParams(vmem_limit_bytes=GRANT),
        name="combine",
    )(hidden, back, high, low)


def turned(size, distance):
    return [(i, (i + distance) % size) for i in range(size)]


def slot_rows(ids, experts):
    rows = ids.shape[0]
    choice = ids[:, :, None] == jnp.arange(experts, dtype=jnp.int32)
    named = jnp.any(choice, axis=1).astype(bf16)
    before = jnp.tril(jnp.ones((rows, rows), bf16), -1)
    ranks = jnp.dot(before, named, preferred_element_type=f32)
    slots = jnp.sum(jnp.where(choice, ranks[:, None, :], 0.0), axis=2).astype(jnp.int32)
    early = slots < 16
    left = ids * 40 + jnp.where(early, slots, slots + 16)
    right = ids * 40 + jnp.where(early, slots + 16, slots + 20)
    return jnp.concatenate([left, right], axis=0)


def body(
    tokens,
    input_gain,
    mixer_weight,
    rate_weight,
    conv_kernel,
    decay_scale,
    decay_bias,
    value_gain,
    output_weight,
    start_state,
    post_gain,
    expert_gateup,
    expert_down,
    route_ids,
    route_weights,
):
    own = tokens[0]
    model_width = own.shape[1]
    experts = lax.axis_size(EXP)
    normed = run_norm(own, input_gain.reshape(1, -1))
    rings = lax.axis_size("y")
    y, core = lax.axis_index("y"), lax.axis_index("core")
    up, down, swap = turned(rings, 1), turned(rings, -1), [(0, 1), (1, 0)]
    below = lax.ppermute(normed, "y", up)
    above = lax.ppermute(normed, "y", down)
    beside = lax.ppermute(normed, "core", swap)
    rate = jnp.concatenate(
        [rate_weight.reshape(model_width, -1), jnp.zeros((model_width, 128 - 2 * HEADS), bf16)], axis=1
    )
    places = slot_rows(route_ids[0], experts)
    count = experts * 40
    hits = places[:, :, None] == jnp.arange(count, dtype=jnp.int32)
    pick = jnp.any(
        places.T[:, None, :] == jnp.arange(count, dtype=jnp.int32)[None, :, None], axis=0
    ).astype(bf16)
    doubled = jnp.concatenate([route_weights[0], route_weights[0]], axis=0)
    share = jnp.sum(jnp.where(hits, doubled[:, :, None], 0.0), axis=1)
    high = share.astype(bf16)
    low = (share - high.astype(f32)).astype(bf16)
    room = 128 - 2 * HEADS
    rate_par = jnp.stack(
        [
            jnp.concatenate([jnp.zeros(HEADS, f32), decay_bias, jnp.zeros(room, f32)]),
            jnp.concatenate([jnp.zeros(HEADS, f32), decay_scale, jnp.zeros(room, f32)]),
        ]
    )
    place = jnp.stack([lax.axis_index("x"), y, lax.axis_index("z"), core]).astype(jnp.int32)
    low_half, high_half, flanks = run_cut(below, above)
    low_half, high_half, flanks, beside, rate, rate_par, conv, place, pick, high, low = lax.optimization_barrier(
        (low_half, high_half, flanks, beside, rate, rate_par, conv_kernel[:, 0], place, pick, high, low)
    )
    far_low = lax.ppermute(low_half, "y", up)
    far_high = lax.ppermute(high_half, "y", down)
    flanks = lax.ppermute(flanks, "core", swap)
    early, early_rate = run_project([normed, beside, below, above], mixer_weight, rate)
    far_low, far_high, flanks, early = lax.optimization_barrier((far_low, far_high, flanks, early))
    far = lax.ppermute(run_join(far_low, far_high), "core", swap)
    late, late_rate = run_project([flanks, far_low, far_high, far], mixer_weight, rate)
    closing = run_closing(place, [normed, beside, below, above, flanks, flanks, far_high, far])
    halo = lax.ppermute(closing, EXP, [(i, i + 1) for i in range(experts - 1)])
    gate, reader, local, summary, packed = run_delta(
        place, early, early_rate, late, late_rate, halo, mixer_weight, conv, rate_par
    )
    depth = lax.axis_size("z")
    other = lax.ppermute(packed, "z", [(i, i ^ 1) for i in range(depth)])
    both = run_couple(place, packed, other)
    pairs = [lax.ppermute(both, "z", turned(depth, 2 * step)) for step in (1, 2, 3)]
    prefix, total = run_row(place, both, *pairs, other)
    rows = [lax.ppermute(total, "x", turned(lax.axis_size("x"), step)) for step in (1, 2, 3)]
    gain = value_gain.reshape(1, -1)
    given, final_state, entering = run_give(
        place, rows, start_state, prefix, summary, reader, local, gate,
        gain, output_weight,
    )
    got = lax.ppermute(given, "core", swap)
    kept = run_keep(place, entering, reader, local, gate, gain, output_weight)
    near, to_up, to_down, far_up, far_down = run_split(kept, got)
    from_below = lax.ppermute(far_up, "y", up)
    from_above = lax.ppermute(far_down, "y", down)
    send_up, send_down = run_pass(to_up, to_down, from_below, from_above)
    mixed_below = lax.ppermute(send_up, "y", up)
    mixed_above = lax.ppermute(send_down, "y", down)

    hidden, outgoing = run_dispatch(
        own, near, mixed_below, mixed_above, post_gain.reshape(1, -1), pick
    )
    width = model_width // 2
    arrived = lax.all_to_all(outgoing.reshape(experts, 40, width), EXP, 0, 0, tiled=True)
    made = run_expert(arrived, expert_gateup[0], expert_down[0])
    back = lax.all_to_all(made, EXP, 0, 0, tiled=True)
    layer_out = run_combine(hidden, back.reshape(count, width), high, low)
    return (layer_out[None], final_state[None])


def solution(mesh):
    fine = Mesh(mesh.devices.reshape(4, 2, 4, 8), CTX + EXP)
    in_specs = (
        P(EXP, CTX, None),
        P(),
        P(None, CTX),
        P(None, CTX, None),
        P(None, CTX, None),
        P(CTX),
        P(CTX),
        P(),
        P(CTX, None),
        P(CTX, None, None),
        P(),
        P(EXP, None, None),
        P(EXP, None, None),
        P(EXP, CTX, None),
        P(EXP, CTX, None),
    )
    out_specs = (P(EXP, CTX, None), P(EXP, CTX, None, None))
    return jax.shard_map(body, mesh=fine, in_specs=in_specs, out_specs=out_specs, check_vma=False)
```

```python
import functools

import jax
import jax.numpy as jnp
from jax import lax
from jax.experimental import pallas as pl
from jax.experimental.pallas import tpu as pltpu
from jax.sharding import Mesh
from jax.sharding import PartitionSpec as P

DK = 128
DV = 128
FFE = 512
HEADS = 2
ROUTES = 4
CHUNK = 128
EPSILON = 1e-06
CTX = ("y", "core")
EXP = ("x", "z")
bf16 = jnp.bfloat16
f32 = jnp.float32
highest = lax.Precision.HIGHEST
VMEM = pl.BlockSpec(memory_space=pltpu.VMEM)
SMEM = pl.BlockSpec(memory_space=pltpu.SMEM)
GRANT = 24 * 1024 * 1024


def mm(a, b):
    return jnp.dot(a.astype(bf16), b.astype(bf16), preferred_element_type=f32)


def mm_t(a, b):
    return lax.dot_general(
        a.astype(bf16), b.astype(bf16), (((1,), (1,)), ((), ())), preferred_element_type=f32
    )


def rms_scale(values, scaling):
    widened = values.astype(f32)
    return (
        widened * lax.rsqrt(jnp.mean(widened * widened, axis=-1, keepdims=True) + EPSILON) * scaling
    )


def unit_rows(values):
    return values * lax.rsqrt(jnp.sum(values * values, axis=-1, keepdims=True) + EPSILON)


def silu(values):
    return values / (1.0 + jnp.exp(-values))


def square_iota(size, axis):
    return lax.broadcasted_iota(jnp.int32, (size, size), axis)


def norm_kernel(own_ref, gain_ref, out_ref):
    out_ref[...] = rms_scale(own_ref[...], gain_ref[...]).astype(bf16)


def run_norm(own, gain):
    return pl.pallas_call(
        norm_kernel,
        out_shape=jax.ShapeDtypeStruct(own.shape, bf16),
        in_specs=[VMEM] * 2,
        out_specs=VMEM,
        compiler_params=pltpu.CompilerParams(vmem_limit_bytes=8 * 1024 * 1024),
        name="norm",
    )(own, gain)


ORDER = ((0, 0), (0, 1), (3, 0), (1, 0), (3, 1), (1, 1), (2, 0), (2, 1))
CLOSING = (112, 112, 112, 112, 112, 240, 48, 112)


def block_of(y, core, i):
    step, side = ORDER[i]
    return (y + step) % 4 * 2 + (core + side) % 2


ANY = pl.BlockSpec(memory_space=pl.ANY)


def cut_kernel(below_ref, above_ref, low_ref, high_ref, both_ref, sems):
    rows = below_ref.shape[0]
    half = rows // 2
    copies = [
        pltpu.make_async_copy(below_ref.at[pl.ds(0, half)], low_ref, sems.at[0]),
        pltpu.make_async_copy(above_ref.at[pl.ds(half, half)], high_ref, sems.at[1]),
        pltpu.make_async_copy(below_ref, both_ref.at[pl.ds(0, rows)], sems.at[2]),
        pltpu.make_async_copy(above_ref, both_ref.at[pl.ds(rows, rows)], sems.at[3]),
    ]
    for copy in copies:
        copy.start()
    for copy in copies:
        copy.wait()


def run_cut(below, above):
    rows, width = below.shape
    return pl.pallas_call(
        cut_kernel,
        out_shape=(
            jax.ShapeDtypeStruct((rows // 2, width), bf16),
            jax.ShapeDtypeStruct((rows // 2, width), bf16),
            jax.ShapeDtypeStruct((2 * rows, width), bf16),
        ),
        in_specs=[ANY] * 2,
        out_specs=(ANY,) * 3,
        scratch_shapes=[pltpu.SemaphoreType.DMA((4,))],
        compiler_params=pltpu.CompilerParams(vmem_limit_bytes=4 * 1024 * 1024),
        name="cut",
    )(below, above)


def join_kernel(first_ref, second_ref, both_ref, sems):
    rows = first_ref.shape[0]
    copies = [
        pltpu.make_async_copy(first_ref, both_ref.at[pl.ds(0, rows)], sems.at[0]),
        pltpu.make_async_copy(second_ref, both_ref.at[pl.ds(rows, rows)], sems.at[1]),
    ]
    for copy in copies:
        copy.start()
    for copy in copies:
        copy.wait()


def run_join(first, second):
    rows, width = first.shape
    return pl.pallas_call(
        join_kernel,
        out_shape=jax.ShapeDtypeStruct((2 * rows, width), bf16),
        in_specs=[ANY] * 2,
        out_specs=ANY,
        scratch_shapes=[pltpu.SemaphoreType.DMA((2,))],
        compiler_params=pltpu.CompilerParams(vmem_limit_bytes=4 * 1024 * 1024),
        name="join",
    )(first, second)


def closing_kernel(place_ref, *refs):
    ends, out_ref, sem = refs[:-2], refs[-2], refs[-1]
    for i, (ref, at) in enumerate(zip(ends, CLOSING)):

        @pl.when(block_of(place_ref[1], place_ref[3], i) == len(ORDER) - 1)
        def _(ref=ref, at=at):
            copy = pltpu.make_async_copy(ref.at[pl.ds(at, 16)], out_ref, sem)
            copy.start()
            copy.wait()


def run_closing(place, ends):
    return pl.pallas_call(
        closing_kernel,
        out_shape=jax.ShapeDtypeStruct((16, ends[0].shape[1]), bf16),
        in_specs=[SMEM] + [ANY] * len(ends),
        out_specs=ANY,
        scratch_shapes=[pltpu.SemaphoreType.DMA],
        compiler_params=pltpu.CompilerParams(vmem_limit_bytes=4 * 1024 * 1024),
        name="closing",
    )(place, *ends)


def project_kernel(count, *refs):
    weight_ref, rate_ref, made_ref, rates_ref, rows_scr, sems = refs[count:]
    copies, at = [], 0
    for i, ref in enumerate(refs[:count]):
        copies.append(pltpu.make_async_copy(ref, rows_scr.at[pl.ds(at, ref.shape[0])], sems.at[i]))
        copies[i].start()
        at += ref.shape[0]
    for copy in copies:
        copy.wait()
    rows = rows_scr[...]
    made_ref[...] = jnp.dot(rows, weight_ref[...], preferred_element_type=f32).astype(bf16)
    rates_ref[...] = jnp.dot(rows, rate_ref[...], preferred_element_type=f32).astype(bf16)


def run_project(blocks, weight, rate):
    rows = sum(block.shape[0] for block in blocks)
    return pl.pallas_call(
        functools.partial(project_kernel, len(blocks)),
        out_shape=(
            jax.ShapeDtypeStruct((rows, weight.shape[1]), bf16),
            jax.ShapeDtypeStruct((rows, rate.shape[1]), bf16),
        ),
        in_specs=[ANY] * len(blocks) + [VMEM] * 2,
        out_specs=(VMEM, VMEM),
        scratch_shapes=[
            pltpu.VMEM((rows, weight.shape[0]), bf16),
            pltpu.SemaphoreType.DMA((len(blocks),)),
        ],
        compiler_params=pltpu.CompilerParams(vmem_limit_bytes=14 * 1024 * 1024),
        cost_estimate=pl.CostEstimate(
            flops=2 * rows * weight.size, bytes_accessed=8 * 10**6, transcendentals=0
        ),
        name="project",
    )(*blocks, weight, rate)


def delta_kernel(
    place_ref, early_ref, early_rate_ref, late_ref, late_rate_ref, halo_ref, weight_ref, conv_ref, rate_par_ref,
    gate_ref, reader_ref, local_ref, summary_ref, packed_ref,
    rows_scr, rate_scr,
):
    seg_rows = gate_ref.shape[0]
    width = conv_ref.shape[1]
    steps = seg_rows // CHUNK
    halo = jnp.dot(halo_ref[...], weight_ref[:, :width], preferred_element_type=f32)
    rows_scr[0:8, :] = halo[8:16].astype(bf16).astype(f32)
    for i in range(steps):
        made_ref, made_rate_ref = (
            (early_ref, early_rate_ref) if 2 * i < steps else (late_ref, late_rate_ref)
        )
        at = i % (steps // 2) * CHUNK
        to = pl.multiple_of(block_of(place_ref[1], place_ref[3], i) * CHUNK, CHUNK)
        rows_scr[pl.ds(pl.multiple_of(to + 8, 8), CHUNK), :] = made_ref[at : at + CHUNK, :width].astype(f32)
        gate_ref[pl.ds(to, CHUNK), :] = made_ref[at : at + CHUNK, width:]
        rate_scr[pl.ds(to, CHUNK), :] = made_rate_ref[at : at + CHUNK, :].astype(f32)

    row = square_iota(CHUNK, 0)
    col = square_iota(CHUNK, 1)
    lower = (row >= col).astype(f32)
    eye = (row == col).astype(f32)
    for h in range(HEADS):
        summary_ref[h, :, :DK] = eye
        summary_ref[h, :, DK:] = jnp.zeros((DK, DV), f32)

    pair = 8

    def chunk_step(i, _):
        units = []
        for u in range(pair):
            at = pl.multiple_of((i * pair + u) * CHUNK, CHUNK)
            window = rows_scr[pl.ds(at, CHUNK + 8), :]
            summed = conv_ref[0:1, :] * window[5 : 5 + CHUNK]
            for tap in range(1, 4):
                summed = summed + conv_ref[tap : tap + 1, :] * window[5 + tap : 5 + tap + CHUNK]
            active = silu(summed)
            query = unit_rows(active[:, :DK]) * DK ** (-0.5)
            key = unit_rows(active[:, DK : 2 * DK])
            rate = rate_scr[pl.ds(at, CHUNK), :]
            shifted = rate + rate_par_ref[0:1, :]
            soft = jnp.maximum(shifted, 0.0) + jnp.log1p(jnp.exp(-jnp.abs(shifted)))
            decay = -rate_par_ref[1:2, :] * soft
            beta_all = 1.0 / (1.0 + jnp.exp(-rate))
            total = jnp.dot(lower, decay, preferred_element_type=f32, precision=highest)
            total_t = total.T
            key_low = key.astype(bf16)
            gram = mm_t(key_low, key_low)
            raw_scores = mm_t(query, key_low)
            for h in range(HEADS):
                cum = total[:, HEADS + h : HEADS + h + 1]
                cum_row = total_t[HEADS + h : HEADS + h + 1, :]
                beta = beta_all[:, h : h + 1]
                causal = jnp.exp(jnp.where(row >= col, cum - cum_row, -1e30))
                grown = jnp.exp(cum)
                last = cum[CHUNK - 1 : CHUNK, :]
                value = active[:, 2 * DK + h * DV : 2 * DK + (h + 1) * DV]
                units.append(
                    dict(
                        at=at,
                        h=h,
                        low=jnp.where(row > col, beta * gram * causal, 0.0),
                        right=jnp.concatenate([beta * key * grown, beta * value], axis=1).astype(bf16),
                        scores=(raw_scores * causal).astype(bf16),
                        read=(query * grown).astype(bf16),
                        faded=(key * jnp.exp(last - cum)).T.astype(bf16),
                        fade=jnp.exp(last),
                    )
                )
        inverses = [
            eye - jnp.where((row // 2 == col // 2), unit["low"], 0.0) for unit in units
        ]
        size = 2
        while size < CHUNK:
            off = (row // (2 * size) == col // (2 * size)) & (row // size != col // size)
            lows = [x.astype(bf16) for x in inverses]
            firsts = [mm(jnp.where(off, unit["low"], 0.0), x) for unit, x in zip(units, lows)]
            inverses = [x - mm(x_low, y) for x, x_low, y in zip(inverses, lows, firsts)]
            size *= 2
        solved = [mm(x, unit["right"]) for unit, x in zip(units, inverses)]
        for unit, done in zip(units, solved):
            h = unit["h"]
            state = summary_ref[h]
            stacked = jnp.concatenate([done[:, :DK].astype(bf16), unit["read"]], axis=0)
            applied = mm(stacked, state)
            fresh = jnp.concatenate([-applied[:CHUNK, :DK], done[:, DK:] - applied[:CHUNK, DK:]], axis=1)
            fresh = fresh.astype(bf16)
            out = applied[CHUNK:] + mm(unit["scores"], fresh)
            summary_ref[h] = unit["fade"] * state + mm(unit["faded"], fresh)
            reader_ref[h, pl.ds(unit["at"], CHUNK), :] = out[:, :DK].astype(bf16)
            local_ref[h, pl.ds(unit["at"], CHUNK), :] = out[:, DK:]
        return 0

    lax.fori_loop(0, steps // pair, chunk_step, 0)
    for h in range(HEADS):
        change = summary_ref[h, :, :DK] - eye
        summary_ref[h, :, :DK] = change
        packed_ref[h, :, :DK] = change.astype(bf16)
        packed_ref[h, :, DK:] = summary_ref[h, :, DK:].astype(bf16)


def run_delta(place, early, early_rate, late, late_rate, halo, weight, conv, rate_par):
    rows = 2 * early.shape[0]
    return pl.pallas_call(
        delta_kernel,
        out_shape=(
            jax.ShapeDtypeStruct((rows, HEADS * DV), bf16),
            jax.ShapeDtypeStruct((HEADS, rows, DK), bf16),
            jax.ShapeDtypeStruct((HEADS, rows, DV), f32),
            jax.ShapeDtypeStruct((HEADS, DK, DK + DV), f32),
            jax.ShapeDtypeStruct((HEADS, DK, DK + DV), bf16),
        ),
        in_specs=[SMEM] + [VMEM] * 8,
        out_specs=(VMEM,) * 5,
        scratch_shapes=[
            pltpu.VMEM((rows + 8, conv.shape[1]), f32),
            pltpu.VMEM((rows, 128), f32),
        ],
        compiler_params=pltpu.CompilerParams(vmem_limit_bytes=GRANT),
        name="delta",
    )(place, early, early_rate, late, late_rate, halo, weight, conv, rate_par)


def then(first, second):
    return first + mm(second[:, :DK], first) + second.astype(f32)


def apply(change, state):
    return state + mm(change[:, :DK], state) + change[:, DK:].astype(f32)


def couple_kernel(place_ref, own_ref, other_ref, both_ref):
    odd = place_ref[2] % 2 == 1
    for h in range(HEADS):
        own = own_ref[h].astype(f32)
        other = other_ref[h].astype(f32)
        both_ref[h] = then(jnp.where(odd, other, own), jnp.where(odd, own, other)).astype(bf16)


def run_couple(place, own, other):
    return pl.pallas_call(
        couple_kernel,
        out_shape=jax.ShapeDtypeStruct(own.shape, bf16),
        in_specs=[SMEM, VMEM, VMEM],
        out_specs=VMEM,
        compiler_params=pltpu.CompilerParams(vmem_limit_bytes=8 * 1024 * 1024),
        name="couple",
    )(place, own, other)


def row_kernel(place_ref, own_ref, back1_ref, back2_ref, back3_ref, other_ref, prefix_ref, total_ref, all_scr):
    odd = place_ref[2] % 2 == 1
    place = place_ref[2] // 2
    for offset, ref in enumerate((own_ref, back1_ref, back2_ref, back3_ref)):
        all_scr[(place + 4 - offset) % 4] = ref[...]
    changes = [jnp.zeros((DK, DK + DV), f32) for _ in range(HEADS)]
    for j in range(4):
        for h in range(HEADS):
            change = changes[h]

            @pl.when(place == j)
            def _(change=change, h=h):
                prefix_ref[h] = change

            changes[h] = then(change, all_scr[j, h])
    for h in range(HEADS):
        total_ref[h] = changes[h].astype(bf16)
        before = prefix_ref[h]
        prefix_ref[h] = jnp.where(odd, then(before, other_ref[h]), before)


def run_row(place, own, back1, back2, back3, other):
    return pl.pallas_call(
        row_kernel,
        out_shape=(
            jax.ShapeDtypeStruct(own.shape, f32),
            jax.ShapeDtypeStruct(own.shape, bf16),
        ),
        in_specs=[SMEM] + [VMEM] * 5,
        out_specs=(VMEM, VMEM),
        scratch_shapes=[pltpu.VMEM((4,) + own.shape, bf16)],
        compiler_params=pltpu.CompilerParams(vmem_limit_bytes=8 * 1024 * 1024),
        name="row",
    )(place, own, back1, back2, back3, other)


def mix(y, core, entering, reader_ref, local_ref, gate_ref, gain_ref, weight_ref, out_refs):
    width = weight_ref.shape[1] // 2
    for i in range(out_refs[0].shape[0] // CHUNK):
        at = pl.ds(pl.multiple_of(((y + i) % 4 * 2 + core) * CHUNK, CHUNK), CHUNK)
        parts = []
        for h in range(HEADS):
            mixed = mm(reader_ref[h, at, :], entering[h]) + local_ref[h, at, :]
            gate = gate_ref[at, h * DV : (h + 1) * DV].astype(f32)
            parts.append((rms_scale(mixed, gain_ref[...]) * silu(gate)).astype(bf16))
        gated = jnp.concatenate(parts, axis=1)
        at = slice(i * CHUNK, (i + 1) * CHUNK)
        made = jnp.dot(gated, weight_ref[...], preferred_element_type=f32).astype(bf16)
        out_refs[0][at, :] = made[:, :width]
        out_refs[1][at, :] = made[:, width:]


def give_kernel(
    place_ref, back1_ref, back2_ref, back3_ref, start_ref, prefix_ref, summary_ref, reader_ref, local_ref,
    gate_ref, gain_ref, weight_ref, out_a_ref, out_b_ref, final_ref, entering_ref,
):
    place = place_ref[0]
    entering = []
    for h in range(HEADS):
        state = start_ref[h]
        for offset, ref in ((3, back3_ref), (2, back2_ref), (1, back1_ref)):
            state = jnp.where(place >= offset, apply(ref[h], state), state)
        state = apply(prefix_ref[h], state)
        final_ref[h] = apply(summary_ref[h], state)
        entering.append(state.astype(bf16))
        entering_ref[h] = entering[h]
    mix(place_ref[1], 1 - place_ref[3], entering, reader_ref, local_ref, gate_ref, gain_ref, weight_ref, (out_a_ref, out_b_ref))


def run_give(place, backs, start, prefix, summary, reader, local, gate, gain, weight):
    return pl.pallas_call(
        give_kernel,
        out_shape=(
            jax.ShapeDtypeStruct((gate.shape[0] // 2, weight.shape[1] // 2), bf16),
            jax.ShapeDtypeStruct((gate.shape[0] // 2, weight.shape[1] // 2), bf16),
            jax.ShapeDtypeStruct(start.shape, f32),
            jax.ShapeDtypeStruct(start.shape, bf16),
        ),
        in_specs=[SMEM] + [VMEM] * 11,
        out_specs=(VMEM,) * 4,
        compiler_params=pltpu.CompilerParams(vmem_limit_bytes=GRANT),
        name="give",
    )(place, *backs, start, prefix, summary, reader, local, gate, gain, weight)


def keep_kernel(
    place_ref, entering_ref, reader_ref, local_ref, gate_ref, gain_ref, weight_ref, out_a_ref, out_b_ref
):
    entering = [entering_ref[h] for h in range(HEADS)]
    mix(place_ref[1], place_ref[3], entering, reader_ref, local_ref, gate_ref, gain_ref, weight_ref, (out_a_ref, out_b_ref))


def run_keep(place, entering, reader, local, gate, gain, weight):
    rows = gate.shape[0] // 2
    return pl.pallas_call(
        keep_kernel,
        out_shape=(jax.ShapeDtypeStruct((rows, weight.shape[1] // 2), bf16),) * 2,
        in_specs=[SMEM] + [VMEM] * 6,
        out_specs=(VMEM,) * 2,
        compiler_params=pltpu.CompilerParams(vmem_limit_bytes=GRANT),
        cost_estimate=pl.CostEstimate(
            flops=2 * rows * weight.size, bytes_accessed=4 * 10**6, transcendentals=0
        ),
        name="keep",
    )(place, entering, reader, local, gate, gain, weight)


def split_kernel(kept_ref, got_ref, near_ref, up_ref, down_ref, far_up_ref, far_down_ref):
    rows = near_ref.shape[0]

    def summed(at, size):
        return kept_ref[at : at + size, :].astype(f32) + got_ref[at : at + size, :].astype(f32)

    half = rows // 2
    far_up_ref[...] = summed(2 * rows, half).astype(bf16)
    far_down_ref[...] = summed(2 * rows + half, half).astype(bf16)
    near_ref[...] = summed(0, rows)
    up_ref[...] = summed(rows, rows)
    down_ref[...] = summed(3 * rows, rows)


def run_split(kept, got):
    rows = kept.shape[0] // 4
    width = kept.shape[1]
    return pl.pallas_call(
        split_kernel,
        out_shape=(jax.ShapeDtypeStruct((rows, width), f32),) * 3
        + (jax.ShapeDtypeStruct((rows // 2, width), bf16),) * 2,
        in_specs=[VMEM] * 2,
        out_specs=(VMEM,) * 5,
        compiler_params=pltpu.CompilerParams(vmem_limit_bytes=12 * 1024 * 1024),
        name="split",
    )(kept, got)


def pass_kernel(up_ref, down_ref, from_below_ref, from_above_ref, send_up_ref, send_down_ref):
    half = from_below_ref.shape[0]
    send_up_ref[:half, :] = (up_ref[:half, :] + from_below_ref[...].astype(f32)).astype(bf16)
    send_up_ref[half:, :] = up_ref[half:, :].astype(bf16)
    send_down_ref[:half, :] = down_ref[:half, :].astype(bf16)
    send_down_ref[half:, :] = (down_ref[half:, :] + from_above_ref[...].astype(f32)).astype(bf16)


def run_pass(up, down, from_below, from_above):
    return pl.pallas_call(
        pass_kernel,
        out_shape=(jax.ShapeDtypeStruct(up.shape, bf16),) * 2,
        in_specs=[VMEM] * 4,
        out_specs=(VMEM,) * 2,
        compiler_params=pltpu.CompilerParams(vmem_limit_bytes=12 * 1024 * 1024),
        name="pass",
    )(up, down, from_below, from_above)


def dispatch_kernel(part, own_ref, near_ref, below_ref, above_ref, pick_ref, hidden_ref, out_ref):
    width = near_ref.shape[1]
    mixed = near_ref[...] + (below_ref[...].astype(f32) + above_ref[...].astype(f32))
    hidden = own_ref[:, part * width : (part + 1) * width].astype(f32) + mixed
    hidden_ref[...] = hidden
    half = width // 2
    low = hidden.astype(bf16)
    stacked = jnp.concatenate([low[:, :half], low[:, half:]], axis=0)
    out_ref[...] = jnp.dot(pick_ref[...], stacked, preferred_element_type=f32).astype(bf16)


def run_dispatch(part, own, near, below, above, pick):
    return pl.pallas_call(
        functools.partial(dispatch_kernel, part),
        out_shape=(
            jax.ShapeDtypeStruct(near.shape, f32),
            jax.ShapeDtypeStruct((pick.shape[0], near.shape[1] // 2), bf16),
        ),
        in_specs=[VMEM] * 5,
        out_specs=(VMEM, VMEM),
        compiler_params=pltpu.CompilerParams(vmem_limit_bytes=12 * 1024 * 1024),
        name="dispatch",
    )(own, near, below, above, pick)


def part_product(rows_ref, up_ref, gain_ref, at, ready):
    count, _, half = rows_ref.shape
    gain_left, gain_right = gain_ref[:, at : at + half], gain_ref[:, at + half : at + 2 * half]
    left = rows_ref[:, 0:16, :].reshape(count * 16, half).astype(f32)
    right = rows_ref[:, 16:32, :].reshape(count * 16, half).astype(f32)
    tail = rows_ref[:, 32:40, :].reshape(count * 8, half).astype(f32)
    turn = count * 8 - 4
    ready()
    up_left, up_right = up_ref[:half, :], up_ref[half:, :]
    product = mm(left * gain_left, up_left) + mm(right * gain_right, up_right)
    tail_product = mm(tail * gain_left, up_left) + pltpu.roll(mm(tail * gain_right, up_right), turn, 0)
    squares = jnp.sum(left * left + right * right, axis=-1, keepdims=True)
    squares = jnp.broadcast_to(squares, (count * 16, 128))
    tail_squares = jnp.broadcast_to(jnp.sum(tail * tail, axis=-1, keepdims=True), (count * 8, 128))
    tail_squares = tail_squares + pltpu.roll(tail_squares, turn, 0)
    return product, tail_product, squares, tail_squares


def first_kernel(rows_ref, up_ref, gain_ref, product_ref, squares_ref, up_scr, sem):
    copy = pltpu.make_async_copy(up_ref.at[pl.ds(0, up_scr.shape[0])], up_scr, sem)
    copy.start()
    product, tail_product, squares, tail_squares = part_product(
        rows_ref, up_scr, gain_ref, 0, copy.wait
    )
    rows = product.shape[0]
    product_ref[:rows, :] = product
    product_ref[rows:, :] = tail_product
    squares_ref[:rows, :] = squares
    squares_ref[rows:, :] = tail_squares


def run_first(rows, up, gain):
    count = rows.shape[0] * 24
    return pl.pallas_call(
        first_kernel,
        out_shape=(
            jax.ShapeDtypeStruct((count, up.shape[1]), f32),
            jax.ShapeDtypeStruct((count, 128), f32),
        ),
        in_specs=[VMEM, ANY, VMEM],
        out_specs=(VMEM, VMEM),
        scratch_shapes=[pltpu.VMEM((up.shape[0] // 2, up.shape[1]), bf16), pltpu.SemaphoreType.DMA],
        compiler_params=pltpu.CompilerParams(vmem_limit_bytes=56 * 1024 * 1024),
        cost_estimate=pl.CostEstimate(flops=count * up.size, bytes_accessed=8 * 10**6, transcendentals=0),
        name="first",
    )(rows, up, gain)


def expert_kernel(
    rows_ref, up_ref, gain_ref, product_ref, squares_ref, down_ref, out_ref, up_scr, product_scr, down_scr, sems
):
    count, _, quarter = rows_ref.shape
    half = 2 * quarter
    main = count * 16
    up_copy = pltpu.make_async_copy(up_ref.at[pl.ds(half, half)], up_scr, sems.at[0])
    product_copy = pltpu.make_async_copy(product_ref, product_scr, sems.at[1])
    down_copy = pltpu.make_async_copy(down_ref, down_scr, sems.at[2])
    up_copy.start()
    product_copy.start()
    down_copy.start()
    product, tail_product, squares, tail_squares = part_product(
        rows_ref, up_scr, gain_ref, half, up_copy.wait
    )
    product_copy.wait()
    down_copy.wait()

    def finished(made, earlier, square, earlier_square):
        scale = lax.rsqrt((square + earlier_square)[:, 0:1] / (2 * half) + EPSILON)
        gate_up = (made + earlier) * scale
        hidden = (silu(gate_up[:, :FFE]) * gate_up[:, FFE:]).astype(bf16)
        return jnp.dot(hidden, down_scr[...], preferred_element_type=f32)

    done = finished(product, product_scr[:main, :], squares, squares_ref[:main, :]).astype(bf16)
    out_ref[:, 0:16, :] = done[:, :half].reshape(count, 16, half)
    out_ref[:, 16:32, :] = done[:, half:].reshape(count, 16, half)
    done = finished(tail_product, product_scr[main:, :], tail_squares, squares_ref[main:, :])
    upper = lax.broadcasted_iota(jnp.int32, (count * 8, half), 0) % 8 < 4
    packed = jnp.where(upper, done[:, :half], pltpu.roll(done[:, half:], 4, 0)).astype(bf16)
    out_ref[:, 32:40, :] = packed.reshape(count, 8, half)


def run_expert(rows, up, gain, product, squares, down):
    return pl.pallas_call(
        expert_kernel,
        out_shape=jax.ShapeDtypeStruct(rows.shape[:2] + (2 * rows.shape[2],), bf16),
        in_specs=[VMEM, ANY, VMEM, ANY, VMEM, ANY],
        out_specs=VMEM,
        scratch_shapes=[
            pltpu.VMEM((up.shape[0] // 2, up.shape[1]), bf16),
            pltpu.VMEM(product.shape, f32),
            pltpu.VMEM(down.shape, bf16),
            pltpu.SemaphoreType.DMA((3,)),
        ],
        compiler_params=pltpu.CompilerParams(vmem_limit_bytes=56 * 1024 * 1024),
        name="expert",
    )(rows, up, gain, product, squares, down)


def combine_kernel(left_ref, right_ref, back_ref, high_ref, low_ref, out_ref):
    rows = left_ref.shape[0]
    half = back_ref.shape[1]
    back = back_ref[...]
    routed = jnp.dot(high_ref[...], back, preferred_element_type=f32) + jnp.dot(
        low_ref[...], back, preferred_element_type=f32
    )
    out_ref[:, :half] = left_ref[...] + routed[:rows]
    out_ref[:, half:] = right_ref[...] + routed[rows:]


def run_combine(left, right, back, high, low):
    return pl.pallas_call(
        combine_kernel,
        out_shape=jax.ShapeDtypeStruct((left.shape[0], 2 * left.shape[1]), f32),
        in_specs=[VMEM] * 5,
        out_specs=VMEM,
        compiler_params=pltpu.CompilerParams(vmem_limit_bytes=GRANT),
        name="combine",
    )(left, right, back, high, low)


def turned(size, distance):
    return [(i, (i + distance) % size) for i in range(size)]


def slot_rows(ids, experts):
    rows = ids.shape[0]
    choice = ids[:, :, None] == jnp.arange(experts, dtype=jnp.int32)
    named = jnp.any(choice, axis=1).astype(bf16)
    before = jnp.tril(jnp.ones((rows, rows), bf16), -1)
    ranks = jnp.dot(before, named, preferred_element_type=f32)
    slots = jnp.sum(jnp.where(choice, ranks[:, None, :], 0.0), axis=2).astype(jnp.int32)
    early = slots < 16
    left = ids * 40 + jnp.where(early, slots, slots + 16)
    right = ids * 40 + jnp.where(early, slots + 16, slots + 20)
    return jnp.concatenate([left, right], axis=0)


def body(
    tokens,
    input_gain,
    mixer_weight,
    rate_weight,
    conv_kernel,
    decay_scale,
    decay_bias,
    value_gain,
    output_weight,
    start_state,
    post_gain,
    expert_gateup,
    expert_down,
    route_ids,
    route_weights,
):
    own = tokens[0]
    model_width = own.shape[1]
    experts = lax.axis_size(EXP)
    normed = run_norm(own, input_gain.reshape(1, -1))
    rings = lax.axis_size("y")
    y, core = lax.axis_index("y"), lax.axis_index("core")
    up, down, swap = turned(rings, 1), turned(rings, -1), [(0, 1), (1, 0)]
    below = lax.ppermute(normed, "y", up)
    above = lax.ppermute(normed, "y", down)
    beside = lax.ppermute(normed, "core", swap)
    rate = jnp.concatenate(
        [rate_weight.reshape(model_width, -1), jnp.zeros((model_width, 128 - 2 * HEADS), bf16)], axis=1
    )
    places = slot_rows(route_ids[0], experts)
    count = experts * 40
    hits = places[:, :, None] == jnp.arange(count, dtype=jnp.int32)
    pick = jnp.any(
        places.T[:, None, :] == jnp.arange(count, dtype=jnp.int32)[None, :, None], axis=0
    ).astype(bf16)
    doubled = jnp.concatenate([route_weights[0], route_weights[0]], axis=0)
    share = jnp.sum(jnp.where(hits, doubled[:, :, None], 0.0), axis=1)
    high = share.astype(bf16)
    low = (share - high.astype(f32)).astype(bf16)
    room = 128 - 2 * HEADS
    rate_par = jnp.stack(
        [
            jnp.concatenate([jnp.zeros(HEADS, f32), decay_bias, jnp.zeros(room, f32)]),
            jnp.concatenate([jnp.zeros(HEADS, f32), decay_scale, jnp.zeros(room, f32)]),
        ]
    )
    place = jnp.stack([lax.axis_index("x"), y, lax.axis_index("z"), core]).astype(jnp.int32)
    low_half, high_half, flanks = run_cut(below, above)
    low_half, high_half, flanks, beside, rate, rate_par, conv, place, pick, high, low = lax.optimization_barrier(
        (low_half, high_half, flanks, beside, rate, rate_par, conv_kernel[:, 0], place, pick, high, low)
    )
    far_low = lax.ppermute(low_half, "y", up)
    far_high = lax.ppermute(high_half, "y", down)
    flanks = lax.ppermute(flanks, "core", swap)
    early, early_rate = run_project([normed, beside, below, above], mixer_weight, rate)
    far_low, far_high, flanks, early = lax.optimization_barrier((far_low, far_high, flanks, early))
    far = lax.ppermute(run_join(far_low, far_high), "core", swap)
    late, late_rate = run_project([flanks, far_low, far_high, far], mixer_weight, rate)
    closing = run_closing(place, [normed, beside, below, above, flanks, flanks, far_high, far])
    halo = lax.ppermute(closing, EXP, [(i, i + 1) for i in range(experts - 1)])
    gate, reader, local, summary, packed = run_delta(
        place, early, early_rate, late, late_rate, halo, mixer_weight, conv, rate_par
    )
    depth = lax.axis_size("z")
    other = lax.ppermute(packed, "z", [(i, i ^ 1) for i in range(depth)])
    both = run_couple(place, packed, other)
    pairs = [lax.ppermute(both, "z", turned(depth, 2 * step)) for step in (1, 2, 3)]
    prefix, total = run_row(place, both, *pairs, other)
    rows = [lax.ppermute(total, "x", turned(lax.axis_size("x"), step)) for step in (1, 2, 3)]
    gain = value_gain.reshape(1, -1)
    given_a, given_b, final_state, entering = run_give(
        place, rows, start_state, prefix, summary, reader, local, gate, gain, output_weight
    )
    got_a = lax.ppermute(given_a, "core", swap)
    kept_a, kept_b = run_keep(place, entering, reader, local, gate, gain, output_weight)
    got_a, given_b = lax.optimization_barrier((got_a, given_b))
    got_b = lax.ppermute(given_b, "core", swap)
    post = post_gain.reshape(1, -1)
    count = experts * 40

    def passed_on(to_up, to_down, far_up, far_down):
        from_below = lax.ppermute(far_up, "y", up)
        from_above = lax.ppermute(far_down, "y", down)
        send_up, send_down = run_pass(to_up, to_down, from_below, from_above)
        return lax.ppermute(send_up, "y", up), lax.ppermute(send_down, "y", down)

    def sent_out(outgoing):
        return lax.all_to_all(outgoing.reshape(experts, 40, -1), EXP, 0, 0, tiled=True)

    near_a, *parts_a = run_split(kept_a, got_a)
    hidden_a, outgoing_a = run_dispatch(0, own, near_a, *passed_on(*parts_a), pick)
    outgoing_a, kept_b, got_b = lax.optimization_barrier((outgoing_a, kept_b, got_b))
    arrived_a = sent_out(outgoing_a)
    near_b, *parts_b = run_split(kept_b, got_b)
    hidden_b, outgoing_b = run_dispatch(1, own, near_b, *passed_on(*parts_b), pick)
    arrived_b = sent_out(outgoing_b)
    product, squares = run_first(arrived_a, expert_gateup[0], post)
    made = run_expert(arrived_b, expert_gateup[0], post, product, squares, expert_down[0])
    back = lax.all_to_all(made, EXP, 0, 0, tiled=True)
    layer_out = run_combine(hidden_a, hidden_b, back.reshape(count, -1), high, low)
    return (layer_out[None], final_state[None])


def solution(mesh):
    fine = Mesh(mesh.devices.reshape(4, 2, 4, 8), CTX + EXP)
    in_specs = (
        P(EXP, CTX, None),
        P(),
        P(None, CTX),
        P(None, CTX, None),
        P(None, CTX, None),
        P(CTX),
        P(CTX),
        P(),
        P(CTX, None),
        P(CTX, None, None),
        P(),
        P(EXP, None, None),
        P(EXP, None, None),
        P(EXP, CTX, None),
        P(EXP, CTX, None),
    )
    out_specs = (P(EXP, CTX, None), P(EXP, CTX, None, None))
    return jax.shard_map(body, mesh=fine, in_specs=in_specs, out_specs=out_specs, check_vma=False)
```

```python
import functools

import jax
import jax.numpy as jnp
from jax import lax
from jax.experimental import pallas as pl
from jax.experimental.pallas import tpu as pltpu
from jax.sharding import Mesh
from jax.sharding import PartitionSpec as P

DK = 128
DV = 128
FFE = 512
HEADS = 2
ROUTES = 4
CHUNK = 128
EPSILON = 1e-06
CTX = ("y", "core")
EXP = ("x", "z")
bf16 = jnp.bfloat16
f32 = jnp.float32
highest = lax.Precision.HIGHEST
VMEM = pl.BlockSpec(memory_space=pltpu.VMEM)
SMEM = pl.BlockSpec(memory_space=pltpu.SMEM)
GRANT = 24 * 1024 * 1024


def mm(a, b):
    return jnp.dot(a.astype(bf16), b.astype(bf16), preferred_element_type=f32)


def mm_t(a, b):
    return lax.dot_general(
        a.astype(bf16), b.astype(bf16), (((1,), (1,)), ((), ())), preferred_element_type=f32
    )


def rms_scale(values, scaling):
    widened = values.astype(f32)
    return (
        widened * lax.rsqrt(jnp.mean(widened * widened, axis=-1, keepdims=True) + EPSILON) * scaling
    )


def unit_rows(values):
    return values * lax.rsqrt(jnp.sum(values * values, axis=-1, keepdims=True) + EPSILON)


def silu(values):
    return values / (1.0 + jnp.exp(-values))


def square_iota(size, axis):
    return lax.broadcasted_iota(jnp.int32, (size, size), axis)


def norm_kernel(own_ref, gain_ref, out_ref):
    out_ref[...] = rms_scale(own_ref[...], gain_ref[...]).astype(bf16)


def run_norm(own, gain):
    return pl.pallas_call(
        norm_kernel,
        out_shape=jax.ShapeDtypeStruct(own.shape, bf16),
        in_specs=[VMEM] * 2,
        out_specs=VMEM,
        compiler_params=pltpu.CompilerParams(vmem_limit_bytes=8 * 1024 * 1024),
        name="norm",
    )(own, gain)


ORDER = ((0, 0), (0, 1), (3, 0), (1, 0), (3, 1), (1, 1), (2, 0), (2, 1))
CLOSING = (112, 112, 112, 112, 112, 240, 48, 112)


def block_of(y, core, i):
    step, side = ORDER[i]
    return (y + step) % 4 * 2 + (core + side) % 2


ANY = pl.BlockSpec(memory_space=pl.ANY)


def cut_kernel(below_ref, above_ref, low_ref, high_ref, both_ref, sems):
    rows = below_ref.shape[0]
    half = rows // 2
    copies = [
        pltpu.make_async_copy(below_ref.at[pl.ds(0, half)], low_ref, sems.at[0]),
        pltpu.make_async_copy(above_ref.at[pl.ds(half, half)], high_ref, sems.at[1]),
        pltpu.make_async_copy(below_ref, both_ref.at[pl.ds(0, rows)], sems.at[2]),
        pltpu.make_async_copy(above_ref, both_ref.at[pl.ds(rows, rows)], sems.at[3]),
    ]
    for copy in copies:
        copy.start()
    for copy in copies:
        copy.wait()


def run_cut(below, above):
    rows, width = below.shape
    return pl.pallas_call(
        cut_kernel,
        out_shape=(
            jax.ShapeDtypeStruct((rows // 2, width), bf16),
            jax.ShapeDtypeStruct((rows // 2, width), bf16),
            jax.ShapeDtypeStruct((2 * rows, width), bf16),
        ),
        in_specs=[ANY] * 2,
        out_specs=(ANY,) * 3,
        scratch_shapes=[pltpu.SemaphoreType.DMA((4,))],
        compiler_params=pltpu.CompilerParams(vmem_limit_bytes=4 * 1024 * 1024),
        name="cut",
    )(below, above)


def join_kernel(first_ref, second_ref, both_ref, sems):
    rows = first_ref.shape[0]
    copies = [
        pltpu.make_async_copy(first_ref, both_ref.at[pl.ds(0, rows)], sems.at[0]),
        pltpu.make_async_copy(second_ref, both_ref.at[pl.ds(rows, rows)], sems.at[1]),
    ]
    for copy in copies:
        copy.start()
    for copy in copies:
        copy.wait()


def run_join(first, second):
    rows, width = first.shape
    return pl.pallas_call(
        join_kernel,
        out_shape=jax.ShapeDtypeStruct((2 * rows, width), bf16),
        in_specs=[ANY] * 2,
        out_specs=ANY,
        scratch_shapes=[pltpu.SemaphoreType.DMA((2,))],
        compiler_params=pltpu.CompilerParams(vmem_limit_bytes=4 * 1024 * 1024),
        name="join",
    )(first, second)


def closing_kernel(place_ref, *refs):
    ends, out_ref, sem = refs[:-2], refs[-2], refs[-1]
    for i, (ref, at) in enumerate(zip(ends, CLOSING)):

        @pl.when(block_of(place_ref[1], place_ref[3], i) == len(ORDER) - 1)
        def _(ref=ref, at=at):
            copy = pltpu.make_async_copy(ref.at[pl.ds(at, 16)], out_ref, sem)
            copy.start()
            copy.wait()


def run_closing(place, ends):
    return pl.pallas_call(
        closing_kernel,
        out_shape=jax.ShapeDtypeStruct((16, ends[0].shape[1]), bf16),
        in_specs=[SMEM] + [ANY] * len(ends),
        out_specs=ANY,
        scratch_shapes=[pltpu.SemaphoreType.DMA],
        compiler_params=pltpu.CompilerParams(vmem_limit_bytes=4 * 1024 * 1024),
        name="closing",
    )(place, *ends)


def project_kernel(count, *refs):
    weight_ref, rate_ref, made_ref, rates_ref, rows_scr, sems = refs[count:]
    copies, at = [], 0
    for i, ref in enumerate(refs[:count]):
        copies.append(pltpu.make_async_copy(ref, rows_scr.at[pl.ds(at, ref.shape[0])], sems.at[i]))
        copies[i].start()
        at += ref.shape[0]
    for copy in copies:
        copy.wait()
    rows = rows_scr[...]
    made_ref[...] = jnp.dot(rows, weight_ref[...], preferred_element_type=f32).astype(bf16)
    rates_ref[...] = jnp.dot(rows, rate_ref[...], preferred_element_type=f32).astype(bf16)


def run_project(blocks, weight, rate):
    rows = sum(block.shape[0] for block in blocks)
    return pl.pallas_call(
        functools.partial(project_kernel, len(blocks)),
        out_shape=(
            jax.ShapeDtypeStruct((rows, weight.shape[1]), bf16),
            jax.ShapeDtypeStruct((rows, rate.shape[1]), bf16),
        ),
        in_specs=[ANY] * len(blocks) + [VMEM] * 2,
        out_specs=(VMEM, VMEM),
        scratch_shapes=[
            pltpu.VMEM((rows, weight.shape[0]), bf16),
            pltpu.SemaphoreType.DMA((len(blocks),)),
        ],
        compiler_params=pltpu.CompilerParams(vmem_limit_bytes=14 * 1024 * 1024),
        cost_estimate=pl.CostEstimate(
            flops=2 * rows * weight.size, bytes_accessed=8 * 10**6, transcendentals=0
        ),
        name="project",
    )(*blocks, weight, rate)


def delta_kernel(
    place_ref, early_ref, early_rate_ref, late_ref, late_rate_ref, halo_ref, weight_ref, conv_ref, rate_par_ref,
    gate_ref, reader_ref, local_ref, summary_ref, packed_ref,
    rows_scr, rate_scr,
):
    seg_rows = gate_ref.shape[0]
    width = conv_ref.shape[1]
    steps = seg_rows // CHUNK
    halo = jnp.dot(halo_ref[...], weight_ref[:, :width], preferred_element_type=f32)
    rows_scr[0:8, :] = halo[8:16].astype(bf16).astype(f32)
    for i in range(steps):
        made_ref, made_rate_ref = (
            (early_ref, early_rate_ref) if 2 * i < steps else (late_ref, late_rate_ref)
        )
        at = i % (steps // 2) * CHUNK
        to = pl.multiple_of(block_of(place_ref[1], place_ref[3], i) * CHUNK, CHUNK)
        rows_scr[pl.ds(pl.multiple_of(to + 8, 8), CHUNK), :] = made_ref[at : at + CHUNK, :width].astype(f32)
        gate_ref[pl.ds(to, CHUNK), :] = made_ref[at : at + CHUNK, width:]
        rate_scr[pl.ds(to, CHUNK), :] = made_rate_ref[at : at + CHUNK, :].astype(f32)

    row = square_iota(CHUNK, 0)
    col = square_iota(CHUNK, 1)
    lower = (row >= col).astype(f32)
    eye = (row == col).astype(f32)
    for h in range(HEADS):
        summary_ref[h, :, :DK] = eye
        summary_ref[h, :, DK:] = jnp.zeros((DK, DV), f32)

    pair = 8

    def chunk_step(i, _):
        units = []
        for u in range(pair):
            at = pl.multiple_of((i * pair + u) * CHUNK, CHUNK)
            window = rows_scr[pl.ds(at, CHUNK + 8), :]
            summed = conv_ref[0:1, :] * window[5 : 5 + CHUNK]
            for tap in range(1, 4):
                summed = summed + conv_ref[tap : tap + 1, :] * window[5 + tap : 5 + tap + CHUNK]
            active = silu(summed)
            query = unit_rows(active[:, :DK]) * DK ** (-0.5)
            key = unit_rows(active[:, DK : 2 * DK])
            rate = rate_scr[pl.ds(at, CHUNK), :]
            shifted = rate + rate_par_ref[0:1, :]
            soft = jnp.maximum(shifted, 0.0) + jnp.log1p(jnp.exp(-jnp.abs(shifted)))
            decay = -rate_par_ref[1:2, :] * soft
            beta_all = 1.0 / (1.0 + jnp.exp(-rate))
            total = jnp.dot(lower, decay, preferred_element_type=f32, precision=highest)
            total_t = total.T
            key_low = key.astype(bf16)
            gram = mm_t(key_low, key_low)
            raw_scores = mm_t(query, key_low)
            for h in range(HEADS):
                cum = total[:, HEADS + h : HEADS + h + 1]
                cum_row = total_t[HEADS + h : HEADS + h + 1, :]
                beta = beta_all[:, h : h + 1]
                causal = jnp.exp(jnp.where(row >= col, cum - cum_row, -1e30))
                grown = jnp.exp(cum)
                last = cum[CHUNK - 1 : CHUNK, :]
                value = active[:, 2 * DK + h * DV : 2 * DK + (h + 1) * DV]
                units.append(
                    dict(
                        at=at,
                        h=h,
                        low=jnp.where(row > col, beta * gram * causal, 0.0),
                        right=jnp.concatenate([beta * key * grown, beta * value], axis=1).astype(bf16),
                        scores=(raw_scores * causal).astype(bf16),
                        read=(query * grown).astype(bf16),
                        faded=(key * jnp.exp(last - cum)).T.astype(bf16),
                        fade=jnp.exp(last),
                    )
                )
        inverses = [
            eye - jnp.where((row // 2 == col // 2), unit["low"], 0.0) for unit in units
        ]
        size = 2
        while size < CHUNK:
            off = (row // (2 * size) == col // (2 * size)) & (row // size != col // size)
            lows = [x.astype(bf16) for x in inverses]
            firsts = [mm(jnp.where(off, unit["low"], 0.0), x) for unit, x in zip(units, lows)]
            inverses = [x - mm(x_low, y) for x, x_low, y in zip(inverses, lows, firsts)]
            size *= 2
        solved = [mm(x, unit["right"]) for unit, x in zip(units, inverses)]
        for unit, done in zip(units, solved):
            h = unit["h"]
            state = summary_ref[h]
            stacked = jnp.concatenate([done[:, :DK].astype(bf16), unit["read"]], axis=0)
            applied = mm(stacked, state)
            fresh = jnp.concatenate([-applied[:CHUNK, :DK], done[:, DK:] - applied[:CHUNK, DK:]], axis=1)
            fresh = fresh.astype(bf16)
            out = applied[CHUNK:] + mm(unit["scores"], fresh)
            summary_ref[h] = unit["fade"] * state + mm(unit["faded"], fresh)
            reader_ref[h, pl.ds(unit["at"], CHUNK), :] = out[:, :DK].astype(bf16)
            local_ref[h, pl.ds(unit["at"], CHUNK), :] = out[:, DK:]
        return 0

    lax.fori_loop(0, steps // pair, chunk_step, 0)
    for h in range(HEADS):
        change = summary_ref[h, :, :DK] - eye
        summary_ref[h, :, :DK] = change
        packed_ref[h, :, :DK] = change.astype(bf16)
        packed_ref[h, :, DK:] = summary_ref[h, :, DK:].astype(bf16)


def run_delta(place, early, early_rate, late, late_rate, halo, weight, conv, rate_par):
    rows = 2 * early.shape[0]
    return pl.pallas_call(
        delta_kernel,
        out_shape=(
            jax.ShapeDtypeStruct((rows, HEADS * DV), bf16),
            jax.ShapeDtypeStruct((HEADS, rows, DK), bf16),
            jax.ShapeDtypeStruct((HEADS, rows, DV), f32),
            jax.ShapeDtypeStruct((HEADS, DK, DK + DV), f32),
            jax.ShapeDtypeStruct((HEADS, DK, DK + DV), bf16),
        ),
        in_specs=[SMEM] + [VMEM] * 8,
        out_specs=(VMEM,) * 5,
        scratch_shapes=[
            pltpu.VMEM((rows + 8, conv.shape[1]), f32),
            pltpu.VMEM((rows, 128), f32),
        ],
        compiler_params=pltpu.CompilerParams(vmem_limit_bytes=GRANT),
        name="delta",
    )(place, early, early_rate, late, late_rate, halo, weight, conv, rate_par)


def then(first, second):
    return first + mm(second[:, :DK], first) + second.astype(f32)


def apply(change, state):
    return state + mm(change[:, :DK], state) + change[:, DK:].astype(f32)


def couple_kernel(place_ref, own_ref, other_ref, both_ref):
    odd = place_ref[2] % 2 == 1
    for h in range(HEADS):
        own = own_ref[h].astype(f32)
        other = other_ref[h].astype(f32)
        both_ref[h] = then(jnp.where(odd, other, own), jnp.where(odd, own, other)).astype(bf16)


def run_couple(place, own, other):
    return pl.pallas_call(
        couple_kernel,
        out_shape=jax.ShapeDtypeStruct(own.shape, bf16),
        in_specs=[SMEM, VMEM, VMEM],
        out_specs=VMEM,
        compiler_params=pltpu.CompilerParams(vmem_limit_bytes=8 * 1024 * 1024),
        name="couple",
    )(place, own, other)


def row_kernel(place_ref, own_ref, back1_ref, back2_ref, back3_ref, other_ref, prefix_ref, total_ref, all_scr):
    odd = place_ref[2] % 2 == 1
    place = place_ref[2] // 2
    for offset, ref in enumerate((own_ref, back1_ref, back2_ref, back3_ref)):
        all_scr[(place + 4 - offset) % 4] = ref[...]
    changes = [jnp.zeros((DK, DK + DV), f32) for _ in range(HEADS)]
    for j in range(4):
        for h in range(HEADS):
            change = changes[h]

            @pl.when(place == j)
            def _(change=change, h=h):
                prefix_ref[h] = change

            changes[h] = then(change, all_scr[j, h])
    for h in range(HEADS):
        total_ref[h] = changes[h].astype(bf16)
        before = prefix_ref[h]
        prefix_ref[h] = jnp.where(odd, then(before, other_ref[h]), before)


def run_row(place, own, back1, back2, back3, other):
    return pl.pallas_call(
        row_kernel,
        out_shape=(
            jax.ShapeDtypeStruct(own.shape, f32),
            jax.ShapeDtypeStruct(own.shape, bf16),
        ),
        in_specs=[SMEM] + [VMEM] * 5,
        out_specs=(VMEM, VMEM),
        scratch_shapes=[pltpu.VMEM((4,) + own.shape, bf16)],
        compiler_params=pltpu.CompilerParams(vmem_limit_bytes=8 * 1024 * 1024),
        name="row",
    )(place, own, back1, back2, back3, other)


def mix(y, core, entering, reader_ref, local_ref, gate_ref, gain_ref, weight_ref, out_ref):
    for i in range(out_ref.shape[0] // CHUNK):
        at = pl.ds(pl.multiple_of(((y + i) % 4 * 2 + core) * CHUNK, CHUNK), CHUNK)
        parts = []
        for h in range(HEADS):
            mixed = mm(reader_ref[h, at, :], entering[h]) + local_ref[h, at, :]
            gate = gate_ref[at, h * DV : (h + 1) * DV].astype(f32)
            parts.append((rms_scale(mixed, gain_ref[...]) * silu(gate)).astype(bf16))
        gated = jnp.concatenate(parts, axis=1)
        at = slice(i * CHUNK, (i + 1) * CHUNK)
        out_ref[at, :] = jnp.dot(gated, weight_ref[...], preferred_element_type=f32).astype(bf16)


def give_kernel(
    place_ref, back1_ref, back2_ref, back3_ref, start_ref, prefix_ref, summary_ref, reader_ref, local_ref,
    gate_ref, gain_ref, weight_ref, out_ref, final_ref, entering_ref,
):
    place = place_ref[0]
    entering = []
    for h in range(HEADS):
        state = start_ref[h]
        for offset, ref in ((3, back3_ref), (2, back2_ref), (1, back1_ref)):
            state = jnp.where(place >= offset, apply(ref[h], state), state)
        state = apply(prefix_ref[h], state)
        final_ref[h] = apply(summary_ref[h], state)
        entering.append(state.astype(bf16))
        entering_ref[h] = entering[h]
    mix(place_ref[1], 1 - place_ref[3], entering, reader_ref, local_ref, gate_ref, gain_ref, weight_ref, out_ref)


def run_give(place, backs, start, prefix, summary, reader, local, gate, gain, weight):
    return pl.pallas_call(
        give_kernel,
        out_shape=(
            jax.ShapeDtypeStruct((gate.shape[0] // 2, weight.shape[1]), bf16),
            jax.ShapeDtypeStruct(start.shape, f32),
            jax.ShapeDtypeStruct(start.shape, bf16),
        ),
        in_specs=[SMEM] + [VMEM] * 11,
        out_specs=(VMEM,) * 3,
        compiler_params=pltpu.CompilerParams(vmem_limit_bytes=GRANT),
        name="give",
    )(place, *backs, start, prefix, summary, reader, local, gate, gain, weight)


def keep_kernel(place_ref, entering_ref, reader_ref, local_ref, gate_ref, gain_ref, weight_ref, out_ref):
    entering = [entering_ref[h] for h in range(HEADS)]
    mix(place_ref[1], place_ref[3], entering, reader_ref, local_ref, gate_ref, gain_ref, weight_ref, out_ref)


def run_keep(place, entering, reader, local, gate, gain, weight):
    rows = gate.shape[0] // 2
    return pl.pallas_call(
        keep_kernel,
        out_shape=jax.ShapeDtypeStruct((rows, weight.shape[1]), bf16),
        in_specs=[SMEM] + [VMEM] * 6,
        out_specs=VMEM,
        compiler_params=pltpu.CompilerParams(vmem_limit_bytes=GRANT),
        cost_estimate=pl.CostEstimate(
            flops=2 * rows * weight.size, bytes_accessed=4 * 10**6, transcendentals=0
        ),
        name="keep",
    )(place, entering, reader, local, gate, gain, weight)


def split_kernel(
    place_ref, kept_ref, got_ref, near_ref, up_ref, down_ref, far_up_ref, far_down_ref, first_ref, second_ref
):
    rows = near_ref.shape[0]
    half = rows // 2

    def summed(at, size):
        return kept_ref[at : at + size, :].astype(f32) + got_ref[at : at + size, :].astype(f32)

    far_up_ref[...] = summed(2 * rows, half).astype(bf16)
    far_down_ref[...] = summed(2 * rows + half, half).astype(bf16)
    near_ref[...] = summed(0, rows)
    up_ref[...] = summed(rows, half)
    down_ref[...] = summed(3 * rows + half, half)
    direct_up = summed(rows + half, half).astype(bf16)
    direct_down = summed(3 * rows, half).astype(bf16)
    even = place_ref[3] == 0

    @pl.when(even)
    def _():
        first_ref[...] = direct_up
        second_ref[...] = direct_down

    @pl.when(jnp.logical_not(even))
    def _():
        first_ref[...] = direct_down
        second_ref[...] = direct_up


def run_split(place, kept, got):
    rows = kept.shape[0] // 4
    width = kept.shape[1]
    return pl.pallas_call(
        split_kernel,
        out_shape=(jax.ShapeDtypeStruct((rows, width), f32),)
        + (jax.ShapeDtypeStruct((rows // 2, width), f32),) * 2
        + (jax.ShapeDtypeStruct((rows // 2, width), bf16),) * 4,
        in_specs=[SMEM] + [VMEM] * 2,
        out_specs=(VMEM,) * 7,
        compiler_params=pltpu.CompilerParams(vmem_limit_bytes=12 * 1024 * 1024),
        name="split",
    )(place, kept, got)


def pass_kernel(up_ref, down_ref, from_below_ref, from_above_ref, send_up_ref, send_down_ref):
    send_up_ref[...] = (up_ref[...] + from_below_ref[...].astype(f32)).astype(bf16)
    send_down_ref[...] = (down_ref[...] + from_above_ref[...].astype(f32)).astype(bf16)


def run_pass(up, down, from_below, from_above):
    return pl.pallas_call(
        pass_kernel,
        out_shape=(jax.ShapeDtypeStruct(up.shape, bf16),) * 2,
        in_specs=[VMEM] * 4,
        out_specs=(VMEM,) * 2,
        compiler_params=pltpu.CompilerParams(vmem_limit_bytes=12 * 1024 * 1024),
        name="pass",
    )(up, down, from_below, from_above)


def dispatch_kernel(
    place_ref, own_ref, near_ref, below_ref, above_ref, first_ref, second_ref, gain_ref, pick_ref, hidden_ref, out_ref
):
    even = place_ref[3] == 0
    first = first_ref[...].astype(f32)
    second = second_ref[...].astype(f32)
    low = below_ref[...].astype(f32) + jnp.where(even, second, first)
    high = above_ref[...].astype(f32) + jnp.where(even, first, second)
    arrived = jnp.concatenate([low, high], axis=0)
    hidden = own_ref[...].astype(f32) + (near_ref[...] + arrived)
    hidden_ref[...] = hidden
    post = rms_scale(hidden, gain_ref[...]).astype(bf16)
    half = post.shape[1] // 2
    stacked = jnp.concatenate([post[:, :half], post[:, half:]], axis=0)
    out_ref[...] = jnp.dot(pick_ref[...], stacked, preferred_element_type=f32).astype(bf16)


def run_dispatch(place, own, near, below, above, first, second, gain, pick):
    return pl.pallas_call(
        dispatch_kernel,
        out_shape=(
            jax.ShapeDtypeStruct(own.shape, f32),
            jax.ShapeDtypeStruct((pick.shape[0], own.shape[1] // 2), bf16),
        ),
        in_specs=[SMEM] + [VMEM] * 8,
        out_specs=(VMEM, VMEM),
        compiler_params=pltpu.CompilerParams(vmem_limit_bytes=GRANT),
        name="dispatch",
    )(place, own, near, below, above, first, second, gain, pick)


def expert_kernel(rows_ref, up_ref, down_ref, out_ref):
    count, _, half = rows_ref.shape

    def hidden_of(gate_up):
        return (silu(gate_up[:, :FFE]) * gate_up[:, FFE:]).astype(bf16)

    group = 32

    def step(i, _):
        some = pl.ds(i * group, group)
        left = rows_ref[some, 0:16, :].reshape(group * 16, half)
        right = rows_ref[some, 16:32, :].reshape(group * 16, half)
        gate_up = jnp.dot(left, up_ref[:half, :], preferred_element_type=f32) + jnp.dot(
            right, up_ref[half:, :], preferred_element_type=f32
        )
        done = jnp.dot(hidden_of(gate_up), down_ref[...], preferred_element_type=f32).astype(bf16)
        out_ref[some, 0:16, :] = done[:, :half].reshape(group, 16, half)
        out_ref[some, 16:32, :] = done[:, half:].reshape(group, 16, half)
        return 0

    lax.fori_loop(0, count // group, step, 0)
    tail = rows_ref[:, 32:40, :].reshape(count * 8, half)
    first = jnp.dot(tail, up_ref[:half, :], preferred_element_type=f32)
    second = jnp.dot(tail, up_ref[half:, :], preferred_element_type=f32)
    turned = count * 8 - 4
    gate_up = first + pltpu.roll(second, turned, 0)
    done = jnp.dot(hidden_of(gate_up), down_ref[...], preferred_element_type=f32)
    upper = lax.broadcasted_iota(jnp.int32, (count * 8, half), 0) % 8 < 4
    packed = jnp.where(upper, done[:, :half], pltpu.roll(done[:, half:], 4, 0)).astype(bf16)
    out_ref[:, 32:40, :] = packed.reshape(count, 8, half)


def run_expert(rows, up, down):
    return pl.pallas_call(
        expert_kernel,
        out_shape=jax.ShapeDtypeStruct(rows.shape, bf16),
        in_specs=[VMEM] * 3,
        out_specs=VMEM,
        compiler_params=pltpu.CompilerParams(vmem_limit_bytes=GRANT),
        name="expert",
    )(rows, up, down)


def combine_kernel(hidden_ref, back_ref, share_ref, out_ref):
    rows = hidden_ref.shape[0]
    half = back_ref.shape[1]
    routed = jnp.dot(share_ref[...], back_ref[...], preferred_element_type=f32)
    out_ref[:, :half] = hidden_ref[:, :half] + routed[:rows]
    out_ref[:, half:] = hidden_ref[:, half:] + routed[rows:]


def run_combine(hidden, back, share):
    return pl.pallas_call(
        combine_kernel,
        out_shape=jax.ShapeDtypeStruct(hidden.shape, f32),
        in_specs=[VMEM] * 3,
        out_specs=VMEM,
        compiler_params=pltpu.CompilerParams(vmem_limit_bytes=GRANT),
        name="combine",
    )(hidden, back, share)


def turned(size, distance):
    return [(i, (i + distance) % size) for i in range(size)]


def slot_rows(ids, experts):
    rows = ids.shape[0]
    choice = ids[:, :, None] == jnp.arange(experts, dtype=jnp.int32)
    named = jnp.any(choice, axis=1).astype(bf16)
    before = jnp.tril(jnp.ones((rows, rows), bf16), -1)
    ranks = jnp.dot(before, named, preferred_element_type=f32)
    slots = jnp.sum(jnp.where(choice, ranks[:, None, :], 0.0), axis=2).astype(jnp.int32)
    early = slots < 16
    left = ids * 40 + jnp.where(early, slots, slots + 16)
    right = ids * 40 + jnp.where(early, slots + 16, slots + 20)
    return jnp.concatenate([left, right], axis=0)


def body(
    tokens,
    input_gain,
    mixer_weight,
    rate_weight,
    conv_kernel,
    decay_scale,
    decay_bias,
    value_gain,
    output_weight,
    start_state,
    post_gain,
    expert_gateup,
    expert_down,
    route_ids,
    route_weights,
):
    own = tokens[0]
    model_width = own.shape[1]
    experts = lax.axis_size(EXP)
    normed = run_norm(own, input_gain.reshape(1, -1))
    rings = lax.axis_size("y")
    y, core = lax.axis_index("y"), lax.axis_index("core")
    up, down, swap = turned(rings, 1), turned(rings, -1), [(0, 1), (1, 0)]
    below = lax.ppermute(normed, "y", up)
    above = lax.ppermute(normed, "y", down)
    beside = lax.ppermute(normed, "core", swap)
    rate = jnp.concatenate(
        [rate_weight.reshape(model_width, -1), jnp.zeros((model_width, 128 - 2 * HEADS), bf16)], axis=1
    )
    places = slot_rows(route_ids[0], experts)
    count = experts * 40
    hits = places[:, :, None] == jnp.arange(count, dtype=jnp.int32)
    pick = jnp.any(
        places.T[:, None, :] == jnp.arange(count, dtype=jnp.int32)[None, :, None], axis=0
    ).astype(bf16)
    doubled = jnp.concatenate([route_weights[0], route_weights[0]], axis=0)
    share = jnp.sum(jnp.where(hits, doubled[:, :, None], 0.0), axis=1)
    share = share.astype(bf16)
    room = 128 - 2 * HEADS
    rate_par = jnp.stack(
        [
            jnp.concatenate([jnp.zeros(HEADS, f32), decay_bias, jnp.zeros(room, f32)]),
            jnp.concatenate([jnp.zeros(HEADS, f32), decay_scale, jnp.zeros(room, f32)]),
        ]
    )
    place = jnp.stack([lax.axis_index("x"), y, lax.axis_index("z"), core]).astype(jnp.int32)
    low_half, high_half, flanks = run_cut(below, above)
    low_half, high_half, flanks, beside, rate, rate_par, conv, place, pick, share = lax.optimization_barrier(
        (low_half, high_half, flanks, beside, rate, rate_par, conv_kernel[:, 0], place, pick, share)
    )
    far_low = lax.ppermute(low_half, "y", up)
    far_high = lax.ppermute(high_half, "y", down)
    flanks = lax.ppermute(flanks, "core", swap)
    early, early_rate = run_project([normed, beside, below, above], mixer_weight, rate)
    far_low, far_high, flanks, early = lax.optimization_barrier((far_low, far_high, flanks, early))
    far = lax.ppermute(run_join(far_low, far_high), "core", swap)
    late, late_rate = run_project([flanks, far_low, far_high, far], mixer_weight, rate)
    closing = run_closing(place, [normed, beside, below, above, flanks, flanks, far_high, far])
    halo = lax.ppermute(closing, EXP, [(i, i + 1) for i in range(experts - 1)])
    gate, reader, local, summary, packed = run_delta(
        place, early, early_rate, late, late_rate, halo, mixer_weight, conv, rate_par
    )
    depth = lax.axis_size("z")
    other = lax.ppermute(packed, "z", [(i, i ^ 1) for i in range(depth)])
    both = run_couple(place, packed, other)
    pairs = [lax.ppermute(both, "z", turned(depth, 2 * step)) for step in (1, 2, 3)]
    prefix, total = run_row(place, both, *pairs, other)
    rows = [lax.ppermute(total, "x", turned(lax.axis_size("x"), step)) for step in (1, 2, 3)]
    gain = value_gain.reshape(1, -1)
    given, final_state, entering = run_give(
        place, rows, start_state, prefix, summary, reader, local, gate,
        gain, output_weight,
    )
    got = lax.ppermute(given, "core", swap)
    kept = run_keep(place, entering, reader, local, gate, gain, output_weight)
    crossed = [(2 * i + c, (i + 1 - 2 * c) % rings * 2 + c) for i in range(rings) for c in (0, 1)]
    uncrossed = [(to, source) for source, to in crossed]
    near, to_up, to_down, far_up, far_down, first, second = run_split(place, kept, got)
    from_below = lax.ppermute(far_up, "y", up)
    from_above = lax.ppermute(far_down, "y", down)
    first = lax.ppermute(first, CTX, crossed)
    second = lax.ppermute(second, CTX, uncrossed)
    send_up, send_down = run_pass(to_up, to_down, from_below, from_above)
    mixed_below = lax.ppermute(send_up, "y", up)
    mixed_above = lax.ppermute(send_down, "y", down)
    hidden, outgoing = run_dispatch(
        place, own, near, mixed_below, mixed_above, first, second, post_gain.reshape(1, -1), pick
    )
    width = model_width // 2
    arrived = lax.all_to_all(outgoing.reshape(experts, 40, width), EXP, 0, 0, tiled=True)
    made = run_expert(arrived, expert_gateup[0], expert_down[0])
    back = lax.all_to_all(made, EXP, 0, 0, tiled=True)
    layer_out = run_combine(hidden, back.reshape(count, width), share)
    return (layer_out[None], final_state[None])


def solution(mesh):
    fine = Mesh(mesh.devices.reshape(4, 2, 4, 8), CTX + EXP)
    in_specs = (
        P(EXP, CTX, None),
        P(),
        P(None, CTX),
        P(None, CTX, None),
        P(None, CTX, None),
        P(CTX),
        P(CTX),
        P(),
        P(CTX, None),
        P(CTX, None, None),
        P(),
        P(EXP, None, None),
        P(EXP, None, None),
        P(EXP, CTX, None),
        P(EXP, CTX, None),
    )
    out_specs = (P(EXP, CTX, None), P(EXP, CTX, None, None))
    return jax.shard_map(body, mesh=fine, in_specs=in_specs, out_specs=out_specs, check_vma=False)
```

```python
import functools

import jax
import jax.numpy as jnp
from jax import lax
from jax.experimental import pallas as pl
from jax.experimental.pallas import tpu as pltpu
from jax.sharding import Mesh
from jax.sharding import PartitionSpec as P

DK = 128
DV = 128
FFE = 512
HEADS = 2
ROUTES = 4
CHUNK = 128
EPSILON = 1e-06
CTX = ("y", "core")
EXP = ("x", "z")
bf16 = jnp.bfloat16
f32 = jnp.float32
highest = lax.Precision.HIGHEST
VMEM = pl.BlockSpec(memory_space=pltpu.VMEM)
SMEM = pl.BlockSpec(memory_space=pltpu.SMEM)
GRANT = 24 * 1024 * 1024


def mm(a, b):
    return jnp.dot(a.astype(bf16), b.astype(bf16), preferred_element_type=f32)


def mm_t(a, b):
    return lax.dot_general(
        a.astype(bf16), b.astype(bf16), (((1,), (1,)), ((), ())), preferred_element_type=f32
    )


def rms_scale(values, scaling):
    widened = values.astype(f32)
    return (
        widened * lax.rsqrt(jnp.mean(widened * widened, axis=-1, keepdims=True) + EPSILON) * scaling
    )


def unit_rows(values):
    return values * lax.rsqrt(jnp.sum(values * values, axis=-1, keepdims=True) + EPSILON)


def silu(values):
    return values / (1.0 + jnp.exp(-values))


def square_iota(size, axis):
    return lax.broadcasted_iota(jnp.int32, (size, size), axis)


def norm_kernel(own_ref, gain_ref, out_ref):
    out_ref[...] = rms_scale(own_ref[...], gain_ref[...]).astype(bf16)


def run_norm(own, gain):
    return pl.pallas_call(
        norm_kernel,
        out_shape=jax.ShapeDtypeStruct(own.shape, bf16),
        in_specs=[VMEM] * 2,
        out_specs=VMEM,
        compiler_params=pltpu.CompilerParams(vmem_limit_bytes=8 * 1024 * 1024),
        name="norm",
    )(own, gain)


ORDER = ((0, 0), (0, 1), (3, 0), (1, 0), (3, 1), (1, 1), (2, 0), (2, 1))
CLOSING = (112, 112, 112, 112, 112, 240, 48, 112)


def block_of(y, core, i):
    step, side = ORDER[i]
    return (y + step) % 4 * 2 + (core + side) % 2


ANY = pl.BlockSpec(memory_space=pl.ANY)


def cut_kernel(below_ref, above_ref, low_ref, high_ref, both_ref, sems):
    rows = below_ref.shape[0]
    half = rows // 2
    copies = [
        pltpu.make_async_copy(below_ref.at[pl.ds(0, half)], low_ref, sems.at[0]),
        pltpu.make_async_copy(above_ref.at[pl.ds(half, half)], high_ref, sems.at[1]),
        pltpu.make_async_copy(below_ref, both_ref.at[pl.ds(0, rows)], sems.at[2]),
        pltpu.make_async_copy(above_ref, both_ref.at[pl.ds(rows, rows)], sems.at[3]),
    ]
    for copy in copies:
        copy.start()
    for copy in copies:
        copy.wait()


def run_cut(below, above):
    rows, width = below.shape
    return pl.pallas_call(
        cut_kernel,
        out_shape=(
            jax.ShapeDtypeStruct((rows // 2, width), bf16),
            jax.ShapeDtypeStruct((rows // 2, width), bf16),
            jax.ShapeDtypeStruct((2 * rows, width), bf16),
        ),
        in_specs=[ANY] * 2,
        out_specs=(ANY,) * 3,
        scratch_shapes=[pltpu.SemaphoreType.DMA((4,))],
        compiler_params=pltpu.CompilerParams(vmem_limit_bytes=4 * 1024 * 1024),
        name="cut",
    )(below, above)


def join_kernel(first_ref, second_ref, both_ref, sems):
    rows = first_ref.shape[0]
    copies = [
        pltpu.make_async_copy(first_ref, both_ref.at[pl.ds(0, rows)], sems.at[0]),
        pltpu.make_async_copy(second_ref, both_ref.at[pl.ds(rows, rows)], sems.at[1]),
    ]
    for copy in copies:
        copy.start()
    for copy in copies:
        copy.wait()


def run_join(first, second):
    rows, width = first.shape
    return pl.pallas_call(
        join_kernel,
        out_shape=jax.ShapeDtypeStruct((2 * rows, width), bf16),
        in_specs=[ANY] * 2,
        out_specs=ANY,
        scratch_shapes=[pltpu.SemaphoreType.DMA((2,))],
        compiler_params=pltpu.CompilerParams(vmem_limit_bytes=4 * 1024 * 1024),
        name="join",
    )(first, second)


def closing_kernel(place_ref, *refs):
    ends, out_ref, sem = refs[:-2], refs[-2], refs[-1]
    for i, (ref, at) in enumerate(zip(ends, CLOSING)):

        @pl.when(block_of(place_ref[1], place_ref[3], i) == len(ORDER) - 1)
        def _(ref=ref, at=at):
            copy = pltpu.make_async_copy(ref.at[pl.ds(at, 16)], out_ref, sem)
            copy.start()
            copy.wait()


def run_closing(place, ends):
    return pl.pallas_call(
        closing_kernel,
        out_shape=jax.ShapeDtypeStruct((16, ends[0].shape[1]), bf16),
        in_specs=[SMEM] + [ANY] * len(ends),
        out_specs=ANY,
        scratch_shapes=[pltpu.SemaphoreType.DMA],
        compiler_params=pltpu.CompilerParams(vmem_limit_bytes=4 * 1024 * 1024),
        name="closing",
    )(place, *ends)


def project_kernel(count, *refs):
    weight_ref, rate_ref, made_ref, rates_ref, rows_scr, sems = refs[count:]
    copies, at = [], 0
    for i, ref in enumerate(refs[:count]):
        copies.append(pltpu.make_async_copy(ref, rows_scr.at[pl.ds(at, ref.shape[0])], sems.at[i]))
        copies[i].start()
        at += ref.shape[0]
    for copy in copies:
        copy.wait()
    rows = rows_scr[...]
    made_ref[...] = jnp.dot(rows, weight_ref[...], preferred_element_type=f32).astype(bf16)
    rates_ref[...] = jnp.dot(rows, rate_ref[...], preferred_element_type=f32).astype(bf16)


def run_project(blocks, weight, rate):
    rows = sum(block.shape[0] for block in blocks)
    return pl.pallas_call(
        functools.partial(project_kernel, len(blocks)),
        out_shape=(
            jax.ShapeDtypeStruct((rows, weight.shape[1]), bf16),
            jax.ShapeDtypeStruct((rows, rate.shape[1]), bf16),
        ),
        in_specs=[ANY] * len(blocks) + [VMEM] * 2,
        out_specs=(VMEM, VMEM),
        scratch_shapes=[
            pltpu.VMEM((rows, weight.shape[0]), bf16),
            pltpu.SemaphoreType.DMA((len(blocks),)),
        ],
        compiler_params=pltpu.CompilerParams(vmem_limit_bytes=14 * 1024 * 1024),
        cost_estimate=pl.CostEstimate(
            flops=2 * rows * weight.size, bytes_accessed=8 * 10**6, transcendentals=0
        ),
        name="project",
    )(*blocks, weight, rate)


def delta_kernel(
    place_ref, early_ref, early_rate_ref, late_ref, late_rate_ref, halo_ref, weight_ref, conv_ref, rate_par_ref,
    gate_ref, reader_ref, local_ref, summary_ref, packed_ref,
    rows_scr, rate_scr,
):
    seg_rows = gate_ref.shape[0]
    width = conv_ref.shape[1]
    steps = seg_rows // CHUNK
    halo = jnp.dot(halo_ref[...], weight_ref[:, :width], preferred_element_type=f32)
    rows_scr[0:8, :] = halo[8:16].astype(bf16).astype(f32)
    for i in range(steps):
        made_ref, made_rate_ref = (
            (early_ref, early_rate_ref) if 2 * i < steps else (late_ref, late_rate_ref)
        )
        at = i % (steps // 2) * CHUNK
        to = pl.multiple_of(block_of(place_ref[1], place_ref[3], i) * CHUNK, CHUNK)
        rows_scr[pl.ds(pl.multiple_of(to + 8, 8), CHUNK), :] = made_ref[at : at + CHUNK, :width].astype(f32)
        gate_ref[pl.ds(to, CHUNK), :] = made_ref[at : at + CHUNK, width:]
        rate_scr[pl.ds(to, CHUNK), :] = made_rate_ref[at : at + CHUNK, :].astype(f32)

    row = square_iota(CHUNK, 0)
    col = square_iota(CHUNK, 1)
    lower = (row >= col).astype(f32)
    eye = (row == col).astype(f32)
    for h in range(HEADS):
        summary_ref[h, :, :DK] = eye
        summary_ref[h, :, DK:] = jnp.zeros((DK, DV), f32)

    pair = 8

    def chunk_step(i, _):
        units = []
        for u in range(pair):
            at = pl.multiple_of((i * pair + u) * CHUNK, CHUNK)
            window = rows_scr[pl.ds(at, CHUNK + 8), :]
            summed = conv_ref[0:1, :] * window[5 : 5 + CHUNK]
            for tap in range(1, 4):
                summed = summed + conv_ref[tap : tap + 1, :] * window[5 + tap : 5 + tap + CHUNK]
            active = silu(summed)
            query = unit_rows(active[:, :DK]) * DK ** (-0.5)
            key = unit_rows(active[:, DK : 2 * DK])
            rate = rate_scr[pl.ds(at, CHUNK), :]
            shifted = rate + rate_par_ref[0:1, :]
            soft = jnp.maximum(shifted, 0.0) + jnp.log1p(jnp.exp(-jnp.abs(shifted)))
            decay = -rate_par_ref[1:2, :] * soft
            beta_all = 1.0 / (1.0 + jnp.exp(-rate))
            total = jnp.dot(lower, decay, preferred_element_type=f32, precision=highest)
            total_t = total.T
            key_low = key.astype(bf16)
            gram = mm_t(key_low, key_low)
            raw_scores = mm_t(query, key_low)
            for h in range(HEADS):
                cum = total[:, HEADS + h : HEADS + h + 1]
                cum_row = total_t[HEADS + h : HEADS + h + 1, :]
                beta = beta_all[:, h : h + 1]
                causal = jnp.exp(jnp.where(row >= col, cum - cum_row, -1e30))
                grown = jnp.exp(cum)
                last = cum[CHUNK - 1 : CHUNK, :]
                value = active[:, 2 * DK + h * DV : 2 * DK + (h + 1) * DV]
                units.append(
                    dict(
                        at=at,
                        h=h,
                        low=jnp.where(row > col, beta * gram * causal, 0.0),
                        right=jnp.concatenate([beta * key * grown, beta * value], axis=1).astype(bf16),
                        scores=(raw_scores * causal).astype(bf16),
                        read=(query * grown).astype(bf16),
                        faded=(key * jnp.exp(last - cum)).T.astype(bf16),
                        fade=jnp.exp(last),
                    )
                )
        inverses = [
            eye - jnp.where((row // 2 == col // 2), unit["low"], 0.0) for unit in units
        ]
        size = 2
        while size < CHUNK:
            off = (row // (2 * size) == col // (2 * size)) & (row // size != col // size)
            lows = [x.astype(bf16) for x in inverses]
            firsts = [mm(jnp.where(off, unit["low"], 0.0), x) for unit, x in zip(units, lows)]
            inverses = [x - mm(x_low, y) for x, x_low, y in zip(inverses, lows, firsts)]
            size *= 2
        solved = [mm(x, unit["right"]) for unit, x in zip(units, inverses)]
        for unit, done in zip(units, solved):
            h = unit["h"]
            state = summary_ref[h]
            stacked = jnp.concatenate([done[:, :DK].astype(bf16), unit["read"]], axis=0)
            applied = mm(stacked, state)
            fresh = jnp.concatenate([-applied[:CHUNK, :DK], done[:, DK:] - applied[:CHUNK, DK:]], axis=1)
            fresh = fresh.astype(bf16)
            out = applied[CHUNK:] + mm(unit["scores"], fresh)
            summary_ref[h] = unit["fade"] * state + mm(unit["faded"], fresh)
            reader_ref[h, pl.ds(unit["at"], CHUNK), :] = out[:, :DK].astype(bf16)
            local_ref[h, pl.ds(unit["at"], CHUNK), :] = out[:, DK:]
        return 0

    lax.fori_loop(0, steps // pair, chunk_step, 0)
    for h in range(HEADS):
        change = summary_ref[h, :, :DK] - eye
        summary_ref[h, :, :DK] = change
        packed_ref[h, :, :DK] = change.astype(bf16)
        packed_ref[h, :, DK:] = summary_ref[h, :, DK:].astype(bf16)


def run_delta(place, early, early_rate, late, late_rate, halo, weight, conv, rate_par):
    rows = 2 * early.shape[0]
    return pl.pallas_call(
        delta_kernel,
        out_shape=(
            jax.ShapeDtypeStruct((rows, HEADS * DV), bf16),
            jax.ShapeDtypeStruct((HEADS, rows, DK), bf16),
            jax.ShapeDtypeStruct((HEADS, rows, DV), f32),
            jax.ShapeDtypeStruct((HEADS, DK, DK + DV), f32),
            jax.ShapeDtypeStruct((HEADS, DK, DK + DV), bf16),
        ),
        in_specs=[SMEM] + [VMEM] * 8,
        out_specs=(VMEM,) * 5,
        scratch_shapes=[
            pltpu.VMEM((rows + 8, conv.shape[1]), f32),
            pltpu.VMEM((rows, 128), f32),
        ],
        compiler_params=pltpu.CompilerParams(vmem_limit_bytes=GRANT),
        name="delta",
    )(place, early, early_rate, late, late_rate, halo, weight, conv, rate_par)


def then(first, second):
    return first + mm(second[:, :DK], first) + second.astype(f32)


def apply(change, state):
    return state + mm(change[:, :DK], state) + change[:, DK:].astype(f32)


def couple_kernel(place_ref, own_ref, other_ref, both_ref):
    odd = place_ref[2] % 2 == 1
    for h in range(HEADS):
        own = own_ref[h].astype(f32)
        other = other_ref[h].astype(f32)
        both_ref[h] = then(jnp.where(odd, other, own), jnp.where(odd, own, other)).astype(bf16)


def run_couple(place, own, other):
    return pl.pallas_call(
        couple_kernel,
        out_shape=jax.ShapeDtypeStruct(own.shape, bf16),
        in_specs=[SMEM, VMEM, VMEM],
        out_specs=VMEM,
        compiler_params=pltpu.CompilerParams(vmem_limit_bytes=8 * 1024 * 1024),
        name="couple",
    )(place, own, other)


def row_kernel(place_ref, own_ref, back1_ref, back2_ref, back3_ref, other_ref, prefix_ref, total_ref, all_scr):
    odd = place_ref[2] % 2 == 1
    place = place_ref[2] // 2
    for offset, ref in enumerate((own_ref, back1_ref, back2_ref, back3_ref)):
        all_scr[(place + 4 - offset) % 4] = ref[...]
    changes = [jnp.zeros((DK, DK + DV), f32) for _ in range(HEADS)]
    for j in range(4):
        for h in range(HEADS):
            change = changes[h]

            @pl.when(place == j)
            def _(change=change, h=h):
                prefix_ref[h] = change

            changes[h] = then(change, all_scr[j, h])
    for h in range(HEADS):
        total_ref[h] = changes[h].astype(bf16)
        before = prefix_ref[h]
        prefix_ref[h] = jnp.where(odd, then(before, other_ref[h]), before)


def run_row(place, own, back1, back2, back3, other):
    return pl.pallas_call(
        row_kernel,
        out_shape=(
            jax.ShapeDtypeStruct(own.shape, f32),
            jax.ShapeDtypeStruct(own.shape, bf16),
        ),
        in_specs=[SMEM] + [VMEM] * 5,
        out_specs=(VMEM, VMEM),
        scratch_shapes=[pltpu.VMEM((4,) + own.shape, bf16)],
        compiler_params=pltpu.CompilerParams(vmem_limit_bytes=8 * 1024 * 1024),
        name="row",
    )(place, own, back1, back2, back3, other)


def mix(y, core, entering, reader_ref, local_ref, gate_ref, gain_ref, weight_ref, out_ref):
    rows = []
    for i in range(out_ref.shape[0] // CHUNK):
        at = pl.ds(pl.multiple_of(((y + i) % 4 * 2 + core) * CHUNK, CHUNK), CHUNK)
        parts = []
        for h in range(HEADS):
            mixed = mm(reader_ref[h, at, :], entering[h]) + local_ref[h, at, :]
            gate = gate_ref[at, h * DV : (h + 1) * DV].astype(f32)
            parts.append((rms_scale(mixed, gain_ref[...]) * silu(gate)).astype(bf16))
        rows.append(jnp.concatenate(parts, axis=1))
    gated = jnp.concatenate(rows, axis=0)
    out_ref[...] = jnp.dot(gated, weight_ref[...], preferred_element_type=f32).astype(bf16)


def give_kernel(
    place_ref, back1_ref, back2_ref, back3_ref, start_ref, prefix_ref, summary_ref, reader_ref, local_ref,
    gate_ref, gain_ref, weight_ref, out_ref, final_ref, entering_ref,
):
    place = place_ref[0]
    entering = []
    for h in range(HEADS):
        state = start_ref[h]
        for offset, ref in ((3, back3_ref), (2, back2_ref), (1, back1_ref)):
            state = jnp.where(place >= offset, apply(ref[h], state), state)
        state = apply(prefix_ref[h], state)
        final_ref[h] = apply(summary_ref[h], state)
        entering.append(state.astype(bf16))
        entering_ref[h] = entering[h]
    mix(place_ref[1], 1 - place_ref[3], entering, reader_ref, local_ref, gate_ref, gain_ref, weight_ref, out_ref)


def run_give(place, backs, start, prefix, summary, reader, local, gate, gain, weight):
    return pl.pallas_call(
        give_kernel,
        out_shape=(
            jax.ShapeDtypeStruct((gate.shape[0] // 2, weight.shape[1]), bf16),
            jax.ShapeDtypeStruct(start.shape, f32),
            jax.ShapeDtypeStruct(start.shape, bf16),
        ),
        in_specs=[SMEM] + [VMEM] * 11,
        out_specs=(VMEM,) * 3,
        compiler_params=pltpu.CompilerParams(vmem_limit_bytes=GRANT),
        name="give",
    )(place, *backs, start, prefix, summary, reader, local, gate, gain, weight)


def keep_kernel(place_ref, entering_ref, reader_ref, local_ref, gate_ref, gain_ref, weight_ref, out_ref):
    entering = [entering_ref[h] for h in range(HEADS)]
    mix(place_ref[1], place_ref[3], entering, reader_ref, local_ref, gate_ref, gain_ref, weight_ref, out_ref)


def run_keep(place, entering, reader, local, gate, gain, weight):
    rows = gate.shape[0] // 2
    return pl.pallas_call(
        keep_kernel,
        out_shape=jax.ShapeDtypeStruct((rows, weight.shape[1]), bf16),
        in_specs=[SMEM] + [VMEM] * 6,
        out_specs=VMEM,
        compiler_params=pltpu.CompilerParams(vmem_limit_bytes=GRANT),
        cost_estimate=pl.CostEstimate(
            flops=2 * rows * weight.size, bytes_accessed=4 * 10**6, transcendentals=0
        ),
        name="keep",
    )(place, entering, reader, local, gate, gain, weight)


def split_kernel(kept_ref, got_ref, near_ref, up_ref, down_ref, far_up_ref, far_down_ref):
    rows = near_ref.shape[0]

    def summed(at, size):
        return kept_ref[at : at + size, :].astype(f32) + got_ref[at : at + size, :].astype(f32)

    half = rows // 2
    far_up_ref[...] = summed(2 * rows, half).astype(bf16)
    far_down_ref[...] = summed(2 * rows + half, half).astype(bf16)
    near_ref[...] = summed(0, rows)
    up_ref[...] = summed(rows, rows)
    down_ref[...] = summed(3 * rows, rows)


def run_split(kept, got):
    rows = kept.shape[0] // 4
    width = kept.shape[1]
    return pl.pallas_call(
        split_kernel,
        out_shape=(jax.ShapeDtypeStruct((rows, width), f32),) * 3
        + (jax.ShapeDtypeStruct((rows // 2, width), bf16),) * 2,
        in_specs=[VMEM] * 2,
        out_specs=(VMEM,) * 5,
        compiler_params=pltpu.CompilerParams(vmem_limit_bytes=12 * 1024 * 1024),
        name="split",
    )(kept, got)


def pass_kernel(up_ref, down_ref, from_below_ref, from_above_ref, send_up_ref, send_down_ref):
    half = from_below_ref.shape[0]
    send_up_ref[:half, :] = (up_ref[:half, :] + from_below_ref[...].astype(f32)).astype(bf16)
    send_up_ref[half:, :] = up_ref[half:, :].astype(bf16)
    send_down_ref[:half, :] = down_ref[:half, :].astype(bf16)
    send_down_ref[half:, :] = (down_ref[half:, :] + from_above_ref[...].astype(f32)).astype(bf16)


def run_pass(up, down, from_below, from_above):
    return pl.pallas_call(
        pass_kernel,
        out_shape=(jax.ShapeDtypeStruct(up.shape, bf16),) * 2,
        in_specs=[VMEM] * 4,
        out_specs=(VMEM,) * 2,
        compiler_params=pltpu.CompilerParams(vmem_limit_bytes=12 * 1024 * 1024),
        name="pass",
    )(up, down, from_below, from_above)


def dispatch_kernel(own_ref, near_ref, below_ref, above_ref, gain_ref, pick_ref, hidden_ref, out_ref):
    mixed = near_ref[...] + (below_ref[...].astype(f32) + above_ref[...].astype(f32))
    hidden = own_ref[...].astype(f32) + mixed
    hidden_ref[...] = hidden
    post = rms_scale(hidden, gain_ref[...]).astype(bf16)
    half = post.shape[1] // 2
    stacked = jnp.concatenate([post[:, :half], post[:, half:]], axis=0)
    out_ref[...] = jnp.dot(pick_ref[...], stacked, preferred_element_type=f32).astype(bf16)


def run_dispatch(own, near, below, above, gain, pick):
    return pl.pallas_call(
        dispatch_kernel,
        out_shape=(
            jax.ShapeDtypeStruct(own.shape, f32),
            jax.ShapeDtypeStruct((pick.shape[0], own.shape[1] // 2), bf16),
        ),
        in_specs=[VMEM] * 6,
        out_specs=(VMEM, VMEM),
        compiler_params=pltpu.CompilerParams(vmem_limit_bytes=GRANT),
        name="dispatch",
    )(own, near, below, above, gain, pick)


def expert_kernel(rows_ref, up_ref, down_ref, out_ref):
    count, _, half = rows_ref.shape

    def hidden_of(gate_up):
        return (silu(gate_up[:, :FFE]) * gate_up[:, FFE:]).astype(bf16)

    group = 32

    def step(i, _):
        some = pl.ds(i * group, group)
        left = rows_ref[some, 0:16, :].reshape(group * 16, half)
        right = rows_ref[some, 16:32, :].reshape(group * 16, half)
        gate_up = jnp.dot(left, up_ref[:half, :], preferred_element_type=f32) + jnp.dot(
            right, up_ref[half:, :], preferred_element_type=f32
        )
        done = jnp.dot(hidden_of(gate_up), down_ref[...], preferred_element_type=f32).astype(bf16)
        out_ref[some, 0:16, :] = done[:, :half].reshape(group, 16, half)
        out_ref[some, 16:32, :] = done[:, half:].reshape(group, 16, half)
        return 0

    lax.fori_loop(0, count // group, step, 0)
    tail = rows_ref[:, 32:40, :].reshape(count * 8, half)
    first = jnp.dot(tail, up_ref[:half, :], preferred_element_type=f32)
    second = jnp.dot(tail, up_ref[half:, :], preferred_element_type=f32)
    turned = count * 8 - 4
    gate_up = first + pltpu.roll(second, turned, 0)
    done = jnp.dot(hidden_of(gate_up), down_ref[...], preferred_element_type=f32)
    upper = lax.broadcasted_iota(jnp.int32, (count * 8, half), 0) % 8 < 4
    packed = jnp.where(upper, done[:, :half], pltpu.roll(done[:, half:], 4, 0)).astype(bf16)
    out_ref[:, 32:40, :] = packed.reshape(count, 8, half)


def run_expert(rows, up, down):
    return pl.pallas_call(
        expert_kernel,
        out_shape=jax.ShapeDtypeStruct(rows.shape, bf16),
        in_specs=[VMEM] * 3,
        out_specs=VMEM,
        compiler_params=pltpu.CompilerParams(vmem_limit_bytes=GRANT),
        name="expert",
    )(rows, up, down)


def combine_kernel(hidden_ref, back_ref, high_ref, low_ref, out_ref):
    rows = hidden_ref.shape[0]
    half = back_ref.shape[1]
    back = back_ref[...]
    routed = jnp.dot(high_ref[...], back, preferred_element_type=f32) + jnp.dot(
        low_ref[...], back, preferred_element_type=f32
    )
    out_ref[:, :half] = hidden_ref[:, :half] + routed[:rows]
    out_ref[:, half:] = hidden_ref[:, half:] + routed[rows:]


def run_combine(hidden, back, high, low):
    return pl.pallas_call(
        combine_kernel,
        out_shape=jax.ShapeDtypeStruct(hidden.shape, f32),
        in_specs=[VMEM] * 4,
        out_specs=VMEM,
        compiler_params=pltpu.CompilerParams(vmem_limit_bytes=GRANT),
        name="combine",
    )(hidden, back, high, low)


def turned(size, distance):
    return [(i, (i + distance) % size) for i in range(size)]


def slot_rows(ids, experts):
    rows = ids.shape[0]
    choice = ids[:, :, None] == jnp.arange(experts, dtype=jnp.int32)
    named = jnp.any(choice, axis=1).astype(bf16)
    before = jnp.tril(jnp.ones((rows, rows), bf16), -1)
    ranks = jnp.dot(before, named, preferred_element_type=f32)
    slots = jnp.sum(jnp.where(choice, ranks[:, None, :], 0.0), axis=2).astype(jnp.int32)
    early = slots < 16
    left = ids * 40 + jnp.where(early, slots, slots + 16)
    right = ids * 40 + jnp.where(early, slots + 16, slots + 20)
    return jnp.concatenate([left, right], axis=0)


def body(
    tokens,
    input_gain,
    mixer_weight,
    rate_weight,
    conv_kernel,
    decay_scale,
    decay_bias,
    value_gain,
    output_weight,
    start_state,
    post_gain,
    expert_gateup,
    expert_down,
    route_ids,
    route_weights,
):
    own = tokens[0]
    model_width = own.shape[1]
    experts = lax.axis_size(EXP)
    normed = run_norm(own, input_gain.reshape(1, -1))
    rings = lax.axis_size("y")
    y, core = lax.axis_index("y"), lax.axis_index("core")
    up, down, swap = turned(rings, 1), turned(rings, -1), [(0, 1), (1, 0)]
    below = lax.ppermute(normed, "y", up)
    above = lax.ppermute(normed, "y", down)
    beside = lax.ppermute(normed, "core", swap)
    rate = jnp.concatenate(
        [rate_weight.reshape(model_width, -1), jnp.zeros((model_width, 128 - 2 * HEADS), bf16)], axis=1
    )
    places = slot_rows(route_ids[0], experts)
    count = experts * 40
    hits = places[:, :, None] == jnp.arange(count, dtype=jnp.int32)
    pick = jnp.any(
        places.T[:, None, :] == jnp.arange(count, dtype=jnp.int32)[None, :, None], axis=0
    ).astype(bf16)
    doubled = jnp.concatenate([route_weights[0], route_weights[0]], axis=0)
    share = jnp.sum(jnp.where(hits, doubled[:, :, None], 0.0), axis=1)
    high = share.astype(bf16)
    low = (share - high.astype(f32)).astype(bf16)
    room = 128 - 2 * HEADS
    rate_par = jnp.stack(
        [
            jnp.concatenate([jnp.zeros(HEADS, f32), decay_bias, jnp.zeros(room, f32)]),
            jnp.concatenate([jnp.zeros(HEADS, f32), decay_scale, jnp.zeros(room, f32)]),
        ]
    )
    place = jnp.stack([lax.axis_index("x"), y, lax.axis_index("z"), core]).astype(jnp.int32)
    low_half, high_half, flanks = run_cut(below, above)
    low_half, high_half, flanks, beside, rate, rate_par, conv, place, pick, high, low = lax.optimization_barrier(
        (low_half, high_half, flanks, beside, rate, rate_par, conv_kernel[:, 0], place, pick, high, low)
    )
    far_low = lax.ppermute(low_half, "y", up)
    far_high = lax.ppermute(high_half, "y", down)
    flanks = lax.ppermute(flanks, "core", swap)
    early, early_rate = run_project([normed, beside, below, above], mixer_weight, rate)
    far_low, far_high, flanks, early = lax.optimization_barrier((far_low, far_high, flanks, early))
    far = lax.ppermute(run_join(far_low, far_high), "core", swap)
    late, late_rate = run_project([flanks, far_low, far_high, far], mixer_weight, rate)
    closing = run_closing(place, [normed, beside, below, above, flanks, flanks, far_high, far])
    halo = lax.ppermute(closing, EXP, [(i, i + 1) for i in range(experts - 1)])
    gate, reader, local, summary, packed = run_delta(
        place, early, early_rate, late, late_rate, halo, mixer_weight, conv, rate_par
    )
    depth = lax.axis_size("z")
    other = lax.ppermute(packed, "z", [(i, i ^ 1) for i in range(depth)])
    both = run_couple(place, packed, other)
    pairs = [lax.ppermute(both, "z", turned(depth, 2 * step)) for step in (1, 2, 3)]
    prefix, total = run_row(place, both, *pairs, other)
    rows = [lax.ppermute(total, "x", turned(lax.axis_size("x"), step)) for step in (1, 2, 3)]
    gain = value_gain.reshape(1, -1)
    given, final_state, entering = run_give(
        place, rows, start_state, prefix, summary, reader, local, gate,
        gain, output_weight,
    )
    got = lax.ppermute(given, "core", swap)
    kept = run_keep(place, entering, reader, local, gate, gain, output_weight)
    near, to_up, to_down, far_up, far_down = run_split(kept, got)
    from_below = lax.ppermute(far_up, "y", up)
    from_above = lax.ppermute(far_down, "y", down)
    send_up, send_down = run_pass(to_up, to_down, from_below, from_above)
    mixed_below = lax.ppermute(send_up, "y", up)
    mixed_above = lax.ppermute(send_down, "y", down)

    hidden, outgoing = run_dispatch(
        own, near, mixed_below, mixed_above, post_gain.reshape(1, -1), pick
    )
    width = model_width // 2
    arrived = lax.all_to_all(outgoing.reshape(experts, 40, width), EXP, 0, 0, tiled=True)
    made = run_expert(arrived, expert_gateup[0], expert_down[0])
    back = lax.all_to_all(made, EXP, 0, 0, tiled=True)
    layer_out = run_combine(hidden, back.reshape(count, width), high, low)
    return (layer_out[None], final_state[None])


def solution(mesh):
    fine = Mesh(mesh.devices.reshape(4, 2, 4, 8), CTX + EXP)
    in_specs = (
        P(EXP, CTX, None),
        P(),
        P(None, CTX),
        P(None, CTX, None),
        P(None, CTX, None),
        P(CTX),
        P(CTX),
        P(),
        P(CTX, None),
        P(CTX, None, None),
        P(),
        P(EXP, None, None),
        P(EXP, None, None),
        P(EXP, CTX, None),
        P(EXP, CTX, None),
    )
    out_specs = (P(EXP, CTX, None), P(EXP, CTX, None, None))
    return jax.shard_map(body, mesh=fine, in_specs=in_specs, out_specs=out_specs, check_vma=False)
```

```python
import functools

import jax
import jax.numpy as jnp
from jax import lax
from jax.experimental import pallas as pl
from jax.experimental.pallas import tpu as pltpu
from jax.sharding import Mesh
from jax.sharding import PartitionSpec as P

DK = 128
DV = 128
FFE = 512
HEADS = 2
ROUTES = 4
CHUNK = 128
EPSILON = 1e-06
CTX = ("y", "core")
EXP = ("x", "z")
bf16 = jnp.bfloat16
f32 = jnp.float32
highest = lax.Precision.HIGHEST
VMEM = pl.BlockSpec(memory_space=pltpu.VMEM)
SMEM = pl.BlockSpec(memory_space=pltpu.SMEM)
GRANT = 24 * 1024 * 1024


def mm(a, b):
    return jnp.dot(a.astype(bf16), b.astype(bf16), preferred_element_type=f32)


def mm_t(a, b):
    return lax.dot_general(
        a.astype(bf16), b.astype(bf16), (((1,), (1,)), ((), ())), preferred_element_type=f32
    )


def rms_scale(values, scaling):
    widened = values.astype(f32)
    return (
        widened * lax.rsqrt(jnp.mean(widened * widened, axis=-1, keepdims=True) + EPSILON) * scaling
    )


def unit_rows(values):
    return values * lax.rsqrt(jnp.sum(values * values, axis=-1, keepdims=True) + EPSILON)


def silu(values):
    return values / (1.0 + jnp.exp(-values))


def square_iota(size, axis):
    return lax.broadcasted_iota(jnp.int32, (size, size), axis)


def norm_kernel(own_ref, gain_ref, out_ref):
    out_ref[...] = rms_scale(own_ref[...], gain_ref[...]).astype(bf16)


def run_norm(own, gain):
    return pl.pallas_call(
        norm_kernel,
        out_shape=jax.ShapeDtypeStruct(own.shape, bf16),
        in_specs=[VMEM] * 2,
        out_specs=VMEM,
        compiler_params=pltpu.CompilerParams(vmem_limit_bytes=8 * 1024 * 1024),
        name="norm",
    )(own, gain)


ORDER = ((0, 0), (0, 1), (3, 0), (1, 0), (3, 1), (1, 1), (2, 0), (2, 1))
CLOSING = (112, 112, 112, 112, 112, 240, 48, 112)


def block_of(y, core, i):
    step, side = ORDER[i]
    return (y + step) % 4 * 2 + (core + side) % 2


ANY = pl.BlockSpec(memory_space=pl.ANY)


def cut_kernel(below_ref, above_ref, low_ref, high_ref, both_ref, sems):
    rows = below_ref.shape[0]
    half = rows // 2
    copies = [
        pltpu.make_async_copy(below_ref.at[pl.ds(0, half)], low_ref, sems.at[0]),
        pltpu.make_async_copy(above_ref.at[pl.ds(half, half)], high_ref, sems.at[1]),
        pltpu.make_async_copy(below_ref, both_ref.at[pl.ds(0, rows)], sems.at[2]),
        pltpu.make_async_copy(above_ref, both_ref.at[pl.ds(rows, rows)], sems.at[3]),
    ]
    for copy in copies:
        copy.start()
    for copy in copies:
        copy.wait()


def run_cut(below, above):
    rows, width = below.shape
    return pl.pallas_call(
        cut_kernel,
        out_shape=(
            jax.ShapeDtypeStruct((rows // 2, width), bf16),
            jax.ShapeDtypeStruct((rows // 2, width), bf16),
            jax.ShapeDtypeStruct((2 * rows, width), bf16),
        ),
        in_specs=[ANY] * 2,
        out_specs=(ANY,) * 3,
        scratch_shapes=[pltpu.SemaphoreType.DMA((4,))],
        compiler_params=pltpu.CompilerParams(vmem_limit_bytes=4 * 1024 * 1024),
        name="cut",
    )(below, above)


def join_kernel(first_ref, second_ref, both_ref, sems):
    rows = first_ref.shape[0]
    copies = [
        pltpu.make_async_copy(first_ref, both_ref.at[pl.ds(0, rows)], sems.at[0]),
        pltpu.make_async_copy(second_ref, both_ref.at[pl.ds(rows, rows)], sems.at[1]),
    ]
    for copy in copies:
        copy.start()
    for copy in copies:
        copy.wait()


def run_join(first, second):
    rows, width = first.shape
    return pl.pallas_call(
        join_kernel,
        out_shape=jax.ShapeDtypeStruct((2 * rows, width), bf16),
        in_specs=[ANY] * 2,
        out_specs=ANY,
        scratch_shapes=[pltpu.SemaphoreType.DMA((2,))],
        compiler_params=pltpu.CompilerParams(vmem_limit_bytes=4 * 1024 * 1024),
        name="join",
    )(first, second)


def closing_kernel(place_ref, *refs):
    ends, out_ref, sem = refs[:-2], refs[-2], refs[-1]
    for i, (ref, at) in enumerate(zip(ends, CLOSING)):

        @pl.when(block_of(place_ref[1], place_ref[3], i) == len(ORDER) - 1)
        def _(ref=ref, at=at):
            copy = pltpu.make_async_copy(ref.at[pl.ds(at, 16)], out_ref, sem)
            copy.start()
            copy.wait()


def run_closing(place, ends):
    return pl.pallas_call(
        closing_kernel,
        out_shape=jax.ShapeDtypeStruct((16, ends[0].shape[1]), bf16),
        in_specs=[SMEM] + [ANY] * len(ends),
        out_specs=ANY,
        scratch_shapes=[pltpu.SemaphoreType.DMA],
        compiler_params=pltpu.CompilerParams(vmem_limit_bytes=4 * 1024 * 1024),
        name="closing",
    )(place, *ends)


def project_kernel(count, *refs):
    weight_ref, rate_ref, made_ref, rates_ref, rows_scr, sems = refs[count:]
    copies, at = [], 0
    for i, ref in enumerate(refs[:count]):
        copies.append(pltpu.make_async_copy(ref, rows_scr.at[pl.ds(at, ref.shape[0])], sems.at[i]))
        copies[i].start()
        at += ref.shape[0]
    for copy in copies:
        copy.wait()
    rows = rows_scr[...]
    made_ref[...] = jnp.dot(rows, weight_ref[...], preferred_element_type=f32).astype(bf16)
    rates_ref[...] = jnp.dot(rows, rate_ref[...], preferred_element_type=f32).astype(bf16)


def run_project(blocks, weight, rate):
    rows = sum(block.shape[0] for block in blocks)
    return pl.pallas_call(
        functools.partial(project_kernel, len(blocks)),
        out_shape=(
            jax.ShapeDtypeStruct((rows, weight.shape[1]), bf16),
            jax.ShapeDtypeStruct((rows, rate.shape[1]), bf16),
        ),
        in_specs=[ANY] * len(blocks) + [VMEM] * 2,
        out_specs=(VMEM, VMEM),
        scratch_shapes=[
            pltpu.VMEM((rows, weight.shape[0]), bf16),
            pltpu.SemaphoreType.DMA((len(blocks),)),
        ],
        compiler_params=pltpu.CompilerParams(vmem_limit_bytes=14 * 1024 * 1024),
        cost_estimate=pl.CostEstimate(
            flops=2 * rows * weight.size, bytes_accessed=8 * 10**6, transcendentals=0
        ),
        name="project",
    )(*blocks, weight, rate)


def delta_kernel(
    place_ref, early_ref, early_rate_ref, late_ref, late_rate_ref, halo_ref, weight_ref, conv_ref, rate_par_ref,
    gate_ref, reader_ref, local_ref, summary_ref, packed_ref,
    rows_scr, rate_scr,
):
    seg_rows = gate_ref.shape[0]
    width = conv_ref.shape[1]
    steps = seg_rows // CHUNK
    halo = jnp.dot(halo_ref[...], weight_ref[:, :width], preferred_element_type=f32)
    rows_scr[0:8, :] = halo[8:16].astype(bf16).astype(f32)
    for i in range(steps):
        made_ref, made_rate_ref = (
            (early_ref, early_rate_ref) if 2 * i < steps else (late_ref, late_rate_ref)
        )
        at = i % (steps // 2) * CHUNK
        to = pl.multiple_of(block_of(place_ref[1], place_ref[3], i) * CHUNK, CHUNK)
        rows_scr[pl.ds(pl.multiple_of(to + 8, 8), CHUNK), :] = made_ref[at : at + CHUNK, :width].astype(f32)
        gate_ref[pl.ds(to, CHUNK), :] = made_ref[at : at + CHUNK, width:]
        rate_scr[pl.ds(to, CHUNK), :] = made_rate_ref[at : at + CHUNK, :].astype(f32)

    row = square_iota(CHUNK, 0)
    col = square_iota(CHUNK, 1)
    lower = (row >= col).astype(f32)
    eye = (row == col).astype(f32)
    for h in range(HEADS):
        summary_ref[h, :, :DK] = eye
        summary_ref[h, :, DK:] = jnp.zeros((DK, DV), f32)

    pair = 8

    def chunk_step(i, _):
        units = []
        for u in range(pair):
            at = pl.multiple_of((i * pair + u) * CHUNK, CHUNK)
            window = rows_scr[pl.ds(at, CHUNK + 8), :]
            summed = conv_ref[0:1, :] * window[5 : 5 + CHUNK]
            for tap in range(1, 4):
                summed = summed + conv_ref[tap : tap + 1, :] * window[5 + tap : 5 + tap + CHUNK]
            active = silu(summed)
            query = unit_rows(active[:, :DK]) * DK ** (-0.5)
            key = unit_rows(active[:, DK : 2 * DK])
            rate = rate_scr[pl.ds(at, CHUNK), :]
            shifted = rate + rate_par_ref[0:1, :]
            soft = jnp.maximum(shifted, 0.0) + jnp.log1p(jnp.exp(-jnp.abs(shifted)))
            decay = -rate_par_ref[1:2, :] * soft
            beta_all = 1.0 / (1.0 + jnp.exp(-rate))
            total = jnp.dot(lower, decay, preferred_element_type=f32, precision=highest)
            total_t = total.T
            key_low = key.astype(bf16)
            gram = mm_t(key_low, key_low)
            raw_scores = mm_t(query, key_low)
            for h in range(HEADS):
                cum = total[:, HEADS + h : HEADS + h + 1]
                cum_row = total_t[HEADS + h : HEADS + h + 1, :]
                beta = beta_all[:, h : h + 1]
                causal = jnp.exp(jnp.where(row >= col, cum - cum_row, -1e30))
                grown = jnp.exp(cum)
                last = cum[CHUNK - 1 : CHUNK, :]
                value = active[:, 2 * DK + h * DV : 2 * DK + (h + 1) * DV]
                units.append(
                    dict(
                        at=at,
                        h=h,
                        low=jnp.where(row > col, beta * gram * causal, 0.0),
                        right=jnp.concatenate([beta * key * grown, beta * value], axis=1).astype(bf16),
                        scores=(raw_scores * causal).astype(bf16),
                        read=(query * grown).astype(bf16),
                        faded=(key * jnp.exp(last - cum)).T.astype(bf16),
                        fade=jnp.exp(last),
                    )
                )
        inverses = [
            eye - jnp.where((row // 2 == col // 2), unit["low"], 0.0) for unit in units
        ]
        size = 2
        while size < CHUNK:
            off = (row // (2 * size) == col // (2 * size)) & (row // size != col // size)
            lows = [x.astype(bf16) for x in inverses]
            firsts = [mm(jnp.where(off, unit["low"], 0.0), x) for unit, x in zip(units, lows)]
            inverses = [x - mm(x_low, y) for x, x_low, y in zip(inverses, lows, firsts)]
            size *= 2
        solved = [mm(x, unit["right"]) for unit, x in zip(units, inverses)]
        for unit, done in zip(units, solved):
            h = unit["h"]
            state = summary_ref[h]
            stacked = jnp.concatenate([done[:, :DK].astype(bf16), unit["read"]], axis=0)
            applied = mm(stacked, state)
            fresh = jnp.concatenate([-applied[:CHUNK, :DK], done[:, DK:] - applied[:CHUNK, DK:]], axis=1)
            fresh = fresh.astype(bf16)
            out = applied[CHUNK:] + mm(unit["scores"], fresh)
            summary_ref[h] = unit["fade"] * state + mm(unit["faded"], fresh)
            reader_ref[h, pl.ds(unit["at"], CHUNK), :] = out[:, :DK].astype(bf16)
            local_ref[h, pl.ds(unit["at"], CHUNK), :] = out[:, DK:]
        return 0

    lax.fori_loop(0, steps // pair, chunk_step, 0)
    for h in range(HEADS):
        change = summary_ref[h, :, :DK] - eye
        summary_ref[h, :, :DK] = change
        packed_ref[h, :, :DK] = change.astype(bf16)
        packed_ref[h, :, DK:] = summary_ref[h, :, DK:].astype(bf16)


def run_delta(place, early, early_rate, late, late_rate, halo, weight, conv, rate_par):
    rows = 2 * early.shape[0]
    return pl.pallas_call(
        delta_kernel,
        out_shape=(
            jax.ShapeDtypeStruct((rows, HEADS * DV), bf16),
            jax.ShapeDtypeStruct((HEADS, rows, DK), bf16),
            jax.ShapeDtypeStruct((HEADS, rows, DV), f32),
            jax.ShapeDtypeStruct((HEADS, DK, DK + DV), f32),
            jax.ShapeDtypeStruct((HEADS, DK, DK + DV), bf16),
        ),
        in_specs=[SMEM] + [VMEM] * 8,
        out_specs=(VMEM,) * 5,
        scratch_shapes=[
            pltpu.VMEM((rows + 8, conv.shape[1]), f32),
            pltpu.VMEM((rows, 128), f32),
        ],
        compiler_params=pltpu.CompilerParams(vmem_limit_bytes=GRANT),
        name="delta",
    )(place, early, early_rate, late, late_rate, halo, weight, conv, rate_par)


def then(first, second):
    return first + mm(second[:, :DK], first) + second.astype(f32)


def apply(change, state):
    return state + mm(change[:, :DK], state) + change[:, DK:].astype(f32)


def couple_kernel(place_ref, own_ref, other_ref, both_ref):
    odd = place_ref[2] % 2 == 1
    for h in range(HEADS):
        own = own_ref[h].astype(f32)
        other = other_ref[h].astype(f32)
        both_ref[h] = then(jnp.where(odd, other, own), jnp.where(odd, own, other)).astype(bf16)


def run_couple(place, own, other):
    return pl.pallas_call(
        couple_kernel,
        out_shape=jax.ShapeDtypeStruct(own.shape, bf16),
        in_specs=[SMEM, VMEM, VMEM],
        out_specs=VMEM,
        compiler_params=pltpu.CompilerParams(vmem_limit_bytes=8 * 1024 * 1024),
        name="couple",
    )(place, own, other)


def row_kernel(place_ref, own_ref, back1_ref, back2_ref, back3_ref, other_ref, prefix_ref, total_ref, all_scr):
    odd = place_ref[2] % 2 == 1
    place = place_ref[2] // 2
    for offset, ref in enumerate((own_ref, back1_ref, back2_ref, back3_ref)):
        all_scr[(place + 4 - offset) % 4] = ref[...]
    changes = [jnp.zeros((DK, DK + DV), f32) for _ in range(HEADS)]
    for j in range(4):
        for h in range(HEADS):
            change = changes[h]

            @pl.when(place == j)
            def _(change=change, h=h):
                prefix_ref[h] = change

            changes[h] = then(change, all_scr[j, h])
    for h in range(HEADS):
        total_ref[h] = changes[h].astype(bf16)
        before = prefix_ref[h]
        prefix_ref[h] = jnp.where(odd, then(before, other_ref[h]), before)


def run_row(place, own, back1, back2, back3, other):
    return pl.pallas_call(
        row_kernel,
        out_shape=(
            jax.ShapeDtypeStruct(own.shape, f32),
            jax.ShapeDtypeStruct(own.shape, bf16),
        ),
        in_specs=[SMEM] + [VMEM] * 5,
        out_specs=(VMEM, VMEM),
        scratch_shapes=[pltpu.VMEM((4,) + own.shape, bf16)],
        compiler_params=pltpu.CompilerParams(vmem_limit_bytes=8 * 1024 * 1024),
        name="row",
    )(place, own, back1, back2, back3, other)


def mix(y, core, entering, reader_ref, local_ref, gate_ref, gain_ref, weight_ref, out_refs):
    rows = []
    for i in range(4):
        at = pl.ds(pl.multiple_of(((y + i) % 4 * 2 + core) * CHUNK, CHUNK), CHUNK)
        parts = []
        for h in range(HEADS):
            mixed = mm(reader_ref[h, at, :], entering[h]) + local_ref[h, at, :]
            gate = gate_ref[at, h * DV : (h + 1) * DV].astype(f32)
            parts.append((rms_scale(mixed, gain_ref[...]) * silu(gate)).astype(bf16))
        rows.append(jnp.concatenate(parts, axis=1))
    gated = jnp.concatenate(rows, axis=0)
    made = jnp.dot(gated, weight_ref[...], preferred_element_type=f32).astype(bf16)
    far_ref, rest_ref = out_refs
    far_ref[...] = made[2 * CHUNK : 3 * CHUNK]
    rest_ref[: 2 * CHUNK, :] = made[: 2 * CHUNK]
    rest_ref[2 * CHUNK :, :] = made[3 * CHUNK :]


def give_kernel(
    place_ref, back1_ref, back2_ref, back3_ref, start_ref, prefix_ref, summary_ref, reader_ref, local_ref,
    gate_ref, gain_ref, weight_ref, far_ref, rest_ref, final_ref, entering_ref,
):
    place = place_ref[0]
    entering = []
    for h in range(HEADS):
        state = start_ref[h]
        for offset, ref in ((3, back3_ref), (2, back2_ref), (1, back1_ref)):
            state = jnp.where(place >= offset, apply(ref[h], state), state)
        state = apply(prefix_ref[h], state)
        final_ref[h] = apply(summary_ref[h], state)
        entering.append(state.astype(bf16))
        entering_ref[h] = entering[h]
    mix(place_ref[1], 1 - place_ref[3], entering, reader_ref, local_ref, gate_ref, gain_ref, weight_ref, (far_ref, rest_ref))


def run_give(place, backs, start, prefix, summary, reader, local, gate, gain, weight):
    return pl.pallas_call(
        give_kernel,
        out_shape=(
            jax.ShapeDtypeStruct((gate.shape[0] // 8, weight.shape[1]), bf16),
            jax.ShapeDtypeStruct((gate.shape[0] // 8 * 3, weight.shape[1]), bf16),
            jax.ShapeDtypeStruct(start.shape, f32),
            jax.ShapeDtypeStruct(start.shape, bf16),
        ),
        in_specs=[SMEM] + [VMEM] * 11,
        out_specs=(VMEM,) * 4,
        compiler_params=pltpu.CompilerParams(vmem_limit_bytes=GRANT),
        name="give",
    )(place, *backs, start, prefix, summary, reader, local, gate, gain, weight)


def keep_kernel(
    place_ref, entering_ref, reader_ref, local_ref, gate_ref, gain_ref, weight_ref, far_ref, rest_ref
):
    entering = [entering_ref[h] for h in range(HEADS)]
    mix(place_ref[1], place_ref[3], entering, reader_ref, local_ref, gate_ref, gain_ref, weight_ref, (far_ref, rest_ref))


def run_keep(place, entering, reader, local, gate, gain, weight):
    rows = gate.shape[0] // 2
    return pl.pallas_call(
        keep_kernel,
        out_shape=(
            jax.ShapeDtypeStruct((gate.shape[0] // 8, weight.shape[1]), bf16),
            jax.ShapeDtypeStruct((gate.shape[0] // 8 * 3, weight.shape[1]), bf16),
        ),
        in_specs=[SMEM] + [VMEM] * 6,
        out_specs=(VMEM, VMEM),
        compiler_params=pltpu.CompilerParams(vmem_limit_bytes=GRANT),
        cost_estimate=pl.CostEstimate(
            flops=2 * rows * weight.size, bytes_accessed=4 * 10**6, transcendentals=0
        ),
        name="keep",
    )(place, entering, reader, local, gate, gain, weight)


def far_kernel(kept_ref, got_ref, far_up_ref, far_down_ref):
    half = far_up_ref.shape[0]
    total = (kept_ref[...].astype(f32) + got_ref[...].astype(f32)).astype(bf16)
    far_up_ref[...] = total[:half]
    far_down_ref[...] = total[half:]


def run_far(kept, got):
    rows, width = kept.shape
    return pl.pallas_call(
        far_kernel,
        out_shape=(jax.ShapeDtypeStruct((rows // 2, width), bf16),) * 2,
        in_specs=[VMEM] * 2,
        out_specs=(VMEM,) * 2,
        compiler_params=pltpu.CompilerParams(vmem_limit_bytes=12 * 1024 * 1024),
        name="far",
    )(kept, got)


def split_kernel(kept_ref, got_ref, near_ref, up_ref, down_ref):
    rows = near_ref.shape[0]
    for i, ref in enumerate((near_ref, up_ref, down_ref)):
        at = slice(i * rows, (i + 1) * rows)
        ref[...] = kept_ref[at, :].astype(f32) + got_ref[at, :].astype(f32)


def run_split(kept, got):
    rows = kept.shape[0] // 3
    return pl.pallas_call(
        split_kernel,
        out_shape=(jax.ShapeDtypeStruct((rows, kept.shape[1]), f32),) * 3,
        in_specs=[VMEM] * 2,
        out_specs=(VMEM,) * 3,
        compiler_params=pltpu.CompilerParams(vmem_limit_bytes=12 * 1024 * 1024),
        name="split",
    )(kept, got)


def pass_kernel(up_ref, down_ref, from_below_ref, from_above_ref, send_up_ref, send_down_ref):
    half = from_below_ref.shape[0]
    send_up_ref[:half, :] = (up_ref[:half, :] + from_below_ref[...].astype(f32)).astype(bf16)
    send_up_ref[half:, :] = up_ref[half:, :].astype(bf16)
    send_down_ref[:half, :] = down_ref[:half, :].astype(bf16)
    send_down_ref[half:, :] = (down_ref[half:, :] + from_above_ref[...].astype(f32)).astype(bf16)


def run_pass(up, down, from_below, from_above):
    return pl.pallas_call(
        pass_kernel,
        out_shape=(jax.ShapeDtypeStruct(up.shape, bf16),) * 2,
        in_specs=[VMEM] * 4,
        out_specs=(VMEM,) * 2,
        compiler_params=pltpu.CompilerParams(vmem_limit_bytes=12 * 1024 * 1024),
        name="pass",
    )(up, down, from_below, from_above)


def dispatch_kernel(own_ref, near_ref, below_ref, above_ref, gain_ref, pick_ref, hidden_ref, out_ref):
    mixed = near_ref[...] + (below_ref[...].astype(f32) + above_ref[...].astype(f32))
    hidden = own_ref[...].astype(f32) + mixed
    hidden_ref[...] = hidden
    post = rms_scale(hidden, gain_ref[...]).astype(bf16)
    half = post.shape[1] // 2
    stacked = jnp.concatenate([post[:, :half], post[:, half:]], axis=0)
    out_ref[...] = jnp.dot(pick_ref[...], stacked, preferred_element_type=f32).astype(bf16)


def run_dispatch(own, near, below, above, gain, pick):
    return pl.pallas_call(
        dispatch_kernel,
        out_shape=(
            jax.ShapeDtypeStruct(own.shape, f32),
            jax.ShapeDtypeStruct((pick.shape[0], own.shape[1] // 2), bf16),
        ),
        in_specs=[VMEM] * 6,
        out_specs=(VMEM, VMEM),
        compiler_params=pltpu.CompilerParams(vmem_limit_bytes=GRANT),
        name="dispatch",
    )(own, near, below, above, gain, pick)


def expert_kernel(rows_ref, up_ref, down_ref, out_ref):
    count, _, half = rows_ref.shape

    def hidden_of(gate_up):
        return (silu(gate_up[:, :FFE]) * gate_up[:, FFE:]).astype(bf16)

    group = 32

    def step(i, _):
        some = pl.ds(i * group, group)
        left = rows_ref[some, 0:16, :].reshape(group * 16, half)
        right = rows_ref[some, 16:32, :].reshape(group * 16, half)
        gate_up = jnp.dot(left, up_ref[:half, :], preferred_element_type=f32) + jnp.dot(
            right, up_ref[half:, :], preferred_element_type=f32
        )
        done = jnp.dot(hidden_of(gate_up), down_ref[...], preferred_element_type=f32).astype(bf16)
        out_ref[some, 0:16, :] = done[:, :half].reshape(group, 16, half)
        out_ref[some, 16:32, :] = done[:, half:].reshape(group, 16, half)
        return 0

    lax.fori_loop(0, count // group, step, 0)
    tail = rows_ref[:, 32:40, :].reshape(count * 8, half)
    first = jnp.dot(tail, up_ref[:half, :], preferred_element_type=f32)
    second = jnp.dot(tail, up_ref[half:, :], preferred_element_type=f32)
    turned = count * 8 - 4
    gate_up = first + pltpu.roll(second, turned, 0)
    done = jnp.dot(hidden_of(gate_up), down_ref[...], preferred_element_type=f32)
    upper = lax.broadcasted_iota(jnp.int32, (count * 8, half), 0) % 8 < 4
    packed = jnp.where(upper, done[:, :half], pltpu.roll(done[:, half:], 4, 0)).astype(bf16)
    out_ref[:, 32:40, :] = packed.reshape(count, 8, half)


def run_expert(rows, up, down):
    return pl.pallas_call(
        expert_kernel,
        out_shape=jax.ShapeDtypeStruct(rows.shape, bf16),
        in_specs=[VMEM] * 3,
        out_specs=VMEM,
        compiler_params=pltpu.CompilerParams(vmem_limit_bytes=GRANT),
        name="expert",
    )(rows, up, down)


def combine_kernel(hidden_ref, back_ref, high_ref, low_ref, out_ref):
    rows = hidden_ref.shape[0]
    half = back_ref.shape[1]
    back = back_ref[...]
    routed = jnp.dot(high_ref[...], back, preferred_element_type=f32) + jnp.dot(
        low_ref[...], back, preferred_element_type=f32
    )
    out_ref[:, :half] = hidden_ref[:, :half] + routed[:rows]
    out_ref[:, half:] = hidden_ref[:, half:] + routed[rows:]


def run_combine(hidden, back, high, low):
    return pl.pallas_call(
        combine_kernel,
        out_shape=jax.ShapeDtypeStruct(hidden.shape, f32),
        in_specs=[VMEM] * 4,
        out_specs=VMEM,
        compiler_params=pltpu.CompilerParams(vmem_limit_bytes=GRANT),
        name="combine",
    )(hidden, back, high, low)


def turned(size, distance):
    return [(i, (i + distance) % size) for i in range(size)]


def slot_rows(ids, experts):
    rows = ids.shape[0]
    choice = ids[:, :, None] == jnp.arange(experts, dtype=jnp.int32)
    named = jnp.any(choice, axis=1).astype(bf16)
    before = jnp.tril(jnp.ones((rows, rows), bf16), -1)
    ranks = jnp.dot(before, named, preferred_element_type=f32)
    slots = jnp.sum(jnp.where(choice, ranks[:, None, :], 0.0), axis=2).astype(jnp.int32)
    early = slots < 16
    left = ids * 40 + jnp.where(early, slots, slots + 16)
    right = ids * 40 + jnp.where(early, slots + 16, slots + 20)
    return jnp.concatenate([left, right], axis=0)


def body(
    tokens,
    input_gain,
    mixer_weight,
    rate_weight,
    conv_kernel,
    decay_scale,
    decay_bias,
    value_gain,
    output_weight,
    start_state,
    post_gain,
    expert_gateup,
    expert_down,
    route_ids,
    route_weights,
):
    own = tokens[0]
    model_width = own.shape[1]
    experts = lax.axis_size(EXP)
    normed = run_norm(own, input_gain.reshape(1, -1))
    rings = lax.axis_size("y")
    y, core = lax.axis_index("y"), lax.axis_index("core")
    up, down, swap = turned(rings, 1), turned(rings, -1), [(0, 1), (1, 0)]
    below = lax.ppermute(normed, "y", up)
    above = lax.ppermute(normed, "y", down)
    beside = lax.ppermute(normed, "core", swap)
    rate = jnp.concatenate(
        [rate_weight.reshape(model_width, -1), jnp.zeros((model_width, 128 - 2 * HEADS), bf16)], axis=1
    )
    places = slot_rows(route_ids[0], experts)
    count = experts * 40
    hits = places[:, :, None] == jnp.arange(count, dtype=jnp.int32)
    pick = jnp.any(
        places.T[:, None, :] == jnp.arange(count, dtype=jnp.int32)[None, :, None], axis=0
    ).astype(bf16)
    doubled = jnp.concatenate([route_weights[0], route_weights[0]], axis=0)
    share = jnp.sum(jnp.where(hits, doubled[:, :, None], 0.0), axis=1)
    high = share.astype(bf16)
    low = (share - high.astype(f32)).astype(bf16)
    room = 128 - 2 * HEADS
    rate_par = jnp.stack(
        [
            jnp.concatenate([jnp.zeros(HEADS, f32), decay_bias, jnp.zeros(room, f32)]),
            jnp.concatenate([jnp.zeros(HEADS, f32), decay_scale, jnp.zeros(room, f32)]),
        ]
    )
    place = jnp.stack([lax.axis_index("x"), y, lax.axis_index("z"), core]).astype(jnp.int32)
    low_half, high_half, flanks = run_cut(below, above)
    low_half, high_half, flanks, beside, rate, rate_par, conv, place, pick, high, low = lax.optimization_barrier(
        (low_half, high_half, flanks, beside, rate, rate_par, conv_kernel[:, 0], place, pick, high, low)
    )
    far_low = lax.ppermute(low_half, "y", up)
    far_high = lax.ppermute(high_half, "y", down)
    flanks = lax.ppermute(flanks, "core", swap)
    early, early_rate = run_project([normed, beside, below, above], mixer_weight, rate)
    far_low, far_high, flanks, early = lax.optimization_barrier((far_low, far_high, flanks, early))
    far = lax.ppermute(run_join(far_low, far_high), "core", swap)
    late, late_rate = run_project([flanks, far_low, far_high, far], mixer_weight, rate)
    closing = run_closing(place, [normed, beside, below, above, flanks, flanks, far_high, far])
    halo = lax.ppermute(closing, EXP, [(i, i + 1) for i in range(experts - 1)])
    gate, reader, local, summary, packed = run_delta(
        place, early, early_rate, late, late_rate, halo, mixer_weight, conv, rate_par
    )
    depth = lax.axis_size("z")
    other = lax.ppermute(packed, "z", [(i, i ^ 1) for i in range(depth)])
    both = run_couple(place, packed, other)
    pairs = [lax.ppermute(both, "z", turned(depth, 2 * step)) for step in (1, 2, 3)]
    prefix, total = run_row(place, both, *pairs, other)
    rows = [lax.ppermute(total, "x", turned(lax.axis_size("x"), step)) for step in (1, 2, 3)]
    gain = value_gain.reshape(1, -1)
    given_far, given_rest, final_state, entering = run_give(
        place, rows, start_state, prefix, summary, reader, local, gate, gain, output_weight
    )
    got_far = lax.ppermute(given_far, "core", swap)
    kept_far, kept_rest = run_keep(place, entering, reader, local, gate, gain, output_weight)
    got_far, given_rest, kept_far, kept_rest = lax.optimization_barrier(
        (got_far, given_rest, kept_far, kept_rest)
    )
    far_up, far_down = run_far(kept_far, got_far)
    from_below = lax.ppermute(far_up, "y", up)
    from_above = lax.ppermute(far_down, "y", down)
    got_rest = lax.ppermute(given_rest, "core", swap)
    near, to_up, to_down = run_split(kept_rest, got_rest)
    send_up, send_down = run_pass(to_up, to_down, from_below, from_above)
    mixed_below = lax.ppermute(send_up, "y", up)
    mixed_above = lax.ppermute(send_down, "y", down)

    hidden, outgoing = run_dispatch(
        own, near, mixed_below, mixed_above, post_gain.reshape(1, -1), pick
    )
    width = model_width // 2
    arrived = lax.all_to_all(outgoing.reshape(experts, 40, width), EXP, 0, 0, tiled=True)
    made = run_expert(arrived, expert_gateup[0], expert_down[0])
    back = lax.all_to_all(made, EXP, 0, 0, tiled=True)
    layer_out = run_combine(hidden, back.reshape(count, width), high, low)
    return (layer_out[None], final_state[None])


def solution(mesh):
    fine = Mesh(mesh.devices.reshape(4, 2, 4, 8), CTX + EXP)
    in_specs = (
        P(EXP, CTX, None),
        P(),
        P(None, CTX),
        P(None, CTX, None),
        P(None, CTX, None),
        P(CTX),
        P(CTX),
        P(),
        P(CTX, None),
        P(CTX, None, None),
        P(),
        P(EXP, None, None),
        P(EXP, None, None),
        P(EXP, CTX, None),
        P(EXP, CTX, None),
    )
    out_specs = (P(EXP, CTX, None), P(EXP, CTX, None, None))
    return jax.shard_map(body, mesh=fine, in_specs=in_specs, out_specs=out_specs, check_vma=False)
```

```python
import functools

import jax
import jax.numpy as jnp
from jax import lax
from jax.experimental import pallas as pl
from jax.experimental.pallas import tpu as pltpu
from jax.sharding import Mesh
from jax.sharding import PartitionSpec as P

DK = 128
DV = 128
FFE = 512
HEADS = 2
ROUTES = 4
CHUNK = 128
EPSILON = 1e-06
CTX = ("y", "core")
EXP = ("x", "z")
bf16 = jnp.bfloat16
f32 = jnp.float32
highest = lax.Precision.HIGHEST
VMEM = pl.BlockSpec(memory_space=pltpu.VMEM)
SMEM = pl.BlockSpec(memory_space=pltpu.SMEM)
GRANT = 24 * 1024 * 1024


def mm(a, b):
    return jnp.dot(a.astype(bf16), b.astype(bf16), preferred_element_type=f32)


def mm_t(a, b):
    return lax.dot_general(
        a.astype(bf16), b.astype(bf16), (((1,), (1,)), ((), ())), preferred_element_type=f32
    )


def rms_scale(values, scaling):
    widened = values.astype(f32)
    return (
        widened * lax.rsqrt(jnp.mean(widened * widened, axis=-1, keepdims=True) + EPSILON) * scaling
    )


def unit_rows(values):
    return values * lax.rsqrt(jnp.sum(values * values, axis=-1, keepdims=True) + EPSILON)


def silu(values):
    return values / (1.0 + jnp.exp(-values))


def square_iota(size, axis):
    return lax.broadcasted_iota(jnp.int32, (size, size), axis)


def norm_kernel(own_ref, gain_ref, out_ref):
    out_ref[...] = rms_scale(own_ref[...], gain_ref[...]).astype(bf16)


def run_norm(own, gain):
    return pl.pallas_call(
        norm_kernel,
        out_shape=jax.ShapeDtypeStruct(own.shape, bf16),
        in_specs=[VMEM] * 2,
        out_specs=VMEM,
        compiler_params=pltpu.CompilerParams(vmem_limit_bytes=8 * 1024 * 1024),
        name="norm",
    )(own, gain)


ORDER = ((0, 0), (0, 1), (3, 0), (1, 0), (3, 1), (1, 1), (2, 0), (2, 1))
CLOSING = (112, 112, 112, 112, 112, 240, 48, 112)


def block_of(y, core, i):
    step, side = ORDER[i]
    return (y + step) % 4 * 2 + (core + side) % 2


ANY = pl.BlockSpec(memory_space=pl.ANY)


def cut_kernel(below_ref, above_ref, low_ref, high_ref, both_ref, sems):
    rows = below_ref.shape[0]
    half = rows // 2
    copies = [
        pltpu.make_async_copy(below_ref.at[pl.ds(0, half)], low_ref, sems.at[0]),
        pltpu.make_async_copy(above_ref.at[pl.ds(half, half)], high_ref, sems.at[1]),
        pltpu.make_async_copy(below_ref, both_ref.at[pl.ds(0, rows)], sems.at[2]),
        pltpu.make_async_copy(above_ref, both_ref.at[pl.ds(rows, rows)], sems.at[3]),
    ]
    for copy in copies:
        copy.start()
    for copy in copies:
        copy.wait()


def run_cut(below, above):
    rows, width = below.shape
    return pl.pallas_call(
        cut_kernel,
        out_shape=(
            jax.ShapeDtypeStruct((rows // 2, width), bf16),
            jax.ShapeDtypeStruct((rows // 2, width), bf16),
            jax.ShapeDtypeStruct((2 * rows, width), bf16),
        ),
        in_specs=[ANY] * 2,
        out_specs=(ANY,) * 3,
        scratch_shapes=[pltpu.SemaphoreType.DMA((4,))],
        compiler_params=pltpu.CompilerParams(vmem_limit_bytes=4 * 1024 * 1024),
        name="cut",
    )(below, above)


def join_kernel(first_ref, second_ref, both_ref, sems):
    rows = first_ref.shape[0]
    copies = [
        pltpu.make_async_copy(first_ref, both_ref.at[pl.ds(0, rows)], sems.at[0]),
        pltpu.make_async_copy(second_ref, both_ref.at[pl.ds(rows, rows)], sems.at[1]),
    ]
    for copy in copies:
        copy.start()
    for copy in copies:
        copy.wait()


def run_join(first, second):
    rows, width = first.shape
    return pl.pallas_call(
        join_kernel,
        out_shape=jax.ShapeDtypeStruct((2 * rows, width), bf16),
        in_specs=[ANY] * 2,
        out_specs=ANY,
        scratch_shapes=[pltpu.SemaphoreType.DMA((2,))],
        compiler_params=pltpu.CompilerParams(vmem_limit_bytes=4 * 1024 * 1024),
        name="join",
    )(first, second)


def closing_kernel(place_ref, *refs):
    ends, out_ref, sem = refs[:-2], refs[-2], refs[-1]
    for i, (ref, at) in enumerate(zip(ends, CLOSING)):

        @pl.when(block_of(place_ref[1], place_ref[3], i) == len(ORDER) - 1)
        def _(ref=ref, at=at):
            copy = pltpu.make_async_copy(ref.at[pl.ds(at, 16)], out_ref, sem)
            copy.start()
            copy.wait()


def run_closing(place, ends):
    return pl.pallas_call(
        closing_kernel,
        out_shape=jax.ShapeDtypeStruct((16, ends[0].shape[1]), bf16),
        in_specs=[SMEM] + [ANY] * len(ends),
        out_specs=ANY,
        scratch_shapes=[pltpu.SemaphoreType.DMA],
        compiler_params=pltpu.CompilerParams(vmem_limit_bytes=4 * 1024 * 1024),
        name="closing",
    )(place, *ends)


def project_kernel(count, *refs):
    weight_ref, rate_ref, made_ref, rates_ref, rows_scr, sems = refs[count:]
    copies, at = [], 0
    for i, ref in enumerate(refs[:count]):
        copies.append(pltpu.make_async_copy(ref, rows_scr.at[pl.ds(at, ref.shape[0])], sems.at[i]))
        copies[i].start()
        at += ref.shape[0]
    for copy in copies:
        copy.wait()
    rows = rows_scr[...]
    made_ref[...] = jnp.dot(rows, weight_ref[...], preferred_element_type=f32).astype(bf16)
    rates_ref[...] = jnp.dot(rows, rate_ref[...], preferred_element_type=f32).astype(bf16)


def run_project(blocks, weight, rate):
    rows = sum(block.shape[0] for block in blocks)
    return pl.pallas_call(
        functools.partial(project_kernel, len(blocks)),
        out_shape=(
            jax.ShapeDtypeStruct((rows, weight.shape[1]), bf16),
            jax.ShapeDtypeStruct((rows, rate.shape[1]), bf16),
        ),
        in_specs=[ANY] * len(blocks) + [VMEM] * 2,
        out_specs=(VMEM, VMEM),
        scratch_shapes=[
            pltpu.VMEM((rows, weight.shape[0]), bf16),
            pltpu.SemaphoreType.DMA((len(blocks),)),
        ],
        compiler_params=pltpu.CompilerParams(vmem_limit_bytes=14 * 1024 * 1024),
        cost_estimate=pl.CostEstimate(
            flops=2 * rows * weight.size, bytes_accessed=8 * 10**6, transcendentals=0
        ),
        name="project",
    )(*blocks, weight, rate)


def delta_kernel(
    place_ref, early_ref, early_rate_ref, late_ref, late_rate_ref, halo_ref, weight_ref, conv_ref, rate_par_ref,
    gate_ref, reader_ref, local_ref, summary_ref, packed_ref,
    rows_scr, rate_scr,
):
    seg_rows = gate_ref.shape[0]
    width = conv_ref.shape[1]
    steps = seg_rows // CHUNK
    halo = jnp.dot(halo_ref[...], weight_ref[:, :width], preferred_element_type=f32)
    rows_scr[0:8, :] = halo[8:16].astype(bf16).astype(f32)
    for i in range(steps):
        made_ref, made_rate_ref = (
            (early_ref, early_rate_ref) if 2 * i < steps else (late_ref, late_rate_ref)
        )
        at = i % (steps // 2) * CHUNK
        to = pl.multiple_of(block_of(place_ref[1], place_ref[3], i) * CHUNK, CHUNK)
        rows_scr[pl.ds(pl.multiple_of(to + 8, 8), CHUNK), :] = made_ref[at : at + CHUNK, :width].astype(f32)
        gate_ref[pl.ds(to, CHUNK), :] = made_ref[at : at + CHUNK, width:]
        rate_scr[pl.ds(to, CHUNK), :] = made_rate_ref[at : at + CHUNK, :].astype(f32)

    row = square_iota(CHUNK, 0)
    col = square_iota(CHUNK, 1)
    lower = (row >= col).astype(f32)
    eye = (row == col).astype(f32)
    for h in range(HEADS):
        summary_ref[h, :, :DK] = eye
        summary_ref[h, :, DK:] = jnp.zeros((DK, DV), f32)

    pair = 8

    def chunk_step(i, _):
        units = []
        for u in range(pair):
            at = pl.multiple_of((i * pair + u) * CHUNK, CHUNK)
            window = rows_scr[pl.ds(at, CHUNK + 8), :]
            summed = conv_ref[0:1, :] * window[5 : 5 + CHUNK]
            for tap in range(1, 4):
                summed = summed + conv_ref[tap : tap + 1, :] * window[5 + tap : 5 + tap + CHUNK]
            active = silu(summed)
            query = unit_rows(active[:, :DK]) * DK ** (-0.5)
            key = unit_rows(active[:, DK : 2 * DK])
            rate = rate_scr[pl.ds(at, CHUNK), :]
            shifted = rate + rate_par_ref[0:1, :]
            soft = jnp.maximum(shifted, 0.0) + jnp.log1p(jnp.exp(-jnp.abs(shifted)))
            decay = -rate_par_ref[1:2, :] * soft
            beta_all = 1.0 / (1.0 + jnp.exp(-rate))
            total = jnp.dot(lower, decay, preferred_element_type=f32, precision=highest)
            total_t = total.T
            key_low = key.astype(bf16)
            gram = mm_t(key_low, key_low)
            raw_scores = mm_t(query, key_low)
            for h in range(HEADS):
                cum = total[:, HEADS + h : HEADS + h + 1]
                cum_row = total_t[HEADS + h : HEADS + h + 1, :]
                beta = beta_all[:, h : h + 1]
                causal = jnp.exp(jnp.where(row >= col, cum - cum_row, -1e30))
                grown = jnp.exp(cum)
                last = cum[CHUNK - 1 : CHUNK, :]
                value = active[:, 2 * DK + h * DV : 2 * DK + (h + 1) * DV]
                units.append(
                    dict(
                        at=at,
                        h=h,
                        low=jnp.where(row > col, beta * gram * causal, 0.0),
                        right=jnp.concatenate([beta * key * grown, beta * value], axis=1).astype(bf16),
                        scores=(raw_scores * causal).astype(bf16),
                        read=(query * grown).astype(bf16),
                        faded=(key * jnp.exp(last - cum)).T.astype(bf16),
                        fade=jnp.exp(last),
                    )
                )
        inverses = [
            eye - jnp.where((row // 2 == col // 2), unit["low"], 0.0) for unit in units
        ]
        size = 2
        while size < CHUNK:
            off = (row // (2 * size) == col // (2 * size)) & (row // size != col // size)
            lows = [x.astype(bf16) for x in inverses]
            firsts = [mm(jnp.where(off, unit["low"], 0.0), x) for unit, x in zip(units, lows)]
            inverses = [x - mm(x_low, y) for x, x_low, y in zip(inverses, lows, firsts)]
            size *= 2
        solved = [mm(x, unit["right"]) for unit, x in zip(units, inverses)]
        for unit, done in zip(units, solved):
            h = unit["h"]
            state = summary_ref[h]
            stacked = jnp.concatenate([done[:, :DK].astype(bf16), unit["read"]], axis=0)
            applied = mm(stacked, state)
            fresh = jnp.concatenate([-applied[:CHUNK, :DK], done[:, DK:] - applied[:CHUNK, DK:]], axis=1)
            fresh = fresh.astype(bf16)
            out = applied[CHUNK:] + mm(unit["scores"], fresh)
            summary_ref[h] = unit["fade"] * state + mm(unit["faded"], fresh)
            reader_ref[h, pl.ds(unit["at"], CHUNK), :] = out[:, :DK].astype(bf16)
            local_ref[h, pl.ds(unit["at"], CHUNK), :] = out[:, DK:]
        return 0

    lax.fori_loop(0, steps // pair, chunk_step, 0)
    for h in range(HEADS):
        change = summary_ref[h, :, :DK] - eye
        summary_ref[h, :, :DK] = change
        packed_ref[h, :, :DK] = change.astype(bf16)
        packed_ref[h, :, DK:] = summary_ref[h, :, DK:].astype(bf16)


def run_delta(place, early, early_rate, late, late_rate, halo, weight, conv, rate_par):
    rows = 2 * early.shape[0]
    return pl.pallas_call(
        delta_kernel,
        out_shape=(
            jax.ShapeDtypeStruct((rows, HEADS * DV), bf16),
            jax.ShapeDtypeStruct((HEADS, rows, DK), bf16),
            jax.ShapeDtypeStruct((HEADS, rows, DV), f32),
            jax.ShapeDtypeStruct((HEADS, DK, DK + DV), f32),
            jax.ShapeDtypeStruct((HEADS, DK, DK + DV), bf16),
        ),
        in_specs=[SMEM] + [VMEM] * 8,
        out_specs=(VMEM,) * 5,
        scratch_shapes=[
            pltpu.VMEM((rows + 8, conv.shape[1]), f32),
            pltpu.VMEM((rows, 128), f32),
        ],
        compiler_params=pltpu.CompilerParams(vmem_limit_bytes=GRANT),
        name="delta",
    )(place, early, early_rate, late, late_rate, halo, weight, conv, rate_par)


def then(first, second):
    return first + mm(second[:, :DK], first) + second.astype(f32)


def apply(change, state):
    return state + mm(change[:, :DK], state) + change[:, DK:].astype(f32)


def couple_kernel(place_ref, own_ref, other_ref, both_ref):
    odd = place_ref[2] % 2 == 1
    for h in range(HEADS):
        own = own_ref[h].astype(f32)
        other = other_ref[h].astype(f32)
        both_ref[h] = then(jnp.where(odd, other, own), jnp.where(odd, own, other)).astype(bf16)


def run_couple(place, own, other):
    return pl.pallas_call(
        couple_kernel,
        out_shape=jax.ShapeDtypeStruct(own.shape, bf16),
        in_specs=[SMEM, VMEM, VMEM],
        out_specs=VMEM,
        compiler_params=pltpu.CompilerParams(vmem_limit_bytes=8 * 1024 * 1024),
        name="couple",
    )(place, own, other)


def row_kernel(place_ref, own_ref, back1_ref, back2_ref, back3_ref, other_ref, prefix_ref, total_ref, all_scr):
    odd = place_ref[2] % 2 == 1
    place = place_ref[2] // 2
    for offset, ref in enumerate((own_ref, back1_ref, back2_ref, back3_ref)):
        all_scr[(place + 4 - offset) % 4] = ref[...]
    changes = [jnp.zeros((DK, DK + DV), f32) for _ in range(HEADS)]
    for j in range(4):
        for h in range(HEADS):
            change = changes[h]

            @pl.when(place == j)
            def _(change=change, h=h):
                prefix_ref[h] = change

            changes[h] = then(change, all_scr[j, h])
    for h in range(HEADS):
        total_ref[h] = changes[h].astype(bf16)
        before = prefix_ref[h]
        prefix_ref[h] = jnp.where(odd, then(before, other_ref[h]), before)


def run_row(place, own, back1, back2, back3, other):
    return pl.pallas_call(
        row_kernel,
        out_shape=(
            jax.ShapeDtypeStruct(own.shape, f32),
            jax.ShapeDtypeStruct(own.shape, bf16),
        ),
        in_specs=[SMEM] + [VMEM] * 5,
        out_specs=(VMEM, VMEM),
        scratch_shapes=[pltpu.VMEM((4,) + own.shape, bf16)],
        compiler_params=pltpu.CompilerParams(vmem_limit_bytes=8 * 1024 * 1024),
        name="row",
    )(place, own, back1, back2, back3, other)


def mix(y, core, entering, reader_ref, local_ref, gate_ref, gain_ref, weight_ref, out_refs):
    rows = []
    for i in range(4):
        at = pl.ds(pl.multiple_of(((y + i) % 4 * 2 + core) * CHUNK, CHUNK), CHUNK)
        parts = []
        for h in range(HEADS):
            mixed = mm(reader_ref[h, at, :], entering[h]) + local_ref[h, at, :]
            gate = gate_ref[at, h * DV : (h + 1) * DV].astype(f32)
            parts.append((rms_scale(mixed, gain_ref[...]) * silu(gate)).astype(bf16))
        rows.append(jnp.concatenate(parts, axis=1))
    gated = jnp.concatenate(rows, axis=0)
    made = jnp.dot(gated, weight_ref[...], preferred_element_type=f32).astype(bf16)
    far_ref, rest_ref = out_refs
    far_ref[...] = made[2 * CHUNK : 3 * CHUNK]
    rest_ref[: 2 * CHUNK, :] = made[: 2 * CHUNK]
    rest_ref[2 * CHUNK :, :] = made[3 * CHUNK :]


def give_kernel(
    place_ref, back1_ref, back2_ref, back3_ref, start_ref, prefix_ref, summary_ref, reader_ref, local_ref,
    gate_ref, gain_ref, weight_ref, far_ref, rest_ref, final_ref, entering_ref,
):
    place = place_ref[0]
    entering = []
    for h in range(HEADS):
        state = start_ref[h]
        for offset, ref in ((3, back3_ref), (2, back2_ref), (1, back1_ref)):
            state = jnp.where(place >= offset, apply(ref[h], state), state)
        state = apply(prefix_ref[h], state)
        final_ref[h] = apply(summary_ref[h], state)
        entering.append(state.astype(bf16))
        entering_ref[h] = entering[h]
    mix(place_ref[1], 1 - place_ref[3], entering, reader_ref, local_ref, gate_ref, gain_ref, weight_ref, (far_ref, rest_ref))


def run_give(place, backs, start, prefix, summary, reader, local, gate, gain, weight):
    return pl.pallas_call(
        give_kernel,
        out_shape=(
            jax.ShapeDtypeStruct((gate.shape[0] // 8, weight.shape[1]), bf16),
            jax.ShapeDtypeStruct((gate.shape[0] // 8 * 3, weight.shape[1]), bf16),
            jax.ShapeDtypeStruct(start.shape, f32),
            jax.ShapeDtypeStruct(start.shape, bf16),
        ),
        in_specs=[SMEM] + [VMEM] * 11,
        out_specs=(VMEM,) * 4,
        compiler_params=pltpu.CompilerParams(vmem_limit_bytes=GRANT),
        name="give",
    )(place, *backs, start, prefix, summary, reader, local, gate, gain, weight)


def keep_kernel(
    place_ref, entering_ref, reader_ref, local_ref, gate_ref, gain_ref, weight_ref, far_ref, rest_ref
):
    entering = [entering_ref[h] for h in range(HEADS)]
    mix(place_ref[1], place_ref[3], entering, reader_ref, local_ref, gate_ref, gain_ref, weight_ref, (far_ref, rest_ref))


def run_keep(place, entering, reader, local, gate, gain, weight):
    rows = gate.shape[0] // 2
    return pl.pallas_call(
        keep_kernel,
        out_shape=(
            jax.ShapeDtypeStruct((gate.shape[0] // 8, weight.shape[1]), bf16),
            jax.ShapeDtypeStruct((gate.shape[0] // 8 * 3, weight.shape[1]), bf16),
        ),
        in_specs=[SMEM] + [VMEM] * 6,
        out_specs=(VMEM, VMEM),
        compiler_params=pltpu.CompilerParams(vmem_limit_bytes=GRANT),
        cost_estimate=pl.CostEstimate(
            flops=2 * rows * weight.size, bytes_accessed=4 * 10**6, transcendentals=0
        ),
        name="keep",
    )(place, entering, reader, local, gate, gain, weight)


def far_kernel(kept_ref, got_ref, far_up_ref, far_down_ref):
    half = far_up_ref.shape[0]
    total = (kept_ref[...].astype(f32) + got_ref[...].astype(f32)).astype(bf16)
    far_up_ref[...] = total[:half]
    far_down_ref[...] = total[half:]


def run_far(kept, got):
    rows, width = kept.shape
    return pl.pallas_call(
        far_kernel,
        out_shape=(jax.ShapeDtypeStruct((rows // 2, width), bf16),) * 2,
        in_specs=[VMEM] * 2,
        out_specs=(VMEM,) * 2,
        compiler_params=pltpu.CompilerParams(vmem_limit_bytes=12 * 1024 * 1024),
        name="far",
    )(kept, got)


def split_kernel(kept_ref, got_ref, near_ref, up_ref, down_ref):
    rows = near_ref.shape[0]
    for i, ref in enumerate((near_ref, up_ref, down_ref)):
        at = slice(i * rows, (i + 1) * rows)
        ref[...] = kept_ref[at, :].astype(f32) + got_ref[at, :].astype(f32)


def run_split(kept, got):
    rows = kept.shape[0] // 3
    return pl.pallas_call(
        split_kernel,
        out_shape=(jax.ShapeDtypeStruct((rows, kept.shape[1]), f32),) * 3,
        in_specs=[VMEM] * 2,
        out_specs=(VMEM,) * 3,
        compiler_params=pltpu.CompilerParams(vmem_limit_bytes=12 * 1024 * 1024),
        name="split",
    )(kept, got)


def pass_kernel(up_ref, down_ref, from_below_ref, from_above_ref, send_up_ref, send_down_ref):
    half = from_below_ref.shape[0]
    send_up_ref[:half, :] = (up_ref[:half, :] + from_below_ref[...].astype(f32)).astype(bf16)
    send_up_ref[half:, :] = up_ref[half:, :].astype(bf16)
    send_down_ref[:half, :] = down_ref[:half, :].astype(bf16)
    send_down_ref[half:, :] = (down_ref[half:, :] + from_above_ref[...].astype(f32)).astype(bf16)


def run_pass(up, down, from_below, from_above):
    return pl.pallas_call(
        pass_kernel,
        out_shape=(jax.ShapeDtypeStruct(up.shape, bf16),) * 2,
        in_specs=[VMEM] * 4,
        out_specs=(VMEM,) * 2,
        compiler_params=pltpu.CompilerParams(vmem_limit_bytes=12 * 1024 * 1024),
        name="pass",
    )(up, down, from_below, from_above)


def dispatch_kernel(own_ref, near_ref, below_ref, above_ref, gain_ref, pick_ref, hidden_ref, out_ref):
    mixed = near_ref[...] + (below_ref[...].astype(f32) + above_ref[...].astype(f32))
    hidden = own_ref[...].astype(f32) + mixed
    hidden_ref[...] = hidden
    post = rms_scale(hidden, gain_ref[...]).astype(bf16)
    half = post.shape[1] // 2
    stacked = jnp.concatenate([post[:, :half], post[:, half:]], axis=0)
    out_ref[...] = jnp.dot(pick_ref[...], stacked, preferred_element_type=f32).astype(bf16)


def run_dispatch(own, near, below, above, gain, pick):
    return pl.pallas_call(
        dispatch_kernel,
        out_shape=(
            jax.ShapeDtypeStruct(own.shape, f32),
            jax.ShapeDtypeStruct((pick.shape[0], own.shape[1] // 2), bf16),
        ),
        in_specs=[VMEM] * 6,
        out_specs=(VMEM, VMEM),
        compiler_params=pltpu.CompilerParams(vmem_limit_bytes=GRANT),
        name="dispatch",
    )(own, near, below, above, gain, pick)


def expert_kernel(rows_ref, up_ref, down_ref, out_ref):
    count, _, half = rows_ref.shape

    def hidden_of(gate_up):
        return (silu(gate_up[:, :FFE]) * gate_up[:, FFE:]).astype(bf16)

    group = 32

    def step(i, _):
        some = pl.ds(i * group, group)
        left = rows_ref[some, 0:16, :].reshape(group * 16, half)
        right = rows_ref[some, 16:32, :].reshape(group * 16, half)
        gate_up = jnp.dot(left, up_ref[:half, :], preferred_element_type=f32) + jnp.dot(
            right, up_ref[half:, :], preferred_element_type=f32
        )
        done = jnp.dot(hidden_of(gate_up), down_ref[...], preferred_element_type=f32).astype(bf16)
        out_ref[some, 0:16, :] = done[:, :half].reshape(group, 16, half)
        out_ref[some, 16:32, :] = done[:, half:].reshape(group, 16, half)
        return 0

    lax.fori_loop(0, count // group, step, 0)
    tail = rows_ref[:, 32:40, :].reshape(count * 8, half)
    first = jnp.dot(tail, up_ref[:half, :], preferred_element_type=f32)
    second = jnp.dot(tail, up_ref[half:, :], preferred_element_type=f32)
    turned = count * 8 - 4
    gate_up = first + pltpu.roll(second, turned, 0)
    done = jnp.dot(hidden_of(gate_up), down_ref[...], preferred_element_type=f32)
    upper = lax.broadcasted_iota(jnp.int32, (count * 8, half), 0) % 8 < 4
    packed = jnp.where(upper, done[:, :half], pltpu.roll(done[:, half:], 4, 0)).astype(bf16)
    out_ref[:, 32:40, :] = packed.reshape(count, 8, half)


def run_expert(rows, up, down):
    return pl.pallas_call(
        expert_kernel,
        out_shape=jax.ShapeDtypeStruct(rows.shape, bf16),
        in_specs=[VMEM] * 3,
        out_specs=VMEM,
        compiler_params=pltpu.CompilerParams(vmem_limit_bytes=GRANT),
        name="expert",
    )(rows, up, down)


def combine_kernel(hidden_ref, back_ref, high_ref, low_ref, out_ref):
    rows = hidden_ref.shape[0]
    half = back_ref.shape[1]
    stacked = jnp.concatenate([high_ref[...], low_ref[...]], axis=0)
    both = jnp.dot(stacked, back_ref[...], preferred_element_type=f32)
    routed = both[: 2 * rows] + both[2 * rows :]
    out_ref[:, :half] = hidden_ref[:, :half] + routed[:rows]
    out_ref[:, half:] = hidden_ref[:, half:] + routed[rows:]


def run_combine(hidden, back, high, low):
    return pl.pallas_call(
        combine_kernel,
        out_shape=jax.ShapeDtypeStruct(hidden.shape, f32),
        in_specs=[VMEM] * 4,
        out_specs=VMEM,
        compiler_params=pltpu.CompilerParams(vmem_limit_bytes=GRANT),
        name="combine",
    )(hidden, back, high, low)


def turned(size, distance):
    return [(i, (i + distance) % size) for i in range(size)]


def slot_rows(ids, experts):
    rows = ids.shape[0]
    choice = ids[:, :, None] == jnp.arange(experts, dtype=jnp.int32)
    named = jnp.any(choice, axis=1).astype(bf16)
    before = jnp.tril(jnp.ones((rows, rows), bf16), -1)
    ranks = jnp.dot(before, named, preferred_element_type=f32)
    slots = jnp.sum(jnp.where(choice, ranks[:, None, :], 0.0), axis=2).astype(jnp.int32)
    early = slots < 16
    left = ids * 40 + jnp.where(early, slots, slots + 16)
    right = ids * 40 + jnp.where(early, slots + 16, slots + 20)
    return jnp.concatenate([left, right], axis=0)


def body(
    tokens,
    input_gain,
    mixer_weight,
    rate_weight,
    conv_kernel,
    decay_scale,
    decay_bias,
    value_gain,
    output_weight,
    start_state,
    post_gain,
    expert_gateup,
    expert_down,
    route_ids,
    route_weights,
):
    own = tokens[0]
    model_width = own.shape[1]
    experts = lax.axis_size(EXP)
    normed = run_norm(own, input_gain.reshape(1, -1))
    rings = lax.axis_size("y")
    y, core = lax.axis_index("y"), lax.axis_index("core")
    up, down, swap = turned(rings, 1), turned(rings, -1), [(0, 1), (1, 0)]
    below = lax.ppermute(normed, "y", up)
    above = lax.ppermute(normed, "y", down)
    beside = lax.ppermute(normed, "core", swap)
    rate = jnp.concatenate(
        [rate_weight.reshape(model_width, -1), jnp.zeros((model_width, 128 - 2 * HEADS), bf16)], axis=1
    )
    places = slot_rows(route_ids[0], experts)
    count = experts * 40
    hits = places[:, :, None] == jnp.arange(count, dtype=jnp.int32)
    pick = jnp.any(
        places.T[:, None, :] == jnp.arange(count, dtype=jnp.int32)[None, :, None], axis=0
    ).astype(bf16)
    doubled = jnp.concatenate([route_weights[0], route_weights[0]], axis=0)
    share = jnp.sum(jnp.where(hits, doubled[:, :, None], 0.0), axis=1)
    high = share.astype(bf16)
    low = (share - high.astype(f32)).astype(bf16)
    room = 128 - 2 * HEADS
    rate_par = jnp.stack(
        [
            jnp.concatenate([jnp.zeros(HEADS, f32), decay_bias, jnp.zeros(room, f32)]),
            jnp.concatenate([jnp.zeros(HEADS, f32), decay_scale, jnp.zeros(room, f32)]),
        ]
    )
    place = jnp.stack([lax.axis_index("x"), y, lax.axis_index("z"), core]).astype(jnp.int32)
    low_half, high_half, flanks = run_cut(below, above)
    low_half, high_half, flanks, beside, rate, rate_par, conv, place, pick, high, low = lax.optimization_barrier(
        (low_half, high_half, flanks, beside, rate, rate_par, conv_kernel[:, 0], place, pick, high, low)
    )
    far_low = lax.ppermute(low_half, "y", up)
    far_high = lax.ppermute(high_half, "y", down)
    flanks = lax.ppermute(flanks, "core", swap)
    early, early_rate = run_project([normed, beside, below, above], mixer_weight, rate)
    far_low, far_high, flanks, early = lax.optimization_barrier((far_low, far_high, flanks, early))
    far = lax.ppermute(run_join(far_low, far_high), "core", swap)
    late, late_rate = run_project([flanks, far_low, far_high, far], mixer_weight, rate)
    closing = run_closing(place, [normed, beside, below, above, flanks, flanks, far_high, far])
    halo = lax.ppermute(closing, EXP, [(i, i + 1) for i in range(experts - 1)])
    gate, reader, local, summary, packed = run_delta(
        place, early, early_rate, late, late_rate, halo, mixer_weight, conv, rate_par
    )
    depth = lax.axis_size("z")
    other = lax.ppermute(packed, "z", [(i, i ^ 1) for i in range(depth)])
    both = run_couple(place, packed, other)
    pairs = [lax.ppermute(both, "z", turned(depth, 2 * step)) for step in (1, 2, 3)]
    prefix, total = run_row(place, both, *pairs, other)
    rows = [lax.ppermute(total, "x", turned(lax.axis_size("x"), step)) for step in (1, 2, 3)]
    gain = value_gain.reshape(1, -1)
    given_far, given_rest, final_state, entering = run_give(
        place, rows, start_state, prefix, summary, reader, local, gate, gain, output_weight
    )
    got_far = lax.ppermute(given_far, "core", swap)
    kept_far, kept_rest = run_keep(place, entering, reader, local, gate, gain, output_weight)
    got_far, given_rest, kept_far, kept_rest = lax.optimization_barrier(
        (got_far, given_rest, kept_far, kept_rest)
    )
    far_up, far_down = run_far(kept_far, got_far)
    from_below = lax.ppermute(far_up, "y", up)
    from_above = lax.ppermute(far_down, "y", down)
    got_rest = lax.ppermute(given_rest, "core", swap)
    near, to_up, to_down = run_split(kept_rest, got_rest)
    send_up, send_down = run_pass(to_up, to_down, from_below, from_above)
    mixed_below = lax.ppermute(send_up, "y", up)
    mixed_above = lax.ppermute(send_down, "y", down)

    hidden, outgoing = run_dispatch(
        own, near, mixed_below, mixed_above, post_gain.reshape(1, -1), pick
    )
    width = model_width // 2
    arrived = lax.all_to_all(outgoing.reshape(experts, 40, width), EXP, 0, 0, tiled=True)
    made = run_expert(arrived, expert_gateup[0], expert_down[0])
    back = lax.all_to_all(made, EXP, 0, 0, tiled=True)
    layer_out = run_combine(hidden, back.reshape(count, width), high, low)
    return (layer_out[None], final_state[None])


def solution(mesh):
    fine = Mesh(mesh.devices.reshape(4, 2, 4, 8), CTX + EXP)
    in_specs = (
        P(EXP, CTX, None),
        P(),
        P(None, CTX),
        P(None, CTX, None),
        P(None, CTX, None),
        P(CTX),
        P(CTX),
        P(),
        P(CTX, None),
        P(CTX, None, None),
        P(),
        P(EXP, None, None),
        P(EXP, None, None),
        P(EXP, CTX, None),
        P(EXP, CTX, None),
    )
    out_specs = (P(EXP, CTX, None), P(EXP, CTX, None, None))
    return jax.shard_map(body, mesh=fine, in_specs=in_specs, out_specs=out_specs, check_vma=False)
```
